128 devices in a mesh: dp: 2 (over x_hi), seq: 32 (over z, y, core), mp: 2 (over x_lo).
Axes of the slice: x: 4 (x_hi: 2, x_lo: 2; x = x_hi * 2 + x_lo), y: 4, z: 4, core: 2. Of those that a mesh axis runs over, the one named last changes fastest.
Arguments:
- inputs: bfloat16 [2, 4096, 2048], P('dp', 'seq'), may hold values from -6 to 6
- clip_starts: int32 [2, 3], P('dp'), may hold values from 0 to 4064, as said below
- pad_lengths: int32 [2], P('dp'), may hold values from 1 to 64, as said below
- w_query: bfloat16 [2048, 2048], P(('dp', 'seq'), 'mp'), may hold values from -0.125 to 0.125
- w_key: bfloat16 [2048, 2048], P(('dp', 'seq'), 'mp'), may hold values from -0.125 to 0.125
- w_value: bfloat16 [2048, 2048], P(('dp', 'seq'), 'mp'), may hold values from -0.125 to 0.125
- w_out: bfloat16 [2048, 2048], P('mp', ('dp', 'seq')), may hold values from -0.75 to 0.75
- w_up: bfloat16 [2048, 8192], P(('dp', 'seq'), 'mp'), may hold values from -0.125 to 0.125
- w_down: bfloat16 [8192, 2048], P('mp', ('dp', 'seq')), may hold values from -0.0625 to 0.0625
- gain_first: bfloat16 [2048], P(('dp', 'seq')), may hold values from 0.099609375 to 1.8984375
- gain_second: bfloat16 [2048], P(('dp', 'seq')), may hold values from 0.099609375 to 1.8984375
- cotangent: bfloat16 [2, 4096, 2048], P('dp', 'seq'), may hold values from -6 to 6
Outputs:
- output: bfloat16 [2, 4096, 2048], P('dp', 'seq')
- grad_input: float32 [2, 4096, 2048], P('dp', 'seq')
- grad_w_query: float32 [2048, 2048], P(('dp', 'seq'), 'mp')
- grad_w_key: float32 [2048, 2048], P(('dp', 'seq'), 'mp')
- grad_w_value: float32 [2048, 2048], P(('dp', 'seq'), 'mp')
- grad_w_out: float32 [2048, 2048], P('mp', ('dp', 'seq'))
- grad_w_up: float32 [2048, 8192], P(('dp', 'seq'), 'mp')
- grad_w_down: float32 [8192, 2048], P('mp', ('dp', 'seq'))
- grad_gain_first: float32 [2048], P(('dp', 'seq'))
- grad_gain_second: float32 [2048], P(('dp', 'seq'))
The draws below stay inside these ranges and needn't reach their ends.
Inputs may be any that keep to these rules, and one draw needn't show every extreme that they name: `clip_starts`: each row rises strictly from 0 and every start is a multiple of 32; a clip runs from its start to the next start or to the end of the sequence; every clip but the second-to-last holds 1 to 3 frames of 32 tokens, and the second-to-last takes the rest of the sequence. `pad_lengths`: padding tokens are the last ones of their sequence.
All inputs are finite; a program needn't handle non-finite values.
Results may differ from the reference program's by a relative error of at most 0.017.
Values may be sent and summed in bfloat16 or wider, within the bound.
A program may use at most 640 MiB of HBM per device.

```python
import jax
import jax.numpy as jnp
from jax import lax

D = 2048
HEADS = 16
HD = 128
FF = 8192
SPAN = 128
FRAME = 32
CLIPS = 3
BATCH = 2
LEN = 4096


def draw_clip_starts(key, part):
    key = jax.random.fold_in(key, 11)
    key_frames, key_row = jax.random.split(key)
    frames = jax.random.randint(key_frames, (BATCH, CLIPS), 1, 4)
    chosen = jax.random.randint(key_row, (), 0, BATCH)
    columns = jnp.arange(CLIPS, dtype=jnp.int32)[None, :]
    rows = jnp.arange(BATCH, dtype=jnp.int32)[:, None]
    frames = jnp.where((columns == CLIPS - 1) & (rows == chosen), 1, frames)
    lengths = frames * FRAME
    before = jnp.where(columns < CLIPS - 2, lengths, 0)
    starts = jnp.cumsum(before, -1) - before
    starts = jnp.where(columns == CLIPS - 1, LEN - lengths[:, CLIPS - 1:], starts)
    return starts.astype(jnp.int32)


def draw_pad_lengths(key, part):
    key = jax.random.fold_in(key, 23)
    key_pad, key_row = jax.random.split(key)
    padding = jax.random.randint(key_pad, (BATCH,), 1, SPAN // 2 + 1)
    chosen = jax.random.randint(key_row, (), 0, BATCH)
    padding = jnp.where(jnp.arange(BATCH) == chosen, SPAN // 2, padding)
    return padding.astype(jnp.int32)


def raised(values, key, source, target, blocks, factor):
    def block_of(axis_at):
        return (jnp.arange(values.shape[axis_at]) // (values.shape[axis_at] // blocks)).reshape((-1,) + (1,) * (values.ndim - 1 - axis_at))

    near = jax.random.permutation(key, blocks)[block_of(target)]
    far = (block_of(target) + blocks // 2) % blocks
    return jnp.where((block_of(source) == near) | (block_of(source) == far), factor * values, values)


def level_of(stream_key, extent, cuts, low, largest):
    factor_of = 1.0
    for dim, parts in cuts:
        steps = jax.random.uniform(jax.random.fold_in(jax.random.fold_in(stream_key, 6), dim), (parts,), jnp.float32, low / len(cuts), largest / len(cuts))
        factor_of = factor_of * jnp.repeat(jnp.exp(steps), extent[dim] // parts).reshape((-1,) + (1,) * (len(extent) - 1 - dim))
    return factor_of


def normal_values(stream_key, extent, width, bound, pieces=(), kind=jnp.bfloat16):
    level = level_of(stream_key, extent, pieces, -0.22, 0.18) if pieces else 1.0
    values = jax.random.normal(stream_key, extent, jnp.float32) * width * level
    return jnp.minimum(jnp.maximum(values, -bound), bound).astype(kind)


def gaussian_with(rng, dims, scale, reach, pieces, heavy, held_as=jnp.bfloat16):
    array = scale * jax.random.normal(rng, dims, jnp.float32)
    if pieces:
        array = array * level_of(rng, dims, pieces, -0.22, 0.18)
    return jnp.clip(raised(array, jax.random.fold_in(rng, 3), *heavy), -reach, reach).astype(held_as)


def setup_inputs(seed: int = 0) -> dict:
    arg_keys = jax.random.split(jax.random.key(seed), 13)
    return {
        "inputs": normal_values(arg_keys[0], (BATCH, LEN, D), 1.0, 6.0, ((0, 2), (1, 32))),
        "clip_starts": draw_clip_starts(jax.random.fold_in(arg_keys[12], 71), 0),
        "pad_lengths": draw_pad_lengths(jax.random.fold_in(arg_keys[12], 71), 0),
        "w_query": normal_values(arg_keys[3], (D, D), D ** -0.5, 0.125, ((0, 64), (1, 2))),
        "w_key": normal_values(arg_keys[4], (D, D), D ** -0.5, 0.125, ((0, 64), (1, 2))),
        "w_value": normal_values(arg_keys[5], (D, D), D ** -0.5, 0.125, ((0, 64), (1, 2))),
        "w_out": normal_values(arg_keys[6], (D, D), (D // FRAME) ** -0.5, 0.75, ((0, 2), (1, 64))),
        "w_up": normal_values(arg_keys[7], (D, FF), D ** -0.5, 0.125, ((0, 64), (1, 2))),
        "w_down": normal_values(arg_keys[8], (FF, D), FF ** -0.5, 0.0625, ((0, 2), (1, 64))),
        "gain_first": jnp.clip(1.0 + 0.18 * jax.random.normal(arg_keys[9], (D,), jnp.float32), 0.099609375, 1.8984375).astype(jnp.bfloat16),
        "gain_second": jnp.clip(1.0 + 0.18 * jax.random.normal(arg_keys[10], (D,), jnp.float32), 0.099609375, 1.8984375).astype(jnp.bfloat16),
        "cotangent": gaussian_with(arg_keys[11], (BATCH, LEN, D), 1.0, 6.0, ((0, 2), (1, 32)), (1, 2, 32, 2.75)),
    }


epsilon = 1e-05
highest = lax.Precision.HIGHEST

@jax.custom_vjp
def low(v):
    return lax.optimization_barrier(v.astype(jnp.bfloat16)).astype(jnp.float32)

@jax.custom_vjp
def low_back(v):
    return v

def low_keep(v):
    return (low(v), None)

def low_pass(kept, grad):
    return (grad,)

def back_keep(v):
    return (v, None)

def back_low(kept, grad):
    return (low(grad),)
low.defvjp(low_keep, low_pass)
low_back.defvjp(back_keep, back_low)

def normed(value, gain):
    centre = value - lax.optimization_barrier(jnp.mean(value, -1, keepdims=True))
    spread = lax.optimization_barrier(jnp.mean(centre * centre, -1, keepdims=True))
    return centre * lax.rsqrt(spread + epsilon) * gain

def rotary(value, places, direction):
    half_dim = value.shape[-1] // 2
    frequency = 10000.0 ** (-2.0 * jnp.arange(half_dim, dtype=jnp.float32) / value.shape[-1])
    angles = places.astype(jnp.float32)[:, None] * frequency[None, :]
    cosine = jnp.cos(angles)[:, None, :]
    sine = jnp.sin(angles)[:, None, :]
    first = value[..., :half_dim]
    second = value[..., half_dim:]
    return jnp.concatenate([first * cosine - direction * second * sine, direction * first * sine + second * cosine], -1)

def layout(starts, padding, length):
    places = jnp.arange(length, dtype=jnp.int32)
    opened = starts[None, :] <= places[:, None]
    segment = lax.optimization_barrier(jnp.sum(opened.astype(jnp.int32), -1)) - 1
    clip_begin = lax.optimization_barrier(jnp.max(jnp.where(opened, starts[None, :], 0), -1))
    position = places - clip_begin
    frame_no = position // FRAME
    living = places < length - padding
    return (places, segment, position, frame_no, living)

def visible(query_info, key_info):
    query_place, query_segment, query_frame, query_living = query_info
    key_place, key_segment, key_frame, key_living = key_info
    same = query_segment[:, None] == key_segment[None, :]
    earlier = key_frame[None, :] <= query_frame[:, None]
    both = query_living[:, None] & key_living[None, :]
    return (query_place[:, None] == key_place[None, :]) | same & earlier & both

def attend(query, keys, values, info):
    places, segment, position, frame_no, living = info
    length = query.shape[0]
    block = min(512, length)
    count = length // block
    key_info = (places, segment, frame_no, living)

    def one_block(element):
        query_block, block_place, block_segment, block_frame, block_living = element
        mask = visible((block_place, block_segment, block_frame, block_living), key_info)
        scores = jnp.einsum('qhd,khd->hqk', query_block, keys, precision=highest) * HD ** (-0.5)
        scores = low_back(jnp.where(mask[None], scores, -1e+30))
        probs = low(jax.nn.softmax(scores, axis=-1))
        return jnp.einsum('hqk,khd->qhd', probs, values, precision=highest)
    blocks = (query.reshape(count, block, HEADS, HD), places.reshape(count, block), segment.reshape(count, block), frame_no.reshape(count, block), living.reshape(count, block))
    result = lax.map(jax.checkpoint(one_block), blocks)
    return result.reshape(length, HEADS * HD)

def forward_one(params, inputs, starts, padding):
    w_query, w_key, w_value, w_out, w_up, w_down, gain_first, gain_second = params
    length = inputs.shape[0]
    info = layout(starts, padding, length)
    normed_one = low(normed(inputs, gain_first))
    query_lin = low_back(jnp.dot(normed_one, w_query, precision=highest)).reshape(length, HEADS, HD)
    key_lin = low_back(jnp.dot(normed_one, w_key, precision=highest)).reshape(length, HEADS, HD)
    value_lin = jnp.dot(normed_one, w_value, precision=highest).reshape(length, HEADS, HD)
    queries = low(rotary(query_lin, info[2], 1.0))
    keys = low(rotary(key_lin, info[2], 1.0))
    values = low_back(low(value_lin))
    mixed = low_back(low(attend(queries, keys, values, info)))
    middle = inputs + low_back(jnp.dot(mixed, w_out, precision=highest))
    normed_two = low(normed(middle, gain_second))
    hidden = low_back(jnp.dot(normed_two, w_up, precision=highest))
    active = low(jax.nn.gelu(hidden, approximate=False))
    return middle + low_back(jnp.dot(active, w_down, precision=highest))

def reference(inputs, clip_starts, pad_lengths, w_query, w_key, w_value, w_out, w_up, w_down, gain_first, gain_second, cotangent):
    params = tuple((w.astype(jnp.float32) for w in (w_query, w_key, w_value, w_out, w_up, w_down, gain_first, gain_second)))

    def one_sequence(totals, element):
        seq_inputs, seq_cotangent, starts, padding = element
        result, pullback = jax.vjp(lambda p, v: forward_one(p, v, starts, padding), params, seq_inputs)
        gradients, grad_in = pullback(seq_cotangent)
        totals = jax.tree.map(lambda a, b: a + b, totals, gradients)
        return (totals, (result.astype(jnp.bfloat16), grad_in))
    zero_grads = jax.tree.map(jnp.zeros_like, params)
    totals, (outputs, grad_inputs) = lax.scan(one_sequence, zero_grads, (inputs.astype(jnp.float32), cotangent.astype(jnp.float32), clip_starts, pad_lengths))
    return (outputs, grad_inputs, totals[0], totals[1], totals[2], totals[3], totals[4], totals[5], totals[6], totals[7])
```

```python
import functools

import jax
import jax.numpy as jnp
from jax import lax
from jax.experimental import pallas as pl
from jax.experimental.pallas import tpu as pltpu
from jax.sharding import Mesh
from jax.sharding import PartitionSpec as P

MESH = pl.DeviceIdType.MESH
HD = 128
FRAME = 32
LEN = 4096
D = 2048
ROWS = 128
BLOCK = 256
ZY = ("z", "y")
epsilon = 1e-05
scale = HD**-0.5
f32 = jnp.float32
bf16 = jnp.bfloat16


def params(collective_id=None, vmem=48, **kw):
    if collective_id is not None:
        kw = dict(collective_id=collective_id, has_side_effects=True, **kw)
    return pltpu.CompilerParams(vmem_limit_bytes=vmem * 2**20, **kw)


def vmem_specs(n):
    return [pl.BlockSpec(memory_space=pltpu.VMEM)] * n


def greet(peers):
    barrier = pltpu.get_barrier_semaphore()
    for peer in peers:
        pl.semaphore_signal(barrier, inc=1, device_id=peer, device_id_type=MESH)
    pl.semaphore_wait(barrier, len(peers))


def remote(src, dst, send, recv, peer):
    return pltpu.make_async_remote_copy(
        src_ref=src, dst_ref=dst, send_sem=send, recv_sem=recv, device_id=peer, device_id_type=MESH
    )


def quarter_kernel(count, *refs):
    srcs, dsts = refs[:count], refs[count : 2 * count]
    send, recv = refs[2 * count :]
    d, c = lax.axis_index("dp"), lax.axis_index("c")
    me = 2 * d + c
    others = [(d, 1 - c), (1 - d, c), (1 - d, 1 - c)]
    peers = [{"dp": a, "c": b} for a, b in others]
    greet(peers)
    out = []
    for k, (a, b) in enumerate(others):
        for i in range(count):
            copy = remote(srcs[i].at[2 * a + b], dsts[i].at[me], send.at[k, i], recv.at[k, i], peers[k])
            copy.start()
            out.append(copy)
    for i in range(count):
        dsts[i][me] = srcs[i][me]
    for copy in out:
        copy.wait()


def swap_quarters(collective_id, *arrays):
    n = len(arrays)
    return pl.pallas_call(
        functools.partial(quarter_kernel, n),
        out_shape=[jax.ShapeDtypeStruct(a.shape, a.dtype) for a in arrays],
        in_specs=vmem_specs(n),
        out_specs=vmem_specs(n),
        scratch_shapes=[pltpu.SemaphoreType.DMA((3, n)), pltpu.SemaphoreType.DMA((3, n))],
        compiler_params=params(collective_id),
        name="swap_quarters",
    )(*arrays)


CHUNKS = 4


def rows_kernel(x, o, send, recv, send_on, recv_on, sems):
    d, c, m = lax.axis_index("dp"), lax.axis_index("c"), lax.axis_index("mp")
    me, far = 2 * d + c, 2 * (1 - d) + c
    core = {"c": 1 - c}
    across = {"dp": 1 - d, "mp": 1 - m}
    greet([core, across])
    step = ROWS // CHUNKS
    first = []
    for k in range(CHUNKS):
        rows = pl.ds(k * step, step)
        copy = remote(x.at[rows], o.at[me, rows], send.at[k], recv.at[k], across)
        copy.start()
        first.append(copy)
    near = remote(x, o.at[me], sems.at[0], sems.at[1], core)
    near.start()
    o[me] = x[...]
    onward = []
    for k in range(CHUNKS):
        rows = pl.ds(k * step, step)
        first[k].wait_recv()
        copy = remote(o.at[far, rows], o.at[far, rows], send_on.at[k], recv_on.at[k], core)
        copy.start()
        onward.append(copy)
    near.wait()
    for k in range(CHUNKS):
        onward[k].wait()
        first[k].wait_send()


def gather_rows(x):
    dma = pltpu.SemaphoreType.DMA
    out = pl.pallas_call(
        rows_kernel,
        out_shape=jax.ShapeDtypeStruct((4, *x.shape), x.dtype),
        in_specs=vmem_specs(1),
        out_specs=vmem_specs(1)[0],
        scratch_shapes=[dma((CHUNKS,)), dma((CHUNKS,)), dma((CHUNKS,)), dma((CHUNKS,)), dma((2,))],
        compiler_params=params(1),
        name="gather_rows",
    )(x)
    return out.reshape(4 * x.shape[0], x.shape[1])


def sum_kernel(x, o, from_core, s_here, s_send, from_across, t_send, from_copy, *sems):
    send0, recv0, send1, recv1, send2, recv2 = sems
    d, c, m = lax.axis_index("dp"), lax.axis_index("c"), lax.axis_index("mp")
    core = {"c": 1 - c}
    across = {"dp": 1 - d, "mp": 1 - m}
    copy_of = {"mp": 1 - m}
    greet([core, across, copy_of])
    step = ROWS // CHUNKS
    rows = [pl.ds(k * step, step) for k in range(CHUNKS)]
    zero, one, two = [], [], []
    for k in range(CHUNKS):
        copy = remote(x.at[:, 1 - c, rows[k]], from_core.at[:, rows[k]], send0.at[k], recv0.at[k], core)
        copy.start()
        zero.append(copy)
    for k in range(CHUNKS):
        zero[k].wait_recv()
        s_send[rows[k]] = (
            x[1 - d, c, rows[k]].astype(f32) + from_core[1 - d, rows[k]].astype(f32)
        ).astype(bf16)
        copy = remote(s_send.at[rows[k]], from_across.at[rows[k]], send1.at[k], recv1.at[k], across)
        copy.start()
        one.append(copy)
        s_here[rows[k]] = x[d, c, rows[k]].astype(f32) + from_core[d, rows[k]].astype(f32)
    for k in range(CHUNKS):
        one[k].wait_recv()
        t_send[rows[k]] = (s_here[rows[k]] + from_across[rows[k]].astype(f32)).astype(bf16)
        copy = remote(t_send.at[rows[k]], from_copy.at[rows[k]], send2.at[k], recv2.at[k], copy_of)
        copy.start()
        two.append(copy)
    for k in range(CHUNKS):
        two[k].wait_recv()
        o[rows[k]] = t_send[rows[k]].astype(f32) + from_copy[rows[k]].astype(f32)
    for k in range(CHUNKS):
        zero[k].wait_send()
        one[k].wait_send()
        two[k].wait_send()


def sum_rows(x):
    wide = x.shape[-1]
    dma = pltpu.SemaphoreType.DMA
    return pl.pallas_call(
        sum_kernel,
        out_shape=jax.ShapeDtypeStruct((ROWS, wide), f32),
        in_specs=vmem_specs(1),
        out_specs=vmem_specs(1)[0],
        scratch_shapes=[
            pltpu.VMEM((2, ROWS, wide), bf16),
            pltpu.VMEM((ROWS, wide), f32),
            pltpu.VMEM((ROWS, wide), bf16),
            pltpu.VMEM((ROWS, wide), bf16),
            pltpu.VMEM((ROWS, wide), bf16),
            pltpu.VMEM((ROWS, wide), bf16),
        ]
        + [dma((CHUNKS,))] * 6,
        compiler_params=params(2),
        name="sum_rows",
    )(x.reshape(2, 2, ROWS, wide))


def ring(axis, size):
    me = lax.axis_index(axis)
    places = [lax.rem(me + k, size) for k in (1, 3, 2)]
    return me, places, [{axis: p} for p in places]


def spread_kernel(x, q, kv, *sems):
    sq, rq, sk, rk, sy, ry = sems
    z, zs, z_peers = ring("z", 4)
    y, ys, y_peers = ring("y", 4)
    greet(z_peers + y_peers)
    first, last, along = [], [], []
    for k in range(3):
        copy = remote(x.at[zs[k], pl.ds(1, 2)], kv.at[z, y], sk.at[k], rk.at[k], z_peers[k])
        copy.start()
        first.append(copy)
    for k in range(3):
        copy = remote(x.at[zs[k], 0], q.at[z], sq.at[k], rq.at[k], z_peers[k])
        copy.start()
        last.append(copy)

    def onward(place, k):
        for j in range(3):
            copy = remote(kv.at[place, y], kv.at[place, y], sy.at[k, j], ry.at[k, j], y_peers[j])
            copy.start()
            along.append(copy)

    q[z] = x[z, 0]
    kv[z, y] = x[z, pl.ds(1, 2)]
    onward(z, 3)
    for k in range(3):
        first[k].wait_recv()
        onward(lax.rem(z + (3, 1, 2)[k], 4), k)
    for copy in last + along:
        copy.wait()
    for copy in first:
        copy.wait_send()


def spread(x):
    dma = pltpu.SemaphoreType.DMA
    return pl.pallas_call(
        spread_kernel,
        out_shape=[
            jax.ShapeDtypeStruct((4, BLOCK, HD), bf16),
            jax.ShapeDtypeStruct((4, 4, 2, BLOCK, HD), bf16),
        ],
        in_specs=vmem_specs(1),
        out_specs=vmem_specs(2),
        scratch_shapes=[dma((3,))] * 4 + [dma((4, 3))] * 2,
        compiler_params=params(3),
        name="spread",
    )(x)


def turn_kernel(x, o, send, recv):
    z, zs, z_peers = ring("z", 4)
    greet(z_peers)
    out = []
    for k in range(3):
        copy = remote(x.at[zs[k]], o.at[z], send.at[k], recv.at[k], z_peers[k])
        copy.start()
        out.append(copy)
    o[z] = x[z]
    for copy in out:
        copy.wait()


def turn(x):
    dma = pltpu.SemaphoreType.DMA
    return pl.pallas_call(
        turn_kernel,
        out_shape=jax.ShapeDtypeStruct(x.shape, x.dtype),
        in_specs=vmem_specs(1),
        out_specs=vmem_specs(1)[0],
        scratch_shapes=[dma((3,))] * 2,
        compiler_params=params(4),
        name="turn",
    )(x)


def collect_kernel(dq, dkv, o, from_y, total, *sems):
    sq, rq, sk, rk, sy, ry = sems
    z, zs, z_peers = ring("z", 4)
    y, ys, y_peers = ring("y", 4)
    greet(z_peers + y_peers)
    along, last = [], []
    order = [zs[0], zs[1], zs[2], z]
    for k in range(4):
        for j in range(3):
            copy = remote(
                dkv.at[order[k], ys[j]], from_y.at[j, k], sy.at[k, j], ry.at[k, j], y_peers[j]
            )
            copy.start()
            along.append(copy)
    for k in range(3):
        copy = remote(dq.at[zs[k]], o.at[z, 0], sq.at[k], rq.at[k], z_peers[k])
        copy.start()
        last.append(copy)
    o[z, 0] = dq[z]
    for k in range(4):
        for j in range(3):
            along[3 * k + j].wait_recv()
        summed = (
            dkv[order[k], y].astype(f32)
            + from_y[0, k].astype(f32)
            + from_y[1, k].astype(f32)
            + from_y[2, k].astype(f32)
        ).astype(bf16)
        if k < 3:
            total[k] = summed
            copy = remote(total.at[k], o.at[z, pl.ds(1, 2)], sk.at[k], rk.at[k], z_peers[k])
            copy.start()
            last.append(copy)
        else:
            o[z, pl.ds(1, 2)] = summed
    for copy in last:
        copy.wait()
    for copy in along:
        copy.wait_send()


def collect(dq, dkv):
    dma = pltpu.SemaphoreType.DMA
    return pl.pallas_call(
        collect_kernel,
        out_shape=jax.ShapeDtypeStruct((4, 3, BLOCK, HD), bf16),
        in_specs=vmem_specs(2),
        out_specs=vmem_specs(1)[0],
        scratch_shapes=[
            pltpu.VMEM((3, 4, 2, BLOCK, HD), bf16),
            pltpu.VMEM((3, 2, BLOCK, HD), bf16),
        ]
        + [dma((3,))] * 4
        + [dma((4, 3))] * 2,
        compiler_params=params(5),
        name="collect",
    )(dq, dkv)


def reach(info, block):
    t = block * BLOCK + lax.broadcasted_iota(jnp.int32, (BLOCK, 1), 0)
    begin = jnp.where(t >= info[2], info[2], jnp.where(t >= info[1], info[1], info[0]))
    end = jnp.minimum((t // FRAME + 1) * FRAME, info[3])
    living = t < info[3]
    return jnp.where(living, begin, t), jnp.where(living, end, t + 1)


def dot_t(a, b):
    return lax.dot_general(a, b, (((1,), (1,)), ((), ())), preferred_element_type=f32)


def dot_l(a, b):
    return lax.dot_general(a, b, (((0,), (0,)), ((), ())), preferred_element_type=f32)


def visible_scores(q, k, j, low, high):
    s = dot_t(q, k) * scale
    at = j * BLOCK + lax.broadcasted_iota(jnp.int32, (1, BLOCK), 1)
    return jnp.where((at >= low) & (at < high), s, -1e30)


def attend_kernel(info, q_ref, kv_ref, o_ref, lse_ref):
    block = 4 * pl.program_id(0) + info[4]
    low, high = reach(info, block)
    q = q_ref[0]

    def step(j, state):
        top, total, acc = state
        s = visible_scores(q, kv_ref[j, 0], j, low, high)
        now = jnp.maximum(top, jnp.max(s, -1, keepdims=True))
        p = jnp.exp(s - now)
        shrink = jnp.exp(top - now)
        total = total * shrink + jnp.sum(p, -1, keepdims=True)
        acc = acc * shrink + jnp.dot(p.astype(bf16), kv_ref[j, 1], preferred_element_type=f32)
        return now, total, acc

    top, total, acc = lax.fori_loop(
        0,
        block + 1,
        step,
        (jnp.full((BLOCK, 1), -1e30, f32), jnp.zeros((BLOCK, 1), f32), jnp.zeros((BLOCK, HD), f32)),
    )
    o_ref[0] = acc / total
    lse_ref[0] = jnp.broadcast_to(top + jnp.log(total), (BLOCK, HD))


def attend(info, q, kv):
    return pl.pallas_call(
        attend_kernel,
        grid=(4,),
        out_shape=[jax.ShapeDtypeStruct((4, BLOCK, HD), f32)] * 2,
        in_specs=[
            pl.BlockSpec(memory_space=pltpu.SMEM),
            pl.BlockSpec((1, BLOCK, HD), lambda i: (i, 0, 0)),
            pl.BlockSpec((16, 2, BLOCK, HD), lambda i: (0, 0, 0, 0)),
        ],
        out_specs=[pl.BlockSpec((1, BLOCK, HD), lambda i: (i, 0, 0))] * 2,
        compiler_params=params(),
        cost_estimate=pl.CostEstimate(flops=20 * 10**9, bytes_accessed=4 * 10**6, transcendentals=10**6),
        name="attend",
    )(info, q, kv.reshape(16, 2, BLOCK, HD))


def attend_back_kernel(info, q_ref, kv_ref, o_ref, lse_ref, do_ref, dq_ref, dkv_ref, acc):
    i = pl.program_id(0)
    block = 4 * i + info[4]
    low, high = reach(info, block)
    q, do = q_ref[0], do_ref[0]
    lse = lse_ref[0][:, :1]
    inner = jnp.sum(o_ref[0] * do.astype(f32), -1, keepdims=True)

    @pl.when(i == 0)
    def _():
        acc[...] = jnp.zeros_like(acc)

    def step(j, dq):
        k, v = kv_ref[j, 0], kv_ref[j, 1]
        p = jnp.exp(visible_scores(q, k, j, low, high) - lse)
        acc[j, 1] += dot_l(p.astype(bf16), do)
        ds = (p * (dot_t(do, v) - inner)).astype(bf16)
        acc[j, 0] += dot_l(ds, q)
        return dq + jnp.dot(ds, k, preferred_element_type=f32)

    dq = lax.fori_loop(0, block + 1, step, jnp.zeros((BLOCK, HD), f32))
    dq_ref[0] = (dq * scale).astype(bf16)

    @pl.when(i == 3)
    def _():
        def cast(j, _):
            dkv_ref[j, 0] = (acc[j, 0] * scale).astype(bf16)
            dkv_ref[j, 1] = acc[j, 1].astype(bf16)
            return 0

        lax.fori_loop(0, 16, cast, 0)


def attend_back(info, q, kv, o, lse, do):
    dq, dkv = pl.pallas_call(
        attend_back_kernel,
        grid=(4,),
        out_shape=[
            jax.ShapeDtypeStruct((4, BLOCK, HD), bf16),
            jax.ShapeDtypeStruct((16, 2, BLOCK, HD), bf16),
        ],
        in_specs=[
            pl.BlockSpec(memory_space=pltpu.SMEM),
            pl.BlockSpec((1, BLOCK, HD), lambda i: (i, 0, 0)),
            pl.BlockSpec((16, 2, BLOCK, HD), lambda i: (0, 0, 0, 0)),
        ]
        + [pl.BlockSpec((1, BLOCK, HD), lambda i: (i, 0, 0))] * 3,
        out_specs=[
            pl.BlockSpec((1, BLOCK, HD), lambda i: (i, 0, 0)),
            pl.BlockSpec((16, 2, BLOCK, HD), lambda i: (0, 0, 0, 0)),
        ],
        scratch_shapes=[pltpu.VMEM((16, 2, BLOCK, HD), f32)],
        compiler_params=params(),
        cost_estimate=pl.CostEstimate(flops=30 * 10**9, bytes_accessed=8 * 10**6, transcendentals=10**6),
        name="attend_back",
    )(info, q, kv.reshape(16, 2, BLOCK, HD), o, lse, do)
    return dq, dkv.reshape(4, 4, 2, BLOCK, HD)


def to_inner(x):
    return x.reshape(-1, 2, 16, 64).swapaxes(1, 2).reshape(-1, D)


def to_outer(x):
    return x.reshape(-1, 16, 2, 64).swapaxes(1, 2).reshape(-1, D)


def norm(value):
    centre = value - jnp.mean(value, -1, keepdims=True)
    r = lax.rsqrt(jnp.mean(centre * centre, -1, keepdims=True) + epsilon)
    return centre * r, r


def norm_back(grad, n, r, gain):
    e = grad * gain
    return r * (e - jnp.mean(e, -1, keepdims=True) - n * jnp.mean(e * n, -1, keepdims=True))


def turned(x, cosine, sine, direction):
    a, b = x[..., :64], x[..., 64:]
    return jnp.concatenate([a * cosine - direction * b * sine, direction * a * sine + b * cosine], -1)


def quarters(w):
    return w.reshape(w.shape[0], 4, -1).swapaxes(0, 1)


def joined(w):
    return w.swapaxes(0, 1).reshape(w.shape[1], -1)


def gelu(v):
    return jax.nn.gelu(v, approximate=False)


def gather_weights(x):
    return lax.all_gather(x, ZY, axis=0, tiled=True)


def scatter_grads(x):
    return lax.psum_scatter(x, ZY, scatter_dimension=0, tiled=True)


def local(
    inputs,
    clip_starts,
    pad_lengths,
    w_query,
    w_key,
    w_value,
    w_out,
    w_up,
    w_down,
    gain_first,
    gain_second,
    cotangent,
):
    z, y = lax.axis_index("z"), lax.axis_index("y")
    living = LEN - pad_lengths
    side = jnp.concatenate(
        [
            gain_first[:, None],
            gain_second[:, None],
            jnp.broadcast_to(clip_starts, (32, 3)).astype(bf16),
            jnp.broadcast_to(pad_lengths[None], (32, 1)).astype(bf16),
            jnp.zeros((32, HD - 6), bf16),
        ],
        1,
    )
    first = jnp.concatenate(
        [quarters(w_query), quarters(w_key), quarters(w_value), jnp.broadcast_to(side, (4, 32, HD))], -1
    )
    second = jnp.concatenate([quarters(w_out.T), quarters(w_up)], -1)
    third = quarters(w_down.T)
    first, second, third = swap_quarters(0, first, second, third)
    first = gather_weights(first.reshape(HD, -1))
    second = gather_weights(second.reshape(HD, -1))
    down = gather_weights(third.reshape(HD, -1))

    side = first[:, 768:]
    gains = side[:, :2].astype(f32).T
    gain_one, gain_two = gains[0], gains[1]
    facts = side[:128:64, 2:6].astype(jnp.int32)
    begins, ends = facts[:, :3], LEN - facts[:, 3]

    x = to_inner(inputs[0]).astype(f32)
    n_one, r_one = norm(x)
    normed_one = gather_rows((n_one * gain_one).astype(bf16))
    incoming = to_inner(cotangent[0])
    incoming_all = gather_rows(incoming)

    places = (4 * z + y) * BLOCK + jnp.arange(BLOCK, dtype=jnp.int32)
    opened = begins[:, None, :] <= places[None, :, None]
    position = places - jnp.max(jnp.where(opened, begins[:, None, :], 0), -1)
    frequency = 10000.0 ** (-2.0 * jnp.arange(HD // 2, dtype=f32) / HD)
    angles = position.astype(f32)[..., None] * frequency
    cosine, sine = jnp.cos(angles)[:, :, None], jnp.sin(angles)[:, :, None]

    lin = jnp.dot(normed_one, first, preferred_element_type=f32)
    lin = lin[:, :768].reshape(2, BLOCK, 3, 2, HD)
    query = turned(lin[:, :, 0], cosine, sine, 1.0)
    key = turned(lin[:, :, 1], cosine, sine, 1.0)
    qkv = jnp.stack([query, key, lin[:, :, 2]], 0).astype(bf16)
    qkv = qkv.transpose(1, 3, 0, 2, 4).reshape(4, 3, BLOCK, HD)
    q, kv = spread(qkv)
    mine = z // 2
    info = jnp.concatenate(
        [lax.dynamic_index_in_dim(begins, mine, 0, False), lax.dynamic_index_in_dim(ends, mine, 0), y[None]]
    ).astype(jnp.int32)
    o, lse = attend(info, q, kv)
    mixed = turn(o.astype(bf16))
    mixed = mixed.reshape(2, 2, BLOCK, HD).swapaxes(1, 2).reshape(512, 2 * HD)

    out = second[:, :256]
    middle = x + sum_rows(dot_t(mixed, out).astype(bf16))
    n_two, r_two = norm(middle)
    normed_two = gather_rows((n_two * gain_two).astype(bf16))
    hidden = jnp.dot(normed_two, second, preferred_element_type=f32)[:, 256:]
    active, pull = jax.vjp(gelu, hidden)
    active = active.astype(bf16)
    grad_active = jnp.dot(incoming_all, down, preferred_element_type=f32)
    grad_hidden = pull(grad_active)[0].astype(bf16)
    grad_normed_two = sum_rows(dot_t(jnp.pad(grad_hidden, ((0, 0), (256, 0))), second).astype(bf16))
    grad_middle = incoming.astype(f32) + norm_back(grad_normed_two, n_two, r_two, gain_two)
    branch = gather_rows(grad_middle.astype(bf16))

    grad_down = scatter_grads(dot_l(incoming_all, active).astype(bf16))
    grad_up = scatter_grads(dot_l(normed_two, grad_hidden).astype(bf16))

    grad_mixed = jnp.dot(branch, out, preferred_element_type=f32).astype(bf16)
    grad_mixed = grad_mixed.reshape(2, BLOCK, 2, HD).swapaxes(1, 2).reshape(4, BLOCK, HD)
    grad_out = scatter_grads(dot_l(branch, mixed).astype(bf16))
    dq, dkv = attend_back(info, q, kv, o, lse, turn(grad_mixed))
    output = middle + sum_rows(dot_t(active, down).astype(bf16))
    grads = collect(dq, dkv).reshape(2, 2, 3, BLOCK, HD).transpose(2, 0, 3, 1, 4)
    grad_query = turned(grads[0].astype(f32), cosine, sine, -1.0).astype(bf16)
    grad_key = turned(grads[1].astype(f32), cosine, sine, -1.0).astype(bf16)
    grad_lin = jnp.stack([grad_query, grad_key, grads[2]], 2).reshape(512, 768)

    grad_normed_one = sum_rows(dot_t(jnp.pad(grad_lin, ((0, 0), (0, HD))), first).astype(bf16))
    grad_input = grad_middle + norm_back(grad_normed_one, n_one, r_one, gain_one)
    gain_grads = jnp.stack([jnp.sum(grad_normed_one * n_one, 0), jnp.sum(grad_normed_two * n_two, 0)], 1)
    grad_first = jnp.concatenate(
        [dot_l(normed_one, grad_lin).astype(bf16), jnp.pad(gain_grads, ((0, 0), (0, HD - 2))).astype(bf16)], 1
    )
    grad_first = scatter_grads(grad_first)

    grad_first, grad_out, grad_up, grad_down = swap_quarters(
        6, *[g.reshape(4, 32, -1) for g in (grad_first, grad_out, grad_up, grad_down)]
    )
    grad_first, grad_out, grad_up, grad_down = [
        g.astype(f32) for g in (grad_first, grad_out, grad_up, grad_down)
    ]
    gain_grads = jnp.sum(grad_first[:, :, 768:770], 0)
    return (
        to_outer(output).astype(bf16)[None],
        to_outer(grad_input)[None],
        joined(grad_first[:, :, :256]),
        joined(grad_first[:, :, 256:512]),
        joined(grad_first[:, :, 512:768]),
        joined(grad_out).T,
        joined(grad_up),
        joined(grad_down).T,
        gain_grads[:, 0],
        gain_grads[:, 1],
    )


def solution(mesh):
    split = Mesh(mesh.devices.reshape(2, 4, 4, 2, 2), ("dp", "z", "y", "c", "mp"))
    seq = ("z", "y", "c")
    weights = ("dp", "z", "y", "c")
    tokens = P("dp", seq, None)
    wide, tall = P(weights, "mp"), P("mp", weights)
    return jax.shard_map(
        local,
        mesh=split,
        in_specs=(tokens, P("dp", None), P("dp"), wide, wide, wide, tall, wide, tall, P(weights), P(weights), tokens),
        out_specs=(tokens, tokens, wide, wide, wide, tall, wide, tall, P(weights), P(weights)),
        check_vma=False,
    )
```

```python
import functools

import jax
import jax.numpy as jnp
from jax import lax
from jax.experimental import pallas as pl
from jax.experimental.pallas import tpu as pltpu
from jax.sharding import Mesh
from jax.sharding import PartitionSpec as P

MESH = pl.DeviceIdType.MESH
HD = 128
FRAME = 32
LEN = 4096
D = 2048
ROWS = 128
BLOCK = 256
ZY = ("z", "y")
epsilon = 1e-05
scale = HD**-0.5
f32 = jnp.float32
bf16 = jnp.bfloat16


def params(collective_id=None, vmem=48, **kw):
    if collective_id is not None:
        kw = dict(collective_id=collective_id, has_side_effects=True, **kw)
    return pltpu.CompilerParams(vmem_limit_bytes=vmem * 2**20, **kw)


def vmem_specs(n):
    return [pl.BlockSpec(memory_space=pltpu.VMEM)] * n


def greet(peers):
    barrier = pltpu.get_barrier_semaphore()
    for peer in peers:
        pl.semaphore_signal(barrier, inc=1, device_id=peer, device_id_type=MESH)
    pl.semaphore_wait(barrier, len(peers))


def remote(src, dst, send, recv, peer):
    return pltpu.make_async_remote_copy(
        src_ref=src, dst_ref=dst, send_sem=send, recv_sem=recv, device_id=peer, device_id_type=MESH
    )


def started(copies, src, dst, send, recv, peer):
    copy = remote(src, dst, send, recv, peer)
    copy.start()
    copies.append(copy)
    return copy


class Sems:
    def __init__(self, send, recv):
        self.send, self.recv, self.used = send, recv, 0

    def take(self):
        k = self.used
        self.used += 1
        return self.send.at[k], self.recv.at[k]


def sem_pair(n):
    return [pltpu.SemaphoreType.DMA((n,)), pltpu.SemaphoreType.DMA((n,))]


def tensor_place():
    d, c, m = lax.axis_index("dp"), lax.axis_index("c"), lax.axis_index("mp")
    return d, c, m, {"c": 1 - c}, {"dp": 1 - d, "mp": 1 - m}, {"mp": 1 - m}


def ring(axis, size=4):
    me = lax.axis_index(axis)
    up, down, far = (lax.rem(me + k, size) for k in (1, size - 1, 2))
    return me, up, down, far, {axis: up}, {axis: down}


def added(*values):
    total = values[0].astype(f32)
    for v in values[1:]:
        total = total + v.astype(f32)
    return total


def run(*protocols):
    live = list(protocols)
    while live:
        for p in list(live):
            try:
                next(p)
            except StopIteration:
                live.remove(p)


def swap_plan(srcs, dsts, sems):
    d, c = lax.axis_index("dp"), lax.axis_index("c")
    me = 2 * d + c
    copies = []
    for a, b in [(d, 1 - c), (1 - d, c), (1 - d, 1 - c)]:
        for src, dst in zip(srcs, dsts):
            started(copies, src.at[2 * a + b], dst(me), *sems.take(), {"dp": a, "c": b})
    for src, dst in zip(srcs, dsts):
        dst(me)[...] = src[me]
    yield
    for copy in copies:
        copy.wait_recv()
    yield
    for copy in copies:
        copy.wait_send()


def swap_peers():
    d, c = lax.axis_index("dp"), lax.axis_index("c")
    return [{"dp": 1 - d}, {"dp": 1 - d, "c": 1 - c}]


def quarter_kernel(count, *refs):
    srcs, dsts = refs[:count], refs[count : 2 * count]
    sems = Sems(*refs[2 * count :])
    greet([tensor_place()[3], *swap_peers()])
    run(swap_plan(srcs, [lambda me, o=o: o.at[me] for o in dsts], sems))


def swap_quarters(collective_id, *arrays):
    n = len(arrays)
    return pl.pallas_call(
        functools.partial(quarter_kernel, n),
        out_shape=[jax.ShapeDtypeStruct(a.shape, a.dtype) for a in arrays],
        in_specs=vmem_specs(n),
        out_specs=vmem_specs(n),
        scratch_shapes=sem_pair(3 * n),
        compiler_params=params(collective_id),
        name="swap_quarters",
    )(*arrays)


CHUNKS = 4
HALF = ROWS // 2


def rows_plan(x, o, sems):
    d, c, m, core, across, copy_of = tensor_place()
    me, far = 2 * d + c, 2 * (1 - d) + c
    copies, firsts, seconds = [], [], []
    step = HALF // 2
    mine = [pl.ds(m * HALF + k * step, step) for k in range(2)]
    other = [pl.ds((1 - m) * HALF + k * step, step) for k in range(2)]
    for rows in mine:
        firsts.append(started(copies, x.at[rows], o.at[me, rows], *sems.take(), across))
    near = started(copies, x, o.at[me], *sems.take(), core)
    o[me] = x[...]
    yield
    for k, rows in enumerate(other):
        firsts[k].wait_recv()
        seconds.append(started(copies, o.at[far, rows], o.at[far, rows], *sems.take(), copy_of))
    yield
    lasts = []
    for rows in other:
        lasts.append(started(copies, o.at[far, rows], o.at[far, rows], *sems.take(), core))
    for k, rows in enumerate(mine):
        seconds[k].wait_recv()
        lasts.append(started(copies, o.at[far, rows], o.at[far, rows], *sems.take(), core))
    yield
    near.wait_recv()
    for copy in lasts:
        copy.wait_recv()
    for copy in copies:
        copy.wait_send()


ROWS_SEMS = 9


def rows_kernel(x, o, send, recv):
    greet(tensor_place()[3:])
    run(rows_plan(x, o, Sems(send, recv)))


def gather_rows(x):
    out = pl.pallas_call(
        rows_kernel,
        out_shape=jax.ShapeDtypeStruct((4, *x.shape), x.dtype),
        in_specs=vmem_specs(1),
        out_specs=vmem_specs(1)[0],
        scratch_shapes=sem_pair(ROWS_SEMS),
        compiler_params=params(1),
        name="gather_rows",
    )(x)
    return out.reshape(4 * x.shape[0], x.shape[1])


def sum_plan(x, o, buffers, sems):
    from_core, s_here, s_send, from_across, t_send, from_copy = buffers
    d, c, m, core, across, copy_of = tensor_place()
    step = ROWS // CHUNKS
    rows = [pl.ds(k * step, step) for k in range(CHUNKS)]
    copies, zero, one, two = [], [], [], []
    for r in rows:
        zero.append(started(copies, x.at[:, 1 - c, r], from_core.at[:, r], *sems.take(), core))
    yield
    for k, r in enumerate(rows):
        zero[k].wait_recv()
        s_send[r] = added(x[1 - d, c, r], from_core[1 - d, r]).astype(bf16)
        one.append(started(copies, s_send.at[r], from_across.at[r], *sems.take(), across))
        s_here[r] = added(x[d, c, r], from_core[d, r])
    yield
    for k, r in enumerate(rows):
        one[k].wait_recv()
        t_send[r] = added(s_here[r], from_across[r]).astype(bf16)
        two.append(started(copies, t_send.at[r], from_copy.at[r], *sems.take(), copy_of))
    yield
    for k, r in enumerate(rows):
        two[k].wait_recv()
        o[r] = added(t_send[r], from_copy[r])
    for copy in copies:
        copy.wait_send()


SUM_SEMS = 3 * CHUNKS
SUM_BUFFERS = [
    pltpu.VMEM((2, ROWS, D), bf16),
    pltpu.VMEM((ROWS, D), f32),
    pltpu.VMEM((ROWS, D), bf16),
    pltpu.VMEM((ROWS, D), bf16),
    pltpu.VMEM((ROWS, D), bf16),
    pltpu.VMEM((ROWS, D), bf16),
]


def sum_kernel(x, o, *scratch):
    greet(tensor_place()[3:])
    run(sum_plan(x, o, scratch[:6], Sems(*scratch[6:])))


def sum_rows(x):
    return pl.pallas_call(
        sum_kernel,
        out_shape=jax.ShapeDtypeStruct((ROWS, D), f32),
        in_specs=vmem_specs(1),
        out_specs=vmem_specs(1)[0],
        scratch_shapes=SUM_BUFFERS + sem_pair(SUM_SEMS),
        compiler_params=params(2),
        name="sum_rows",
    )(x.reshape(2, 2, ROWS, D))


def weights_plan(w, first, second, low, sems):
    i0, i_up, i_down, i_far, to_i_up, to_i_down = ring(first)
    j0, j_up, j_down, j_far, to_j_up, to_j_down = ring(second)

    def at(i, j, part, n):
        return w.at[(j, i) if first == "y" else (i, j)].at[pl.ds(low + part, n)]

    copies = []

    def send(ref, peer):
        return started(copies, ref, ref, *sems.take(), peer)

    def along(i):
        return i, send(at(i, j0, 0, 2), to_j_up), send(at(i, j0, 0, 2), to_j_down)

    from_down, from_up = send(at(i0, j0, 0, 2), to_i_up), send(at(i0, j0, 0, 2), to_i_down)
    second_leg = [along(i0)]
    yield
    from_down.wait_recv()
    far_low = send(at(i_down, j0, 0, 1), to_i_up)
    from_up.wait_recv()
    far_high = send(at(i_up, j0, 1, 1), to_i_down)
    second_leg += [along(i_down), along(i_up)]
    yield
    onward = []

    def relay(leg):
        i, a, b = leg
        a.wait_recv()
        onward.append(send(at(i, j_down, 0, 1), to_j_up))
        b.wait_recv()
        onward.append(send(at(i, j_up, 1, 1), to_j_down))

    relay(second_leg[0])
    yield
    far_low.wait_recv()
    far_high.wait_recv()
    second_leg.append(along(i_far))
    for leg in second_leg[1:]:
        yield
        relay(leg)
    yield
    for copy in onward:
        copy.wait_recv()
    for copy in copies:
        copy.wait_send()


WEIGHT_SEMS = 20


def start_kernel(first, second, third, x, w, s2, s3, rows, *sems):
    z, y = lax.axis_index("z"), lax.axis_index("y")
    _, _, _, _, z_up, z_down = ring("z")
    _, _, _, _, y_up, y_down = ring("y")
    greet([*tensor_place()[3:], *swap_peers(), z_up, z_down, y_up, y_down])
    one = Sems(*sems[:2])
    swap_first = swap_plan([first], [lambda me: w.at[z, y, me]], one)
    next(swap_first)
    gather_x = rows_plan(x, rows, Sems(*sems[2:4]))
    next(gather_x)
    swap_rest = swap_plan([second, third], [lambda me: s2.at[me], lambda me: s3.at[me]], one)
    next(swap_rest)
    next(swap_first)
    run(
        weights_plan(w, "y", "z", 0, Sems(*sems[4:6])),
        weights_plan(w, "z", "y", 2, Sems(*sems[6:8])),
        gather_x,
        swap_rest,
        swap_first,
    )


def start(first, second, third, x):
    return pl.pallas_call(
        start_kernel,
        out_shape=[
            jax.ShapeDtypeStruct((4, 4, *first.shape), bf16),
            jax.ShapeDtypeStruct(second.shape, bf16),
            jax.ShapeDtypeStruct(third.shape, bf16),
            jax.ShapeDtypeStruct((4, *x.shape), bf16),
        ],
        in_specs=vmem_specs(4),
        out_specs=vmem_specs(4),
        scratch_shapes=sem_pair(9) + sem_pair(ROWS_SEMS) + sem_pair(WEIGHT_SEMS) + sem_pair(WEIGHT_SEMS),
        compiler_params=params(3),
        name="start",
    )(first, second, third, x)


def spread_plan(x, q, kv, sems):
    z, z_up, z_down, z_far, to_z_up, to_z_down = ring("z")
    y, y_up, y_down, y_far, to_y_up, to_y_down = ring("y")
    far = {"z": z_far}
    copies, firsts, queries, nears, fars = [], [], [], [], []
    both = pl.ds(1, 2)
    peers = [(z_up, to_z_up, z_down), (z_down, to_z_down, z_up), (z_far, far, z_far)]
    for place, peer, _ in peers:
        firsts.append(started(copies, x.at[place, both], kv.at[z, y], *sems.take(), peer))
    kv[z, y] = x[z, both]

    def along(place):
        ref = kv.at[place, y]
        nears.append(
            (place, started(copies, ref, ref, *sems.take(), to_y_up), started(copies, ref, ref, *sems.take(), to_y_down))
        )

    along(z)
    for place, peer, _ in peers:
        queries.append(started(copies, x.at[place, 0], q.at[z], *sems.take(), peer))
    q[z] = x[z, 0]
    yield

    def relay(k):
        place, a, b = nears[k]
        a.wait_recv()
        ref = kv.at[place, y_down, 0]
        fars.append(started(copies, ref, ref, *sems.take(), to_y_up))
        b.wait_recv()
        ref = kv.at[place, y_up, 1]
        fars.append(started(copies, ref, ref, *sems.take(), to_y_down))

    for k, (_, _, source) in enumerate(peers):
        firsts[k].wait_recv()
        along(source)
        yield
        relay(k)
    yield
    relay(3)
    yield
    for copy in queries + fars:
        copy.wait_recv()
    for copy in copies:
        copy.wait_send()


def spread_kernel(x, cot, q, kv, rows, *sems):
    _, _, _, z_far, z_up, z_down = ring("z")
    _, _, _, _, y_up, y_down = ring("y")
    greet([*tensor_place()[3:], z_up, z_down, {"z": z_far}, y_up, y_down])
    run(spread_plan(x, q, kv, Sems(*sems[:2])), rows_plan(cot, rows, Sems(*sems[2:])))


def spread(x, cot):
    return pl.pallas_call(
        spread_kernel,
        out_shape=[
            jax.ShapeDtypeStruct((4, BLOCK, HD), bf16),
            jax.ShapeDtypeStruct((4, 4, 2, BLOCK, HD), bf16),
            jax.ShapeDtypeStruct((4, *cot.shape), bf16),
        ],
        in_specs=vmem_specs(2),
        out_specs=vmem_specs(3),
        scratch_shapes=sem_pair(22) + sem_pair(ROWS_SEMS),
        compiler_params=params(4),
        name="spread",
    )(x, cot)


def turn_kernel(x, o, send, recv):
    z, z_up, z_down, z_far, to_z_up, to_z_down = ring("z")
    peers = [(z_up, to_z_up), (z_down, to_z_down), (z_far, {"z": z_far})]
    greet([peer for _, peer in peers])
    sems, copies = Sems(send, recv), []
    for place, peer in peers:
        started(copies, x.at[place], o.at[z], *sems.take(), peer)
    o[z] = x[z]
    for copy in copies:
        copy.wait()


def turn(x):
    return pl.pallas_call(
        turn_kernel,
        out_shape=jax.ShapeDtypeStruct(x.shape, x.dtype),
        in_specs=vmem_specs(1),
        out_specs=vmem_specs(1)[0],
        scratch_shapes=sem_pair(3),
        compiler_params=params(5),
        name="turn",
    )(x)


def ring_sum(at, axis, buffers, sems, put):
    one, two, passed = buffers
    me, up, down, far, to_up, to_down = ring(axis)
    copies = []
    a = started(copies, at(far, 0), one.at[0], *sems.take(), to_up)
    b = started(copies, at(far, 1), one.at[1], *sems.take(), to_down)
    plain = [
        started(copies, at(up, 1), two.at[0, 1], *sems.take(), to_up),
        started(copies, at(down, 0), two.at[1, 0], *sems.take(), to_down),
    ]
    yield
    a.wait_recv()
    passed[0] = added(at(up, 0)[...], one[0]).astype(bf16)
    plain.append(started(copies, passed.at[0], two.at[0, 0], *sems.take(), to_up))
    b.wait_recv()
    passed[1] = added(at(down, 1)[...], one[1]).astype(bf16)
    plain.append(started(copies, passed.at[1], two.at[1, 1], *sems.take(), to_down))
    yield
    for copy in plain:
        copy.wait_recv()
    for part in range(2):
        put(part, added(at(me, part)[...], two[0, part], two[1, part]))
    yield
    for copy in copies:
        copy.wait_send()


RING_SEMS = 6


def ring_buffers(n, part):
    return [pltpu.VMEM((n, 2, *part), bf16), pltpu.VMEM((n, 2, 2, *part), bf16), pltpu.VMEM((n, 2, *part), bf16)]


def collect_plan(dq, dkv, o, total, buffers, sems):
    z, z_up, z_down, z_far, to_z_up, to_z_down = ring("z")
    y = lax.axis_index("y")
    peers = [(z_up, to_z_up), (z_down, to_z_down), (z_far, {"z": z_far}), (z, None)]
    copies, rings = [], []
    for k, (place, peer) in enumerate(peers):

        def at(i, part, place=place):
            return dkv.at[place, i, part]

        def put(part, value, k=k):
            if k < 3:
                total[k, part] = value.astype(bf16)
            else:
                o[z, 1 + part] = value.astype(bf16)

        rings.append(ring_sum(at, "y", [b.at[k] for b in buffers], sems, put))
    for r in rings:
        next(r)
    for place, peer in peers[:3]:
        started(copies, dq.at[place], o.at[z, 0], *sems.take(), peer)
    o[z, 0] = dq[z]
    yield
    for r in rings:
        next(r)
        yield
    for k, r in enumerate(rings):
        next(r)
        if k < 3:
            started(copies, total.at[k], o.at[z, pl.ds(1, 2)], *sems.take(), peers[k][1])
        yield
    for copy in copies:
        copy.wait()
    run(*rings)


def collect_kernel(dq, dkv, part, o, summed, total, *scratch):
    _, _, _, z_far, z_up, z_down = ring("z")
    _, _, _, _, y_up, y_down = ring("y")
    greet([*tensor_place()[3:], z_up, z_down, {"z": z_far}, y_up, y_down])
    run(
        collect_plan(dq, dkv, o, total, scratch[:3], Sems(*scratch[3:5])),
        sum_plan(part, summed, scratch[5:11], Sems(*scratch[11:])),
    )


def collect(dq, dkv, part):
    return pl.pallas_call(
        collect_kernel,
        out_shape=[jax.ShapeDtypeStruct((4, 3, BLOCK, HD), bf16), jax.ShapeDtypeStruct((ROWS, D), f32)],
        in_specs=vmem_specs(3),
        out_specs=vmem_specs(2),
        scratch_shapes=[pltpu.VMEM((3, 2, BLOCK, HD), bf16)]
        + ring_buffers(4, (BLOCK, HD))
        + sem_pair(4 * RING_SEMS + 6)
        + SUM_BUFFERS
        + sem_pair(SUM_SEMS),
        compiler_params=params(6),
        name="collect",
    )(dq, dkv, part.reshape(2, 2, ROWS, D))


def grads_plan(g, shard, first, second, low, legs, buffers, sems):
    rings = []
    for j in range(4):

        def at(i, part, j=j):
            return g.at[(j, i) if first == "y" else (i, j)].at[low + part]

        def put(part, value, j=j):
            legs[j, part] = value.astype(bf16)

        rings.append(ring_sum(at, first, [b.at[j] for b in buffers], sems, put))
    for r in rings:
        next(r)
    yield
    for r in rings:
        next(r)
    yield
    for r in rings:
        next(r)

    def put_last(part, value):
        shard[low + part] = value.astype(bf16)

    rings.append(ring_sum(lambda i, part: legs.at[i, part], second, [b.at[4] for b in buffers], sems, put_last))
    for _ in range(3):
        next(rings[-1])
        yield
    run(*rings)


def end_kernel(wide, g, part, o, gain, summed, *scratch):
    d, c, m, core, across, copy_of = tensor_place()
    _, _, _, _, z_up, z_down = ring("z")
    _, _, _, _, y_up, y_down = ring("y")
    greet([core, across, copy_of, *swap_peers(), z_up, z_down, y_up, y_down])
    shard, mine, theirs, legs_a, legs_b = scratch[:5]
    scratch = scratch[5:]
    run(
        sum_plan(part, summed, scratch[6:12], Sems(*scratch[12:14])),
        grads_plan(g, shard, "z", "y", 0, legs_a, scratch[:3], Sems(*scratch[14:16])),
        grads_plan(g, shard, "y", "z", 2, legs_b, scratch[3:6], Sems(*scratch[16:18])),
    )
    last = Sems(*scratch[18:])
    run(swap_plan([shard], [lambda me: o.at[me]], last))
    lanes = pl.ds(wide, HD)
    mine[...] = added(o[0, :, lanes], o[1, :, lanes], o[2, :, lanes], o[3, :, lanes])
    copy = remote(mine, theirs, *last.take(), copy_of)
    copy.start()
    copy.wait()
    gain[...] = mine[...] + theirs[...]


def end(g, part):
    block = (32, g.shape[1])
    return pl.pallas_call(
        functools.partial(end_kernel, g.shape[1] - HD),
        out_shape=[
            jax.ShapeDtypeStruct((4, *block), bf16),
            jax.ShapeDtypeStruct((32, HD), f32),
            jax.ShapeDtypeStruct((ROWS, D), f32),
        ],
        in_specs=vmem_specs(2),
        out_specs=vmem_specs(3),
        scratch_shapes=[
            pltpu.VMEM((4, *block), bf16),
            pltpu.VMEM((32, HD), f32),
            pltpu.VMEM((32, HD), f32),
            pltpu.VMEM((4, 2, *block), bf16),
            pltpu.VMEM((4, 2, *block), bf16),
        ]
        + ring_buffers(5, block)
        + ring_buffers(5, block)
        + SUM_BUFFERS
        + sem_pair(SUM_SEMS)
        + sem_pair(5 * RING_SEMS)
        + sem_pair(5 * RING_SEMS)
        + sem_pair(4),
        compiler_params=params(7),
        name="end",
    )(g.reshape(4, 4, 4, *block), part.reshape(2, 2, ROWS, D))


def reach(info, block):
    t = block * BLOCK + lax.broadcasted_iota(jnp.int32, (BLOCK, 1), 0)
    begin = jnp.where(t >= info[2], info[2], jnp.where(t >= info[1], info[1], info[0]))
    end = jnp.minimum((t // FRAME + 1) * FRAME, info[3])
    living = t < info[3]
    return jnp.where(living, begin, t), jnp.where(living, end, t + 1)


def dot_t(a, b):
    return lax.dot_general(a, b, (((1,), (1,)), ((), ())), preferred_element_type=f32)


def dot_l(a, b):
    return lax.dot_general(a, b, (((0,), (0,)), ((), ())), preferred_element_type=f32)


def visible_scores(q, k, j, low, high):
    s = dot_t(q, k) * scale
    at = j * BLOCK + lax.broadcasted_iota(jnp.int32, (1, BLOCK), 1)
    return jnp.where((at >= low) & (at < high), s, -1e30)


def attend_kernel(info, q_ref, kv_ref, o_ref, lse_ref):
    block = 4 * pl.program_id(0) + info[4]
    low, high = reach(info, block)
    q = q_ref[0]

    def step(j, state):
        top, total, acc = state
        s = visible_scores(q, kv_ref[j, 0], j, low, high)
        now = jnp.maximum(top, jnp.max(s, -1, keepdims=True))
        p = jnp.exp(s - now)
        shrink = jnp.exp(top - now)
        total = total * shrink + jnp.sum(p, -1, keepdims=True)
        acc = acc * shrink + jnp.dot(p.astype(bf16), kv_ref[j, 1], preferred_element_type=f32)
        return now, total, acc

    top, total, acc = lax.fori_loop(
        0,
        block + 1,
        step,
        (jnp.full((BLOCK, 1), -1e30, f32), jnp.zeros((BLOCK, 1), f32), jnp.zeros((BLOCK, HD), f32)),
    )
    o_ref[0] = acc / total
    lse_ref[0] = jnp.broadcast_to(top + jnp.log(total), (BLOCK, HD))


def attend(info, q, kv):
    return pl.pallas_call(
        attend_kernel,
        grid=(4,),
        out_shape=[jax.ShapeDtypeStruct((4, BLOCK, HD), f32)] * 2,
        in_specs=[
            pl.BlockSpec(memory_space=pltpu.SMEM),
            pl.BlockSpec((1, BLOCK, HD), lambda i: (i, 0, 0)),
            pl.BlockSpec((16, 2, BLOCK, HD), lambda i: (0, 0, 0, 0)),
        ],
        out_specs=[pl.BlockSpec((1, BLOCK, HD), lambda i: (i, 0, 0))] * 2,
        compiler_params=params(),
        cost_estimate=pl.CostEstimate(flops=20 * 10**9, bytes_accessed=4 * 10**6, transcendentals=10**6),
        name="attend",
    )(info, q, kv.reshape(16, 2, BLOCK, HD))


def attend_back_kernel(info, q_ref, kv_ref, o_ref, lse_ref, do_ref, dq_ref, dkv_ref, acc):
    i = pl.program_id(0)
    block = 4 * i + info[4]
    low, high = reach(info, block)
    q, do = q_ref[0], do_ref[0]
    lse = lse_ref[0][:, :1]
    inner = jnp.sum(o_ref[0] * do.astype(f32), -1, keepdims=True)

    @pl.when(i == 0)
    def _():
        acc[...] = jnp.zeros_like(acc)

    def step(j, dq):
        k, v = kv_ref[j, 0], kv_ref[j, 1]
        p = jnp.exp(visible_scores(q, k, j, low, high) - lse)
        acc[j, 1] += dot_l(p.astype(bf16), do)
        ds = (p * (dot_t(do, v) - inner)).astype(bf16)
        acc[j, 0] += dot_l(ds, q)
        return dq + jnp.dot(ds, k, preferred_element_type=f32)

    dq = lax.fori_loop(0, block + 1, step, jnp.zeros((BLOCK, HD), f32))
    dq_ref[0] = (dq * scale).astype(bf16)

    @pl.when(i == 3)
    def _():
        def cast(j, _):
            dkv_ref[j, 0] = (acc[j, 0] * scale).astype(bf16)
            dkv_ref[j, 1] = acc[j, 1].astype(bf16)
            return 0

        lax.fori_loop(0, 16, cast, 0)


def attend_back(info, q, kv, o, lse, do):
    dq, dkv = pl.pallas_call(
        attend_back_kernel,
        grid=(4,),
        out_shape=[
            jax.ShapeDtypeStruct((4, BLOCK, HD), bf16),
            jax.ShapeDtypeStruct((16, 2, BLOCK, HD), bf16),
        ],
        in_specs=[
            pl.BlockSpec(memory_space=pltpu.SMEM),
            pl.BlockSpec((1, BLOCK, HD), lambda i: (i, 0, 0)),
            pl.BlockSpec((16, 2, BLOCK, HD), lambda i: (0, 0, 0, 0)),
        ]
        + [pl.BlockSpec((1, BLOCK, HD), lambda i: (i, 0, 0))] * 3,
        out_specs=[
            pl.BlockSpec((1, BLOCK, HD), lambda i: (i, 0, 0)),
            pl.BlockSpec((16, 2, BLOCK, HD), lambda i: (0, 0, 0, 0)),
        ],
        scratch_shapes=[pltpu.VMEM((16, 2, BLOCK, HD), f32)],
        compiler_params=params(),
        cost_estimate=pl.CostEstimate(flops=30 * 10**9, bytes_accessed=8 * 10**6, transcendentals=10**6),
        name="attend_back",
    )(info, q, kv.reshape(16, 2, BLOCK, HD), o, lse, do)
    return dq, dkv.reshape(4, 4, 2, BLOCK, HD)


def to_inner(x):
    return x.reshape(-1, 2, 16, 64).swapaxes(1, 2).reshape(-1, D)


def to_outer(x):
    return x.reshape(-1, 16, 2, 64).swapaxes(1, 2).reshape(-1, D)


def norm(value):
    centre = value - jnp.mean(value, -1, keepdims=True)
    r = lax.rsqrt(jnp.mean(centre * centre, -1, keepdims=True) + epsilon)
    return centre * r, r


def norm_back(grad, n, r, gain):
    e = grad * gain
    return r * (e - jnp.mean(e, -1, keepdims=True) - n * jnp.mean(e * n, -1, keepdims=True))


def turned(x, cosine, sine, direction):
    a, b = x[..., :64], x[..., 64:]
    return jnp.concatenate([a * cosine - direction * b * sine, direction * a * sine + b * cosine], -1)


def quarters(w):
    return w.reshape(w.shape[0], 4, -1).swapaxes(0, 1)


def joined(w):
    return w.swapaxes(0, 1).reshape(w.shape[1], -1)


def gelu(v):
    return jax.nn.gelu(v, approximate=False)


def gather_weights(x):
    return lax.all_gather(x, ZY, axis=0, tiled=True)


def scatter_grads(x):
    return lax.psum_scatter(x, ZY, scatter_dimension=0, tiled=True)


def local(
    inputs,
    clip_starts,
    pad_lengths,
    w_query,
    w_key,
    w_value,
    w_out,
    w_up,
    w_down,
    gain_first,
    gain_second,
    cotangent,
):
    z, y = lax.axis_index("z"), lax.axis_index("y")
    living = LEN - pad_lengths
    side = jnp.concatenate(
        [
            gain_first[:, None],
            gain_second[:, None],
            jnp.broadcast_to(clip_starts, (32, 3)).astype(bf16),
            jnp.broadcast_to(pad_lengths[None], (32, 1)).astype(bf16),
            jnp.zeros((32, HD - 6), bf16),
        ],
        1,
    )
    first = jnp.concatenate(
        [quarters(w_query), quarters(w_key), quarters(w_value), jnp.broadcast_to(side, (4, 32, HD))], -1
    )
    second = jnp.concatenate([quarters(w_out.T), quarters(w_up)], -1)
    third = quarters(w_down.T)
    x_here = to_inner(inputs[0])
    first, second, third, x_all = start(first, second, third, x_here)
    first = first.reshape(D, -1)
    second = gather_weights(second.reshape(HD, -1))
    down = gather_weights(third.reshape(HD, -1))

    side = first[:, 768:]
    gains = side[:, :2].astype(f32).T
    gain_one, gain_two = gains[0], gains[1]
    facts = side[:128:64, 2:6].astype(jnp.int32)
    begins, ends = facts[:, :3], LEN - facts[:, 3]

    n_all, _ = norm(x_all.reshape(512, D).astype(f32))
    normed_one = (n_all * gain_one).astype(bf16)
    incoming = to_inner(cotangent[0])

    places = (4 * z + y) * BLOCK + jnp.arange(BLOCK, dtype=jnp.int32)
    opened = begins[:, None, :] <= places[None, :, None]
    position = places - jnp.max(jnp.where(opened, begins[:, None, :], 0), -1)
    frequency = 10000.0 ** (-2.0 * jnp.arange(HD // 2, dtype=f32) / HD)
    angles = position.astype(f32)[..., None] * frequency
    cosine, sine = jnp.cos(angles)[:, :, None], jnp.sin(angles)[:, :, None]

    lin = jnp.dot(normed_one, first, preferred_element_type=f32)
    lin = lin[:, :768].reshape(2, BLOCK, 3, 2, HD)
    query = turned(lin[:, :, 0], cosine, sine, 1.0)
    key = turned(lin[:, :, 1], cosine, sine, 1.0)
    qkv = jnp.stack([query, key, lin[:, :, 2]], 0).astype(bf16)
    qkv = qkv.transpose(1, 3, 0, 2, 4).reshape(4, 3, BLOCK, HD)
    q, kv, incoming_all = spread(qkv, incoming)
    incoming_all = incoming_all.reshape(512, D)
    mine = z // 2
    info = jnp.concatenate(
        [lax.dynamic_index_in_dim(begins, mine, 0, False), lax.dynamic_index_in_dim(ends, mine, 0), y[None]]
    ).astype(jnp.int32)
    o, lse = attend(info, q, kv)
    mixed = turn(o.astype(bf16))
    mixed = mixed.reshape(2, 2, BLOCK, HD).swapaxes(1, 2).reshape(512, 2 * HD)

    x = x_here.astype(f32)
    out = second[:, :256]
    middle = x + sum_rows(dot_t(mixed, out).astype(bf16))
    n_two, r_two = norm(middle)
    normed_two = gather_rows((n_two * gain_two).astype(bf16))
    hidden = jnp.dot(normed_two, second, preferred_element_type=f32)[:, 256:]
    active, pull = jax.vjp(gelu, hidden)
    active = active.astype(bf16)
    grad_active = jnp.dot(incoming_all, down, preferred_element_type=f32)
    grad_hidden = pull(grad_active)[0].astype(bf16)
    part_two = dot_t(jnp.pad(grad_hidden, ((0, 0), (256, 0))), second).astype(bf16)
    feed = jnp.concatenate(
        [dot_l(incoming_all, active).astype(bf16), dot_l(normed_two, grad_hidden).astype(bf16)], 1
    )
    part_two, feed = lax.optimization_barrier((part_two, feed))
    feed = scatter_grads(feed)
    grad_normed_two = sum_rows(part_two)
    grad_middle = incoming.astype(f32) + norm_back(grad_normed_two, n_two, r_two, gain_two)
    branch = gather_rows(grad_middle.astype(bf16))

    grad_mixed = jnp.dot(branch, out, preferred_element_type=f32).astype(bf16)
    grad_mixed = grad_mixed.reshape(2, BLOCK, 2, HD).swapaxes(1, 2).reshape(4, BLOCK, HD)
    dq, dkv = attend_back(info, q, kv, o, lse, turn(grad_mixed))
    grads, fed = collect(dq, dkv, dot_t(active, down).astype(bf16))
    output = middle + fed
    grads = grads.reshape(2, 2, 3, BLOCK, HD).transpose(2, 0, 3, 1, 4)
    grad_query = turned(grads[0].astype(f32), cosine, sine, -1.0).astype(bf16)
    grad_key = turned(grads[1].astype(f32), cosine, sine, -1.0).astype(bf16)
    grad_lin = jnp.stack([grad_query, grad_key, grads[2]], 2).reshape(512, 768)

    part_one = dot_t(jnp.pad(grad_lin, ((0, 0), (0, HD))), first)
    gain_grads = jnp.stack([jnp.sum(part_one * n_all, 0), 0.5 * jnp.sum(grad_normed_two * n_two, 0)], 1)
    last = jnp.concatenate(
        [
            dot_l(normed_one, grad_lin).astype(bf16),
            dot_l(branch, mixed).astype(bf16),
            jnp.pad(gain_grads, ((0, 0), (0, HD - 2))).astype(bf16),
        ],
        1,
    )
    last, gain_grads, grad_normed_one = end(last, part_one.astype(bf16))
    n_one, r_one = norm(x)
    grad_input = grad_middle + norm_back(grad_normed_one, n_one, r_one, gain_one)
    feed = swap_quarters(8, feed.reshape(4, 32, -1))[0].astype(f32)
    last = last.astype(f32)
    return (
        to_outer(output).astype(bf16)[None],
        to_outer(grad_input)[None],
        joined(last[:, :, :256]),
        joined(last[:, :, 256:512]),
        joined(last[:, :, 512:768]),
        joined(last[:, :, 768:1024]).T,
        joined(feed[:, :, 1024:]),
        joined(feed[:, :, :1024]).T,
        gain_grads[:, 0],
        gain_grads[:, 1],
    )


def solution(mesh):
    split = Mesh(mesh.devices.reshape(2, 4, 4, 2, 2), ("dp", "z", "y", "c", "mp"))
    seq = ("z", "y", "c")
    weights = ("dp", "z", "y", "c")
    tokens = P("dp", seq, None)
    wide, tall = P(weights, "mp"), P("mp", weights)
    return jax.shard_map(
        local,
        mesh=split,
        in_specs=(tokens, P("dp", None), P("dp"), wide, wide, wide, tall, wide, tall, P(weights), P(weights), tokens),
        out_specs=(tokens, tokens, wide, wide, wide, tall, wide, tall, P(weights), P(weights)),
        check_vma=False,
    )
```

```python
import functools

import jax
import jax.numpy as jnp
from jax import lax
from jax.experimental import pallas as pl
from jax.experimental.pallas import tpu as pltpu
from jax.sharding import Mesh
from jax.sharding import PartitionSpec as P

MESH = pl.DeviceIdType.MESH
HD = 128
FRAME = 32
LEN = 4096
D = 2048
ROWS = 128
BLOCK = 256
ZY = ("z", "y")
epsilon = 1e-05
scale = HD**-0.5
LOG_BASE = 9.210340371976184
f32 = jnp.float32
bf16 = jnp.bfloat16


def params(collective_id=None, vmem=48, **kw):
    if collective_id is not None:
        kw = dict(collective_id=collective_id, has_side_effects=True, **kw)
    return pltpu.CompilerParams(vmem_limit_bytes=vmem * 2**20, **kw)


def vmem_specs(n):
    return [pl.BlockSpec(memory_space=pltpu.VMEM)] * n


def greet(peers):
    barrier = pltpu.get_barrier_semaphore()
    for peer in peers:
        pl.semaphore_signal(barrier, inc=1, device_id=peer, device_id_type=MESH)
    pl.semaphore_wait(barrier, len(peers))


def remote(src, dst, send, recv, peer):
    return pltpu.make_async_remote_copy(
        src_ref=src, dst_ref=dst, send_sem=send, recv_sem=recv, device_id=peer, device_id_type=MESH
    )


def started(copies, src, dst, send, recv, peer):
    copy = remote(src, dst, send, recv, peer)
    copy.start()
    copies.append(copy)
    return copy


class Sems:
    def __init__(self, send, recv):
        self.send, self.recv, self.used = send, recv, 0

    def take(self):
        k = self.used
        self.used += 1
        return self.send.at[k], self.recv.at[k]


def sem_pair(n):
    return [pltpu.SemaphoreType.DMA((n,)), pltpu.SemaphoreType.DMA((n,))]


def tensor_place():
    d, c, m = lax.axis_index("dp"), lax.axis_index("c"), lax.axis_index("mp")
    return d, c, m, {"c": 1 - c}, {"dp": 1 - d, "mp": 1 - m}, {"mp": 1 - m}


def ring(axis, size=4):
    me = lax.axis_index(axis)
    up, down, far = (lax.rem(me + k, size) for k in (1, size - 1, 2))
    return me, up, down, far, {axis: up}, {axis: down}


def added(*values):
    total = values[0].astype(f32)
    for v in values[1:]:
        total = total + v.astype(f32)
    return total


def run(*protocols):
    live = list(protocols)
    while live:
        for p in list(live):
            try:
                next(p)
            except StopIteration:
                live.remove(p)


def swap_plan(srcs, dsts, sems):
    d, c = lax.axis_index("dp"), lax.axis_index("c")
    me = 2 * d + c
    copies = []
    for a, b in [(d, 1 - c), (1 - d, c), (1 - d, 1 - c)]:
        for src, dst in zip(srcs, dsts):
            started(copies, src.at[2 * a + b], dst(me), *sems.take(), {"dp": a, "c": b})
    for src, dst in zip(srcs, dsts):
        dst(me)[...] = src[me]
    yield
    for copy in copies:
        copy.wait_recv()
    yield
    for copy in copies:
        copy.wait_send()


def swap_peers():
    d, c = lax.axis_index("dp"), lax.axis_index("c")
    return [{"dp": 1 - d}, {"dp": 1 - d, "c": 1 - c}]


CHUNKS = 4
HALF = ROWS // 2


def rows_plan(x, o, sems):
    d, c, m, core, across, copy_of = tensor_place()
    me, far = 2 * d + c, 2 * (1 - d) + c
    copies, firsts, seconds = [], [], []
    step = HALF // 2
    mine = [pl.ds(m * HALF + k * step, step) for k in range(2)]
    other = [pl.ds((1 - m) * HALF + k * step, step) for k in range(2)]
    for rows in mine:
        firsts.append(started(copies, x.at[rows], o.at[me, rows], *sems.take(), across))
    near = started(copies, x, o.at[me], *sems.take(), core)
    o[me] = x[...]
    yield
    for k, rows in enumerate(other):
        firsts[k].wait_recv()
        seconds.append(started(copies, o.at[far, rows], o.at[far, rows], *sems.take(), copy_of))
    yield
    lasts = []
    for rows in other:
        lasts.append(started(copies, o.at[far, rows], o.at[far, rows], *sems.take(), core))
    for k, rows in enumerate(mine):
        seconds[k].wait_recv()
        lasts.append(started(copies, o.at[far, rows], o.at[far, rows], *sems.take(), core))
    yield
    near.wait_recv()
    for copy in lasts:
        copy.wait_recv()
    for copy in copies:
        copy.wait_send()


ROWS_SEMS = 9


def sum_plan(x, o, buffers, sems):
    from_core, s_here, s_send, from_across, t_send, from_copy = buffers
    d, c, m, core, across, copy_of = tensor_place()
    step = ROWS // CHUNKS
    rows = [pl.ds(k * step, step) for k in range(CHUNKS)]
    copies, zero, one, two = [], [], [], []
    for r in rows:
        zero.append(started(copies, x.at[:, 1 - c, r], from_core.at[:, r], *sems.take(), core))
    yield
    for k, r in enumerate(rows):
        zero[k].wait_recv()
        s_send[r] = added(x[1 - d, c, r], from_core[1 - d, r]).astype(bf16)
        one.append(started(copies, s_send.at[r], from_across.at[r], *sems.take(), across))
        s_here[r] = added(x[d, c, r], from_core[d, r])
    yield
    for k, r in enumerate(rows):
        one[k].wait_recv()
        t_send[r] = added(s_here[r], from_across[r]).astype(bf16)
        two.append(started(copies, t_send.at[r], from_copy.at[r], *sems.take(), copy_of))
    yield
    for k, r in enumerate(rows):
        two[k].wait_recv()
        o[r] = added(t_send[r], from_copy[r])
    for copy in copies:
        copy.wait_send()


SUM_SEMS = 3 * CHUNKS
SUM_BUFFERS = [
    pltpu.VMEM((2, ROWS, D), bf16),
    pltpu.VMEM((ROWS, D), f32),
    pltpu.VMEM((ROWS, D), bf16),
    pltpu.VMEM((ROWS, D), bf16),
    pltpu.VMEM((ROWS, D), bf16),
    pltpu.VMEM((ROWS, D), bf16),
]


def weights_plan(w, first, second, low, sems):
    i0, i_up, i_down, i_far, to_i_up, to_i_down = ring(first)
    j0, j_up, j_down, j_far, to_j_up, to_j_down = ring(second)

    def at(i, j, part, n):
        return w.at[(j, i) if first == "y" else (i, j)].at[pl.ds(low + part, n)]

    copies = []

    def send(ref, peer):
        return started(copies, ref, ref, *sems.take(), peer)

    def along(i):
        return i, send(at(i, j0, 0, 2), to_j_up), send(at(i, j0, 0, 2), to_j_down)

    from_down, from_up = send(at(i0, j0, 0, 2), to_i_up), send(at(i0, j0, 0, 2), to_i_down)
    second_leg = [along(i0)]
    yield
    from_down.wait_recv()
    far_low = send(at(i_down, j0, 0, 1), to_i_up)
    from_up.wait_recv()
    far_high = send(at(i_up, j0, 1, 1), to_i_down)
    second_leg += [along(i_down), along(i_up)]
    yield
    onward = []

    def relay(leg):
        i, a, b = leg
        a.wait_recv()
        onward.append(send(at(i, j_down, 0, 1), to_j_up))
        b.wait_recv()
        onward.append(send(at(i, j_up, 1, 1), to_j_down))

    relay(second_leg[0])
    yield
    far_low.wait_recv()
    far_high.wait_recv()
    second_leg.append(along(i_far))
    for leg in second_leg[1:]:
        yield
        relay(leg)
    yield
    for copy in onward:
        copy.wait_recv()
    for copy in copies:
        copy.wait_send()


WEIGHT_SEMS = 20


def start_kernel(first, second, third, x, w, s2, s3, rows, *sems):
    z, y = lax.axis_index("z"), lax.axis_index("y")
    _, _, _, _, z_up, z_down = ring("z")
    _, _, _, _, y_up, y_down = ring("y")
    greet([*tensor_place()[3:], *swap_peers(), z_up, z_down, y_up, y_down])
    one = Sems(*sems[:2])
    swap_first = swap_plan([first], [lambda me: w.at[z, y, me]], one)
    next(swap_first)
    gather_x = rows_plan(x, rows, Sems(*sems[2:4]))
    next(gather_x)
    swap_rest = swap_plan([second, third], [lambda me: s2.at[me], lambda me: s3.at[me]], one)
    next(swap_rest)
    next(swap_first)
    run(
        weights_plan(w, "y", "z", 0, Sems(*sems[4:6])),
        weights_plan(w, "z", "y", 2, Sems(*sems[6:8])),
        gather_x,
        swap_rest,
        swap_first,
    )


def start(first, second, third, x):
    return pl.pallas_call(
        start_kernel,
        out_shape=[
            jax.ShapeDtypeStruct((4, 4, *first.shape), bf16),
            jax.ShapeDtypeStruct(second.shape, bf16),
            jax.ShapeDtypeStruct(third.shape, bf16),
            jax.ShapeDtypeStruct((4, *x.shape), bf16),
        ],
        in_specs=vmem_specs(4),
        out_specs=vmem_specs(4),
        scratch_shapes=sem_pair(9) + sem_pair(ROWS_SEMS) + sem_pair(WEIGHT_SEMS) + sem_pair(WEIGHT_SEMS),
        compiler_params=params(3),
        name="start",
    )(first, second, third, x)


def spread_plan(x, q, kv, sems):
    z, z_up, z_down, z_far, to_z_up, to_z_down = ring("z")
    y, y_up, y_down, y_far, to_y_up, to_y_down = ring("y")
    far = {"z": z_far}
    copies, firsts, queries, nears, fars = [], [], [], [], []
    both = pl.ds(1, 2)
    peers = [(z_up, to_z_up, z_down), (z_down, to_z_down, z_up), (z_far, far, z_far)]
    for place, peer, _ in peers:
        firsts.append(started(copies, x.at[place, both], kv.at[z, y], *sems.take(), peer))
    kv[z, y] = x[z, both]

    def along(place):
        ref = kv.at[place, y]
        nears.append(
            (place, started(copies, ref, ref, *sems.take(), to_y_up), started(copies, ref, ref, *sems.take(), to_y_down))
        )

    along(z)
    for place, peer, _ in peers:
        queries.append(started(copies, x.at[place, 0], q.at[z], *sems.take(), peer))
    q[z] = x[z, 0]
    yield

    def relay(k):
        place, a, b = nears[k]
        a.wait_recv()
        ref = kv.at[place, y_down, 0]
        fars.append(started(copies, ref, ref, *sems.take(), to_y_up))
        b.wait_recv()
        ref = kv.at[place, y_up, 1]
        fars.append(started(copies, ref, ref, *sems.take(), to_y_down))

    for k, (_, _, source) in enumerate(peers):
        firsts[k].wait_recv()
        along(source)
        yield
        relay(k)
    yield
    relay(3)
    yield
    for copy in queries + fars:
        copy.wait_recv()
    for copy in copies:
        copy.wait_send()


def spread_kernel(x, cot, q, kv, rows, *sems):
    _, _, _, z_far, z_up, z_down = ring("z")
    _, _, _, _, y_up, y_down = ring("y")
    greet([*tensor_place()[3:], z_up, z_down, {"z": z_far}, y_up, y_down])
    run(spread_plan(x, q, kv, Sems(*sems[:2])), rows_plan(cot, rows, Sems(*sems[2:])))


def spread(x, cot):
    return pl.pallas_call(
        spread_kernel,
        out_shape=[
            jax.ShapeDtypeStruct((4, BLOCK, HD), bf16),
            jax.ShapeDtypeStruct((4, 4, 2, BLOCK, HD), bf16),
            jax.ShapeDtypeStruct((4, *cot.shape), bf16),
        ],
        in_specs=vmem_specs(2),
        out_specs=vmem_specs(3),
        scratch_shapes=sem_pair(22) + sem_pair(ROWS_SEMS),
        compiler_params=params(4),
        name="spread",
    )(x, cot)


def ring_sum(at, axis, buffers, sems, put):
    one, two, passed = buffers
    me, up, down, far, to_up, to_down = ring(axis)
    copies = []
    a = started(copies, at(far, 0), one.at[0], *sems.take(), to_up)
    b = started(copies, at(far, 1), one.at[1], *sems.take(), to_down)
    plain = [
        started(copies, at(up, 1), two.at[0, 1], *sems.take(), to_up),
        started(copies, at(down, 0), two.at[1, 0], *sems.take(), to_down),
    ]
    yield
    a.wait_recv()
    passed[0] = added(at(up, 0)[...], one[0]).astype(bf16)
    plain.append(started(copies, passed.at[0], two.at[0, 0], *sems.take(), to_up))
    b.wait_recv()
    passed[1] = added(at(down, 1)[...], one[1]).astype(bf16)
    plain.append(started(copies, passed.at[1], two.at[1, 1], *sems.take(), to_down))
    yield
    for copy in plain:
        copy.wait_recv()
    for part in range(2):
        put(part, added(at(me, part)[...], two[0, part], two[1, part]))
    yield
    for copy in copies:
        copy.wait_send()


RING_SEMS = 6


def ring_buffers(n, part):
    return [pltpu.VMEM((n, 2, *part), bf16), pltpu.VMEM((n, 2, 2, *part), bf16), pltpu.VMEM((n, 2, *part), bf16)]


def collect_plan(dq, dkv, o, total, buffers, sems):
    z, z_up, z_down, z_far, to_z_up, to_z_down = ring("z")
    y = lax.axis_index("y")
    peers = [(z_up, to_z_up), (z_down, to_z_down), (z_far, {"z": z_far}), (z, None)]
    copies, rings = [], []
    for k, (place, peer) in enumerate(peers):

        def at(i, part, place=place):
            return dkv.at[place, i, part]

        def put(part, value, k=k):
            if k < 3:
                total[k, part] = value.astype(bf16)
            else:
                o[z, 1 + part] = value.astype(bf16)

        rings.append(ring_sum(at, "y", [b.at[k] for b in buffers], sems, put))
    for r in rings:
        next(r)
    for place, peer in peers[:3]:
        started(copies, dq.at[place], o.at[z, 0], *sems.take(), peer)
    o[z, 0] = dq[z]
    yield
    for r in rings:
        next(r)
        yield
    for k, r in enumerate(rings):
        next(r)
        if k < 3:
            started(copies, total.at[k], o.at[z, pl.ds(1, 2)], *sems.take(), peers[k][1])
        yield
    for copy in copies:
        copy.wait()
    run(*rings)


def collect_kernel(dq, dkv, part, o, summed, total, *scratch):
    _, _, _, z_far, z_up, z_down = ring("z")
    _, _, _, _, y_up, y_down = ring("y")
    greet([*tensor_place()[3:], z_up, z_down, {"z": z_far}, y_up, y_down])
    run(
        collect_plan(dq, dkv, o, total, scratch[:3], Sems(*scratch[3:5])),
        sum_plan(part, summed, scratch[5:11], Sems(*scratch[11:])),
    )


def collect(dq, dkv, part):
    return pl.pallas_call(
        collect_kernel,
        out_shape=[jax.ShapeDtypeStruct((4, 3, BLOCK, HD), bf16), jax.ShapeDtypeStruct((ROWS, D), f32)],
        in_specs=vmem_specs(3),
        out_specs=vmem_specs(2),
        scratch_shapes=[pltpu.VMEM((3, 2, BLOCK, HD), bf16)]
        + ring_buffers(4, (BLOCK, HD))
        + sem_pair(4 * RING_SEMS + 6)
        + SUM_BUFFERS
        + sem_pair(SUM_SEMS),
        compiler_params=params(6),
        name="collect",
    )(dq, dkv, part.reshape(2, 2, ROWS, D))


def grads_plan(g, shard, first, second, low, legs, buffers, sems):
    rings = []
    for j in range(4):

        def at(i, part, j=j):
            return g.at[(j, i) if first == "y" else (i, j)].at[low + part]

        def put(part, value, j=j):
            legs[j, part] = value.astype(bf16)

        rings.append(ring_sum(at, first, [b.at[j] for b in buffers], sems, put))
    for r in rings:
        next(r)
    yield
    for r in rings:
        next(r)
    yield
    for r in rings:
        next(r)

    def put_last(part, value):
        shard[low + part] = value.astype(bf16)

    rings.append(ring_sum(lambda i, part: legs.at[i, part], second, [b.at[4] for b in buffers], sems, put_last))
    for _ in range(3):
        next(rings[-1])
        yield
    run(*rings)


def end_kernel(wide, g, part, feed_part, o, gain, summed, feed_all, *scratch):
    d, c, m, core, across, copy_of = tensor_place()
    _, _, _, _, z_up, z_down = ring("z")
    _, _, _, _, y_up, y_down = ring("y")
    greet([core, across, copy_of, *swap_peers(), z_up, z_down, y_up, y_down])
    shard, mine, theirs, legs_a, legs_b = scratch[:5]
    scratch = scratch[5:]
    last = Sems(*scratch[18:])
    run(
        swap_plan([feed_part], [lambda me: feed_all.at[me]], last),
        sum_plan(part, summed, scratch[6:12], Sems(*scratch[12:14])),
        grads_plan(g, shard, "z", "y", 0, legs_a, scratch[:3], Sems(*scratch[14:16])),
        grads_plan(g, shard, "y", "z", 2, legs_b, scratch[3:6], Sems(*scratch[16:18])),
    )
    run(swap_plan([shard], [lambda me: o.at[me]], last))
    lanes = pl.ds(wide, HD)
    mine[...] = added(o[0, :, lanes], o[1, :, lanes], o[2, :, lanes], o[3, :, lanes])
    copy = remote(mine, theirs, *last.take(), copy_of)
    copy.start()
    copy.wait()
    gain[...] = mine[...] + theirs[...]


def end(g, part, feed_part):
    block = (32, g.shape[1])
    return pl.pallas_call(
        functools.partial(end_kernel, g.shape[1] - HD),
        out_shape=[
            jax.ShapeDtypeStruct((4, *block), bf16),
            jax.ShapeDtypeStruct((32, HD), f32),
            jax.ShapeDtypeStruct((ROWS, D), f32),
            jax.ShapeDtypeStruct(feed_part.shape, bf16),
        ],
        in_specs=vmem_specs(3),
        out_specs=vmem_specs(4),
        scratch_shapes=[
            pltpu.VMEM((4, *block), bf16),
            pltpu.VMEM((32, HD), f32),
            pltpu.VMEM((32, HD), f32),
            pltpu.VMEM((4, 2, *block), bf16),
            pltpu.VMEM((4, 2, *block), bf16),
        ]
        + ring_buffers(5, block)
        + ring_buffers(5, block)
        + SUM_BUFFERS
        + sem_pair(SUM_SEMS)
        + sem_pair(5 * RING_SEMS)
        + sem_pair(5 * RING_SEMS)
        + sem_pair(7),
        compiler_params=params(7),
        name="end",
    )(g.reshape(4, 4, 4, *block), part.reshape(2, 2, ROWS, D), feed_part)


def reach(facts, block, rows):
    t = block * rows + lax.broadcasted_iota(jnp.int32, (rows, 1), 0)
    one, two, three, padding = (facts[:, k : k + 1].astype(jnp.int32) for k in range(2, 6))
    begin = jnp.where(t >= three, three, jnp.where(t >= two, two, one))
    living = t < LEN - padding
    end = jnp.minimum((t // FRAME + 1) * FRAME, LEN - padding)
    return t, begin, jnp.where(living, begin, t), jnp.where(living, end, t + 1)


def dot_t(a, b):
    return lax.dot_general(a, b, (((1,), (1,)), ((), ())), preferred_element_type=f32)


def dot_l(a, b):
    return lax.dot_general(a, b, (((0,), (0,)), ((), ())), preferred_element_type=f32)


def visible_scores(q, k, j, low, high):
    s = dot_t(q, k) * scale
    at = j * BLOCK + lax.broadcasted_iota(jnp.int32, (1, BLOCK), 1)
    return jnp.where((at >= low) & (at < high), s, -1e30)


def attend_kernel(facts, q_ref, kv_ref, o_ref, lse_ref, mixed_ref):
    block = 4 * pl.program_id(0) + lax.axis_index("y")
    _, _, low, high = reach(facts[pl.ds(lax.axis_index("z") // 2, 1)], block, BLOCK)
    q = q_ref[0]

    def step(j, state):
        top, total, acc = state
        s = visible_scores(q, kv_ref[j, 0], j, low, high)
        now = jnp.maximum(top, jnp.max(s, -1, keepdims=True))
        p = jnp.exp(s - now)
        shrink = jnp.exp(top - now)
        total = total * shrink + jnp.sum(p, -1, keepdims=True)
        acc = acc * shrink + jnp.dot(p.astype(bf16), kv_ref[j, 1], preferred_element_type=f32)
        return now, total, acc

    top, total, acc = lax.fori_loop(
        0,
        block + 1,
        step,
        (jnp.full((BLOCK, 1), -1e30, f32), jnp.zeros((BLOCK, 1), f32), jnp.zeros((BLOCK, HD), f32)),
    )
    out = acc / total
    o_ref[0] = out
    mixed_ref[0] = out.astype(bf16)
    lse_ref[0] = jnp.broadcast_to(top + jnp.log(total), (BLOCK, HD))


def attend(facts, q, kv):
    return pl.pallas_call(
        attend_kernel,
        grid=(4,),
        out_shape=[jax.ShapeDtypeStruct((4, BLOCK, HD), f32)] * 2 + [jax.ShapeDtypeStruct((4, BLOCK, HD), bf16)],
        in_specs=[
            pl.BlockSpec((8, HD), lambda i: (0, 0)),
            pl.BlockSpec((1, BLOCK, HD), lambda i: (i, 0, 0)),
            pl.BlockSpec((16, 2, BLOCK, HD), lambda i: (0, 0, 0, 0)),
        ],
        out_specs=[pl.BlockSpec((1, BLOCK, HD), lambda i: (i, 0, 0))] * 3,
        compiler_params=params(),
        cost_estimate=pl.CostEstimate(flops=20 * 10**9, bytes_accessed=4 * 10**6, transcendentals=10**6),
        name="attend",
    )(facts, q, kv.reshape(16, 2, BLOCK, HD))


def attend_back_kernel(facts, q_ref, kv_ref, o_ref, lse_ref, do_ref, dq_ref, dkv_ref, acc):
    i = pl.program_id(0)
    block = 4 * i + lax.axis_index("y")
    _, _, low, high = reach(facts[pl.ds(lax.axis_index("z") // 2, 1)], block, BLOCK)
    q, do = q_ref[0], do_ref[0]
    lse = lse_ref[0][:, :1]
    inner = jnp.sum(o_ref[0] * do.astype(f32), -1, keepdims=True)

    @pl.when(i == 0)
    def _():
        acc[...] = jnp.zeros_like(acc)

    def step(j, dq):
        k, v = kv_ref[j, 0], kv_ref[j, 1]
        p = jnp.exp(visible_scores(q, k, j, low, high) - lse)
        acc[j, 1] += dot_l(p.astype(bf16), do)
        ds = (p * (dot_t(do, v) - inner)).astype(bf16)
        acc[j, 0] += dot_l(ds, q)
        return dq + jnp.dot(ds, k, preferred_element_type=f32)

    dq = lax.fori_loop(0, block + 1, step, jnp.zeros((BLOCK, HD), f32))
    dq_ref[0] = (dq * scale).astype(bf16)

    @pl.when(i == 3)
    def _():
        def cast(j, _):
            dkv_ref[j, 0] = (acc[j, 0] * scale).astype(bf16)
            dkv_ref[j, 1] = acc[j, 1].astype(bf16)
            return 0

        lax.fori_loop(0, 16, cast, 0)


def attend_back(facts, q, kv, o, lse, do):
    dq, dkv = pl.pallas_call(
        attend_back_kernel,
        grid=(4,),
        out_shape=[
            jax.ShapeDtypeStruct((4, BLOCK, HD), bf16),
            jax.ShapeDtypeStruct((16, 2, BLOCK, HD), bf16),
        ],
        in_specs=[
            pl.BlockSpec((8, HD), lambda i: (0, 0)),
            pl.BlockSpec((1, BLOCK, HD), lambda i: (i, 0, 0)),
            pl.BlockSpec((16, 2, BLOCK, HD), lambda i: (0, 0, 0, 0)),
        ]
        + [pl.BlockSpec((1, BLOCK, HD), lambda i: (i, 0, 0))] * 3,
        out_specs=[
            pl.BlockSpec((1, BLOCK, HD), lambda i: (i, 0, 0)),
            pl.BlockSpec((16, 2, BLOCK, HD), lambda i: (0, 0, 0, 0)),
        ],
        scratch_shapes=[pltpu.VMEM((16, 2, BLOCK, HD), f32)],
        compiler_params=params(),
        cost_estimate=pl.CostEstimate(flops=30 * 10**9, bytes_accessed=8 * 10**6, transcendentals=10**6),
        name="attend_back",
    )(facts, q, kv.reshape(16, 2, BLOCK, HD), o, lse, do)
    return dq, dkv.reshape(4, 4, 2, BLOCK, HD)


def norm(value):
    centre = value - jnp.mean(value, -1, keepdims=True)
    r = lax.rsqrt(jnp.mean(centre * centre, -1, keepdims=True) + epsilon)
    return centre * r, r


def norm_back(grad, n, r, gain):
    e = grad * gain
    return r * (e - jnp.mean(e, -1, keepdims=True) - n * jnp.mean(e * n, -1, keepdims=True))


def one_hot(rows, places):
    at = lax.broadcasted_iota(jnp.int32, (rows, HD), 0)
    lane = lax.broadcasted_iota(jnp.int32, (rows, HD), 1)
    hot = at < 0
    for k, place in enumerate(places):
        hot = hot | ((at == k) & (lane == place))
    return jnp.where(hot, 1.0, 0.0).astype(bf16)


def tables(facts, seq, c):
    block = (4 * lax.axis_index("z") + lax.axis_index("y")) * 2 + c
    t, begin, _, _ = reach(facts[seq : seq + 1], block, ROWS)
    lane = lax.broadcasted_iota(jnp.int32, (1, HD), 1)
    i = jnp.where(lane < HD // 2, lane, lane - HD // 2).astype(f32)
    angles = (t - begin).astype(f32) * jnp.exp(i * (-2.0 * LOG_BASE / HD))
    return jnp.cos(angles), jnp.where(lane < HD // 2, -1.0, 1.0) * jnp.sin(angles)


def project_kernel(x, w, n1, qkv, gains, facts):
    side = w[:, 768:896]
    gains[...] = dot_t(one_hot(8, (0, 1)), side)
    facts[...] = jnp.zeros_like(facts)
    facts[0:1] = side[0:1].astype(f32)
    facts[1:2] = side[64:65].astype(f32)
    for seq in range(2):
        for c in range(2):
            rows = pl.ds((2 * seq + c) * ROWS, ROWS)
            n, _ = norm(x[rows].astype(f32))
            n1[rows] = (n * gains[0:1]).astype(bf16)
            lin = jnp.dot(n1[rows], w[:, :768], preferred_element_type=f32)
            cosine, sine = tables(facts, seq, c)
            for kind in range(3):
                for h in range(2):
                    v = lin[:, (2 * kind + h) * HD : (2 * kind + h + 1) * HD]
                    if kind < 2:
                        v = v * cosine + pltpu.roll(v, HD // 2, 1) * sine
                    qkv[2 * seq + h, kind, c * ROWS : (c + 1) * ROWS] = v.astype(bf16)


def project(x, w):
    return pl.pallas_call(
        project_kernel,
        out_shape=[
            jax.ShapeDtypeStruct((512, D), bf16),
            jax.ShapeDtypeStruct((4, 3, BLOCK, HD), bf16),
            jax.ShapeDtypeStruct((8, D), f32),
            jax.ShapeDtypeStruct((8, HD), f32),
        ],
        in_specs=vmem_specs(2),
        out_specs=vmem_specs(4),
        compiler_params=params(),
        cost_estimate=pl.CostEstimate(flops=10 * 10**9, bytes_accessed=8 * 10**6, transcendentals=10**5),
        name="project",
    )(x, w)


def unproject_kernel(grads, w, n1, branch, mixed, gains, facts, gain_two, part, last, lin):
    for seq in range(2):
        for c in range(2):
            rows = pl.ds((2 * seq + c) * ROWS, ROWS)
            cosine, sine = tables(facts, seq, c)
            for kind in range(3):
                for h in range(2):
                    v = grads[2 * seq + h, kind, c * ROWS : (c + 1) * ROWS]
                    if kind < 2:
                        v = v.astype(f32)
                        v = (v * cosine - pltpu.roll(v, HD // 2, 1) * sine).astype(bf16)
                    lin[rows, (2 * kind + h) * HD : (2 * kind + h + 1) * HD] = v
    step = 512

    def body(k, _):
        some = pl.ds(pl.multiple_of(k * step, step), step)
        p = dot_t(lin[...], w[some, 0:768])
        part[:, some] = p.astype(bf16)
        n = n1[:, some]
        gain_one = jnp.sum(p * n.astype(f32), 0, keepdims=True) / gains[0:1, some]
        both = jnp.concatenate([gain_one, gain_two[0:1, some], jnp.zeros((6, step), f32)], 0)
        last[some, 0:768] = dot_l(n, lin[...]).astype(bf16)
        last[some, 768:1024] = dot_l(branch[:, some], mixed[...]).astype(bf16)
        last[some, 1024:1152] = dot_l(both.astype(bf16), one_hot(8, (0, 1))).astype(bf16)
        return 0

    lax.fori_loop(0, D // step, body, 0)


def unproject(grads, w, n1, branch, mixed, gains, facts, gain_two):
    return pl.pallas_call(
        unproject_kernel,
        out_shape=[jax.ShapeDtypeStruct((512, D), bf16), jax.ShapeDtypeStruct((D, 1152), bf16)],
        in_specs=vmem_specs(8),
        out_specs=vmem_specs(2),
        scratch_shapes=[pltpu.VMEM((512, 768), bf16)],
        compiler_params=params(),
        cost_estimate=pl.CostEstimate(flops=10 * 10**9, bytes_accessed=8 * 10**6, transcendentals=10**5),
        name="unproject",
    )(grads, w, n1, branch, mixed, gains, facts, gain_two)


def feed_kernel(n2, cot, up, down, part, fed, grads, n2_t, cot_t, part_sum, fed_sum):
    j = pl.program_id(0)

    @pl.when(j == 0)
    def _():
        def body(k, _):
            some = pl.ds(pl.multiple_of(k * 512, 512), 512)
            n2_t[some] = n2[:, some].T
            cot_t[some] = cot[:, some].T
            return 0

        lax.fori_loop(0, D // 512, body, 0)

    hidden = jnp.dot(n2[...], up[...], preferred_element_type=f32)
    half = 0.5 * (1.0 + lax.erf(hidden * 0.5**0.5))
    slope = half + hidden * jnp.exp(-0.5 * hidden * hidden) * (0.5 / jnp.pi) ** 0.5
    active = (hidden * half).astype(bf16)
    grad_active = jnp.dot(cot[...], down[...], preferred_element_type=f32)
    grad_hidden = (grad_active * slope).astype(bf16)
    grads[:, :256] = jnp.dot(cot_t[...], active, preferred_element_type=f32).astype(bf16)
    grads[:, 256:] = jnp.dot(n2_t[...], grad_hidden, preferred_element_type=f32).astype(bf16)

    @pl.when(j == 0)
    def _():
        part_sum[...] = dot_t(grad_hidden, up[...])
        fed_sum[...] = dot_t(active, down[...])

    @pl.when(j > 0)
    def _():
        part_sum[...] += dot_t(grad_hidden, up[...])
        fed_sum[...] += dot_t(active, down[...])

    @pl.when(j == 3)
    def _():
        part[...] = part_sum[...].astype(bf16)
        fed[...] = fed_sum[...].astype(bf16)


def feed(n2, cot, second, down):
    whole = pl.BlockSpec((512, D), lambda j: (0, 0))
    return pl.pallas_call(
        feed_kernel,
        grid=(4,),
        out_shape=[jax.ShapeDtypeStruct((512, D), bf16)] * 2 + [jax.ShapeDtypeStruct((D, 2048), bf16)],
        in_specs=[
            whole,
            whole,
            pl.BlockSpec((D, 256), lambda j: (0, j + 1)),
            pl.BlockSpec((D, 256), lambda j: (0, j)),
        ],
        out_specs=[whole, whole, pl.BlockSpec((D, 512), lambda j: (0, j))],
        scratch_shapes=[pltpu.VMEM((D, 512), bf16)] * 2 + [pltpu.VMEM((512, D), f32)] * 2,
        compiler_params=params(vmem=56),
        cost_estimate=pl.CostEstimate(flops=20 * 10**9, bytes_accessed=24 * 10**6, transcendentals=10**6),
        name="feed",
    )(n2, cot, second, down)


def sum_norm_plan(x, own, all_rows, make, buffers, sems):
    from_core, s_here, s_send, from_across, t_send, from_copy = buffers
    d, c, m, core, across, copy_of = tensor_place()
    me, far = 2 * d + c, 2 * (1 - d) + c
    step = ROWS // CHUNKS
    rows = [pl.ds(k * step, step) for k in range(CHUNKS)]
    copies, zero, one, two = [], [], [], []
    for r in rows:
        zero.append(started(copies, x.at[:, 1 - c, r], from_core.at[:, r], *sems.take(), core))
    yield
    for k, r in enumerate(rows):
        zero[k].wait_recv()
        s_send[r] = added(x[1 - d, c, r], from_core[1 - d, r]).astype(bf16)
        one.append(started(copies, s_send.at[r], from_across.at[r], *sems.take(), across))
        s_here[r] = added(x[d, c, r], from_core[d, r])
    for k, r in enumerate(rows):
        one[k].wait_recv()
        t_send[r] = added(s_here[r], from_across[r]).astype(bf16)
        two.append(started(copies, t_send.at[r], from_copy.at[r], *sems.take(), copy_of))
    yield
    nears, firsts, seconds, lasts = [], [], [], []
    for k, r in enumerate(rows):
        two[k].wait_recv()
        all_rows[me, r] = make(r, added(t_send[r], from_copy[r])).astype(bf16)
        nears.append(started(copies, all_rows.at[me, r], all_rows.at[me, r], *sems.take(), core))
        half = pl.ds(pl.multiple_of(k * step + m * (step // 2), step // 2), step // 2)
        firsts.append(started(copies, all_rows.at[me, half], all_rows.at[me, half], *sems.take(), across))
    yield

    def onward(half, peer):
        return started(copies, all_rows.at[far, half], all_rows.at[far, half], *sems.take(), peer)

    for k in range(CHUNKS):
        firsts[k].wait_recv()
        half = pl.ds(pl.multiple_of(k * step + (1 - m) * (step // 2), step // 2), step // 2)
        seconds.append(onward(half, copy_of))
        lasts.append(onward(half, core))
    yield
    for k in range(CHUNKS):
        seconds[k].wait_recv()
        half = pl.ds(pl.multiple_of(k * step + m * (step // 2), step // 2), step // 2)
        lasts.append(onward(half, core))
    yield
    for copy in nears + lasts:
        copy.wait_recv()
    yield
    for copy in copies:
        copy.wait_send()


SUM_NORM_SEMS = 8 * CHUNKS


def z_peers():
    z, z_up, z_down, z_far, to_z_up, to_z_down = ring("z")
    return z, [(z_up, to_z_up), (z_down, to_z_down), (z_far, {"z": z_far})]


def mix_kernel(o, w, x, gains, mixed, middle, n2, turned, part, *scratch):
    z, peers = z_peers()
    c = lax.axis_index("c")
    greet([*tensor_place()[3:], *[peer for _, peer in peers]])
    turns, copies = Sems(*scratch[8:]), []
    for place, peer in peers:
        started(copies, o.at[place], turned.at[z], *turns.take(), peer)
    turned[z] = o[z]
    for copy in copies:
        copy.wait()
    for seq in range(2):
        for h in range(2):
            mixed[seq * BLOCK : (seq + 1) * BLOCK, h * HD : (h + 1) * HD] = turned[2 * seq + h]

    def partial(to):
        for seq in range(2):
            rows = pl.ds(pl.multiple_of(seq * BLOCK + to * ROWS, ROWS), ROWS)
            part[seq, to] = dot_t(mixed[rows], w[...]).astype(bf16)

    def make(r, total):
        value = x[r].astype(f32) + total
        middle[r] = value
        return norm(value)[0] * gains[1:2]

    partial(1 - c)
    plan = sum_norm_plan(part, middle, n2, make, scratch[:6], Sems(*scratch[6:8]))
    next(plan)
    partial(c)
    run(plan)


def mix(o, second, x, gains):
    whole = lambda *shape: pl.BlockSpec(shape, lambda i: (0,) * len(shape))
    return pl.pallas_call(
        mix_kernel,
        grid=(1,),
        out_shape=[
            jax.ShapeDtypeStruct((512, 256), bf16),
            jax.ShapeDtypeStruct((ROWS, D), f32),
            jax.ShapeDtypeStruct((4, ROWS, D), bf16),
        ],
        in_specs=[whole(4, BLOCK, HD), whole(D, 256), whole(ROWS, D), whole(8, D)],
        out_specs=[whole(512, 256), whole(ROWS, D), whole(4, ROWS, D)],
        scratch_shapes=[pltpu.VMEM((4, BLOCK, HD), bf16), pltpu.VMEM((2, 2, ROWS, D), bf16)]
        + SUM_BUFFERS
        + sem_pair(SUM_NORM_SEMS)
        + sem_pair(3),
        compiler_params=params(1),
        name="mix",
    )(o, second, x, gains)


def unmix_kernel(part, middle, cot, gains, w, grad_middle, branch, turned, gain_two, grad_mixed, *scratch):
    z, peers = z_peers()
    greet([*tensor_place()[3:], *[peer for _, peer in peers]])
    gain_two[...] = jnp.zeros_like(gain_two)

    def make(r, total):
        n, rate = norm(middle[r])
        gain_two[0:1] += 0.5 * jnp.sum(total * n, 0, keepdims=True)
        value = cot[r].astype(f32) + norm_back(total, n, rate, gains[1:2])
        grad_middle[r] = value
        return value

    run(sum_norm_plan(part, grad_middle, branch, make, scratch[:6], Sems(*scratch[6:8])))
    for k in range(4):
        value = jnp.dot(branch[k], w[...], preferred_element_type=f32).astype(bf16)
        for h in range(2):
            grad_mixed[2 * (k // 2) + h, (k % 2) * ROWS : (k % 2 + 1) * ROWS] = value[:, h * HD : (h + 1) * HD]
    turns, copies = Sems(*scratch[8:]), []
    for place, peer in peers:
        started(copies, grad_mixed.at[place], turned.at[z], *turns.take(), peer)
    turned[z] = grad_mixed[z]
    for copy in copies:
        copy.wait()


def unmix(part, middle, cot, gains, second):
    whole = lambda *shape: pl.BlockSpec(shape, lambda i: (0,) * len(shape))
    return pl.pallas_call(
        unmix_kernel,
        grid=(1,),
        out_shape=[
            jax.ShapeDtypeStruct((ROWS, D), f32),
            jax.ShapeDtypeStruct((4, ROWS, D), bf16),
            jax.ShapeDtypeStruct((4, BLOCK, HD), bf16),
            jax.ShapeDtypeStruct((8, D), f32),
        ],
        in_specs=[whole(2, 2, ROWS, D), whole(ROWS, D), whole(ROWS, D), whole(8, D), whole(D, 256)],
        out_specs=[whole(ROWS, D), whole(4, ROWS, D), whole(4, BLOCK, HD), whole(8, D)],
        scratch_shapes=[pltpu.VMEM((4, BLOCK, HD), bf16)] + SUM_BUFFERS + sem_pair(SUM_NORM_SEMS) + sem_pair(3),
        compiler_params=params(2),
        name="unmix",
    )(part.reshape(2, 2, ROWS, D), middle, cot, gains, second)


def to_inner(x):
    return x.reshape(-1, 2, 16, 64).swapaxes(1, 2).reshape(-1, D)


def to_outer(x):
    return x.reshape(-1, 16, 2, 64).swapaxes(1, 2).reshape(-1, D)


def quarters(w):
    return w.reshape(w.shape[0], 4, -1).swapaxes(0, 1)


def joined(w):
    return w.swapaxes(0, 1).reshape(w.shape[1], -1)


def gather_weights(x):
    return lax.all_gather(x, ZY, axis=0, tiled=True)


def scatter_grads(x):
    return lax.psum_scatter(x, ZY, scatter_dimension=0, tiled=True)


def local(
    inputs,
    clip_starts,
    pad_lengths,
    w_query,
    w_key,
    w_value,
    w_out,
    w_up,
    w_down,
    gain_first,
    gain_second,
    cotangent,
):
    side = jnp.concatenate(
        [
            gain_first[:, None],
            gain_second[:, None],
            jnp.broadcast_to(clip_starts, (32, 3)).astype(bf16),
            jnp.broadcast_to(pad_lengths[None], (32, 1)).astype(bf16),
            jnp.zeros((32, HD - 6), bf16),
        ],
        1,
    )
    first = jnp.concatenate(
        [quarters(w_query), quarters(w_key), quarters(w_value), jnp.broadcast_to(side, (4, 32, HD))], -1
    )
    second = jnp.concatenate([quarters(w_out.T), quarters(w_up)], -1)
    third = quarters(w_down.T)
    x_here = to_inner(inputs[0])
    first, second, third, x_all = start(first, second, third, x_here)
    first = first.reshape(D, -1)
    second = gather_weights(second.reshape(HD, -1))
    down = gather_weights(third.reshape(HD, -1))

    incoming = to_inner(cotangent[0])
    normed_one, qkv, gains, facts = project(x_all.reshape(512, D), first)
    q, kv, incoming_all = spread(qkv, incoming)
    incoming_all = incoming_all.reshape(512, D)
    o, lse, attended = attend(facts, q, kv)
    mixed, middle, normed_two = mix(attended, second, x_here, gains)
    part_two, part_out, grad_feed = feed(normed_two.reshape(512, D), incoming_all, second, down)
    grad_feed = scatter_grads(grad_feed)
    grad_middle, branch, grad_mixed, gain_two = unmix(part_two, middle, incoming, gains, second)
    dq, dkv = attend_back(facts, q, kv, o, lse, grad_mixed)
    grads, fed = collect(dq, dkv, part_out)
    output = middle + fed
    part_one, last = unproject(grads, first, normed_one, branch.reshape(512, D), mixed, gains, facts, gain_two)
    last, gain_grads, grad_normed_one, grad_feed = end(last, part_one, grad_feed.reshape(4, 32, -1))
    n_one, r_one = norm(x_here.astype(f32))
    grad_input = grad_middle + norm_back(grad_normed_one, n_one, r_one, gains[0])
    grad_feed = grad_feed.reshape(4, 32, 4, 2, 256).transpose(3, 1, 0, 2, 4).reshape(2, 32, -1).astype(f32)
    last = last.astype(f32)
    return (
        to_outer(output).astype(bf16)[None],
        to_outer(grad_input)[None],
        joined(last[:, :, :256]),
        joined(last[:, :, 256:512]),
        joined(last[:, :, 512:768]),
        joined(last[:, :, 768:1024]).T,
        grad_feed[1],
        grad_feed[0].T,
        gain_grads[:, 0],
        gain_grads[:, 1],
    )


def solution(mesh):
    split = Mesh(mesh.devices.reshape(2, 4, 4, 2, 2), ("dp", "z", "y", "c", "mp"))
    seq = ("z", "y", "c")
    weights = ("dp", "z", "y", "c")
    tokens = P("dp", seq, None)
    wide, tall = P(weights, "mp"), P("mp", weights)
    return jax.shard_map(
        local,
        mesh=split,
        in_specs=(tokens, P("dp", None), P("dp"), wide, wide, wide, tall, wide, tall, P(weights), P(weights), tokens),
        out_specs=(tokens, tokens, wide, wide, wide, tall, wide, tall, P(weights), P(weights)),
        check_vma=False,
    )
```

```python
import functools

import jax
import jax.numpy as jnp
from jax import lax
from jax.experimental import pallas as pl
from jax.experimental.pallas import tpu as pltpu
from jax.sharding import Mesh
from jax.sharding import PartitionSpec as P

MESH = pl.DeviceIdType.MESH
HD = 128
FRAME = 32
LEN = 4096
D = 2048
ROWS = 128
BLOCK = 256
ZY = ("z", "y")
epsilon = 1e-05
scale = HD**-0.5
LOG_BASE = 9.210340371976184
f32 = jnp.float32
bf16 = jnp.bfloat16


def params(collective_id=None, vmem=48, **kw):
    if collective_id is not None:
        kw = dict(collective_id=collective_id, has_side_effects=True, **kw)
    return pltpu.CompilerParams(vmem_limit_bytes=vmem * 2**20, **kw)


def vmem_specs(n):
    return [pl.BlockSpec(memory_space=pltpu.VMEM)] * n


def greet(peers):
    barrier = pltpu.get_barrier_semaphore()
    for peer in peers:
        pl.semaphore_signal(barrier, inc=1, device_id=peer, device_id_type=MESH)
    pl.semaphore_wait(barrier, len(peers))


def remote(src, dst, send, recv, peer):
    return pltpu.make_async_remote_copy(
        src_ref=src, dst_ref=dst, send_sem=send, recv_sem=recv, device_id=peer, device_id_type=MESH
    )


def started(copies, src, dst, send, recv, peer):
    copy = remote(src, dst, send, recv, peer)
    copy.start()
    copies.append(copy)
    return copy


class Sems:
    def __init__(self, send, recv):
        self.send, self.recv, self.used = send, recv, 0

    def take(self):
        k = self.used
        self.used += 1
        return self.send.at[k], self.recv.at[k]


def sem_pair(n):
    return [pltpu.SemaphoreType.DMA((n,)), pltpu.SemaphoreType.DMA((n,))]


def tensor_place():
    d, c, m = lax.axis_index("dp"), lax.axis_index("c"), lax.axis_index("mp")
    return d, c, m, {"c": 1 - c}, {"dp": 1 - d, "mp": 1 - m}, {"mp": 1 - m}


def ring(axis, size=4):
    me = lax.axis_index(axis)
    up, down, far = (lax.rem(me + k, size) for k in (1, size - 1, 2))
    return me, up, down, far, {axis: up}, {axis: down}


def added(*values):
    total = values[0].astype(f32)
    for v in values[1:]:
        total = total + v.astype(f32)
    return total


def run(*protocols):
    live = list(protocols)
    while live:
        for p in list(live):
            try:
                next(p)
            except StopIteration:
                live.remove(p)


def swap_plan(pairs, sems):
    d, c = lax.axis_index("dp"), lax.axis_index("c")
    me = 2 * d + c
    copies = []
    for a, b in [(d, 1 - c), (1 - d, c), (1 - d, 1 - c)]:
        for src, dst in pairs:
            started(copies, src(2 * a + b), dst(me), *sems.take(), {"dp": a, "c": b})
    for src, dst in pairs:
        dst(me)[...] = src(me)[...]
    yield
    for copy in copies:
        copy.wait_recv()
    yield
    for copy in copies:
        copy.wait_send()


def quarter(ref):
    wide = ref.shape[1] // 4
    return lambda q: ref.at[:, pl.ds(pl.multiple_of(q * wide, wide), wide)]


def swap_peers():
    d, c = lax.axis_index("dp"), lax.axis_index("c")
    return [{"dp": 1 - d}, {"dp": 1 - d, "c": 1 - c}]


CHUNKS = 4
HALF = ROWS // 2


def rows_plan(x, o, sems):
    d, c, m, core, across, copy_of = tensor_place()
    me, far = 2 * d + c, 2 * (1 - d) + c
    copies, firsts, seconds = [], [], []
    step = HALF // 2
    mine = [pl.ds(m * HALF + k * step, step) for k in range(2)]
    other = [pl.ds((1 - m) * HALF + k * step, step) for k in range(2)]
    for rows in mine:
        firsts.append(started(copies, x.at[rows], o.at[me, rows], *sems.take(), across))
    near = started(copies, x, o.at[me], *sems.take(), core)
    o[me] = x[...]
    yield
    for k, rows in enumerate(other):
        firsts[k].wait_recv()
        seconds.append(started(copies, o.at[far, rows], o.at[far, rows], *sems.take(), copy_of))
    yield
    lasts = []
    for rows in other:
        lasts.append(started(copies, o.at[far, rows], o.at[far, rows], *sems.take(), core))
    for k, rows in enumerate(mine):
        seconds[k].wait_recv()
        lasts.append(started(copies, o.at[far, rows], o.at[far, rows], *sems.take(), core))
    yield
    near.wait_recv()
    for copy in lasts:
        copy.wait_recv()
    for copy in copies:
        copy.wait_send()


ROWS_SEMS = 9


def sum_plan(x, o, buffers, sems):
    from_core, s_here, s_send, from_across, t_send, from_copy = buffers
    d, c, m, core, across, copy_of = tensor_place()
    step = ROWS // CHUNKS
    rows = [pl.ds(k * step, step) for k in range(CHUNKS)]
    copies, zero, one, two = [], [], [], []
    for r in rows:
        zero.append(started(copies, x.at[:, 1 - c, r], from_core.at[:, r], *sems.take(), core))
    yield
    for k, r in enumerate(rows):
        zero[k].wait_recv()
        s_send[r] = added(x[1 - d, c, r], from_core[1 - d, r]).astype(bf16)
        one.append(started(copies, s_send.at[r], from_across.at[r], *sems.take(), across))
        s_here[r] = added(x[d, c, r], from_core[d, r])
    yield
    for k, r in enumerate(rows):
        one[k].wait_recv()
        t_send[r] = added(s_here[r], from_across[r]).astype(bf16)
        two.append(started(copies, t_send.at[r], from_copy.at[r], *sems.take(), copy_of))
    yield
    for k, r in enumerate(rows):
        two[k].wait_recv()
        o[r] = added(t_send[r], from_copy[r])
    for copy in copies:
        copy.wait_send()


SUM_SEMS = 3 * CHUNKS
SUM_BUFFERS = [
    pltpu.VMEM((2, ROWS, D), bf16),
    pltpu.VMEM((ROWS, D), f32),
    pltpu.VMEM((ROWS, D), bf16),
    pltpu.VMEM((ROWS, D), bf16),
    pltpu.VMEM((ROWS, D), bf16),
    pltpu.VMEM((ROWS, D), bf16),
]


def weights_plan(w, first, second, low, sems):
    i0, i_up, i_down, i_far, to_i_up, to_i_down = ring(first)
    j0, j_up, j_down, j_far, to_j_up, to_j_down = ring(second)

    def at(i, j, part, n):
        return w.at[(j, i) if first == "y" else (i, j)].at[pl.ds(low + part, n)]

    copies = []

    def send(ref, peer):
        return started(copies, ref, ref, *sems.take(), peer)

    def along(i):
        return i, send(at(i, j0, 0, 2), to_j_up), send(at(i, j0, 0, 2), to_j_down)

    from_down, from_up = send(at(i0, j0, 0, 2), to_i_up), send(at(i0, j0, 0, 2), to_i_down)
    second_leg = [along(i0)]
    yield
    from_down.wait_recv()
    far_low = send(at(i_down, j0, 0, 1), to_i_up)
    from_up.wait_recv()
    far_high = send(at(i_up, j0, 1, 1), to_i_down)
    second_leg += [along(i_down), along(i_up)]
    yield
    onward = []

    def relay(leg):
        i, a, b = leg
        a.wait_recv()
        onward.append(send(at(i, j_down, 0, 1), to_j_up))
        b.wait_recv()
        onward.append(send(at(i, j_up, 1, 1), to_j_down))

    relay(second_leg[0])
    yield
    far_low.wait_recv()
    far_high.wait_recv()
    second_leg.append(along(i_far))
    for leg in second_leg[1:]:
        yield
        relay(leg)
    yield
    for copy in onward:
        copy.wait_recv()
    for copy in copies:
        copy.wait_send()


WEIGHT_SEMS = 20


def to_inner(x, o):
    for k in range(16):
        low, high = x[:, k * 64 : (k + 1) * 64], x[:, D // 2 + k * 64 : D // 2 + (k + 1) * 64]
        o[:, k * HD : (k + 1) * HD] = jnp.concatenate([low, high], 1)


def to_outer(x, o, kind):
    for k in range(0, 16, 2):
        one, two = x(k), x(k + 1)
        o[:, k * 64 : k * 64 + HD] = jnp.concatenate([one[:, :64], two[:, :64]], 1).astype(kind)
        o[:, D // 2 + k * 64 : D // 2 + k * 64 + HD] = jnp.concatenate([one[:, 64:], two[:, 64:]], 1).astype(kind)


def side_of(one, two, starts, padding):
    lane = lax.broadcasted_iota(jnp.int32, (32, HD), 1)
    same = lax.broadcasted_iota(jnp.int32, (32, 32), 0) == lax.broadcasted_iota(jnp.int32, (32, 32), 1)

    def column(row):
        return jnp.sum(jnp.where(same, row[...].astype(f32), 0.0), 1, keepdims=True)

    value = jnp.where(lane == 0, column(one), 0.0)
    value = jnp.where(lane == 1, column(two), value)
    for k in range(3):
        value = jnp.where(lane == 2 + k, starts[:, k : k + 1].astype(f32), value)
    return jnp.where(lane == 5, padding[...].astype(f32), value).astype(bf16)


def start_kernel(
    wq, wk, wv, wo, wu, wd, x_hbm, cot_hbm, one, two, starts, padding, w, s2, rows, x_in, cot_in, x, cot, side, *sems
):
    z, y = lax.axis_index("z"), lax.axis_index("y")
    _, _, _, _, z_up, z_down = ring("z")
    _, _, _, _, y_up, y_down = ring("y")
    d, c = lax.axis_index("dp"), lax.axis_index("c")
    me = 2 * d + c
    here = w.at[z, y, me]
    far = s2.at[me]
    firsts = [(wq, 0, 256), (wk, 256, 256), (wv, 512, 256), (wo, 768, 256)]
    rests = [(wu, 0, 1024), (wd, 1024, 1024)]
    local = sems[8]
    locals_ = [pltpu.make_async_copy(x_hbm, x, local.at[0]), pltpu.make_async_copy(cot_hbm, cot, local.at[1])]
    for k, (src, low, n) in enumerate(firsts):
        locals_.append(pltpu.make_async_copy(quarter(src)(me), here.at[:, pl.ds(low, n)], local.at[2 + k]))
    for k, (src, low, n) in enumerate(rests):
        locals_.append(pltpu.make_async_copy(quarter(src)(me), far.at[:, pl.ds(low, n)], local.at[6 + k]))
    for copy in locals_:
        copy.start()
    side[...] = side_of(one, two, starts, padding)
    here[:, 1024:1152] = side[...]
    greet([*tensor_place()[3:], *swap_peers(), z_up, z_down, y_up, y_down])
    swaps = Sems(*sems[:2])

    def swap(pairs, dst):
        copies = []
        for a, b in [(d, 1 - c), (1 - d, c), (1 - d, 1 - c)]:
            for src, low, n in pairs:
                started(copies, src(2 * a + b), dst.at[:, pl.ds(low, n)], *swaps.take(), {"dp": a, "c": b})
        return copies

    swap_first = swap([(quarter(src), low, n) for src, low, n in firsts] + [(lambda q: side, 1024, HD)], here)
    locals_[0].wait()
    to_inner(x, x_in)
    gather_x = rows_plan(x_in, rows, Sems(*sems[2:4]))
    next(gather_x)
    for copy in locals_[2:6]:
        copy.wait()
    for copy in swap_first:
        copy.wait_recv()
    legs = [weights_plan(w, "y", "z", 0, Sems(*sems[4:6])), weights_plan(w, "z", "y", 2, Sems(*sems[6:8]))]
    for leg in legs:
        next(leg)
    swap_rest = swap([(quarter(src), low, n) for src, low, n in rests], far)
    locals_[1].wait()
    to_inner(cot, cot_in)
    run(*legs, gather_x)
    for copy in locals_[6:] + swap_rest:
        copy.wait()
    for copy in swap_first:
        copy.wait_send()


def start(*args):
    whole = lambda *shape: pl.BlockSpec(shape, lambda i: (0,) * len(shape))
    return pl.pallas_call(
        start_kernel,
        grid=(1,),
        out_shape=[
            jax.ShapeDtypeStruct((4, 4, 4, 32, 1152), bf16),
            jax.ShapeDtypeStruct((4, 32, 2048), bf16),
            jax.ShapeDtypeStruct((4, ROWS, D), bf16),
            jax.ShapeDtypeStruct((ROWS, D), bf16),
            jax.ShapeDtypeStruct((ROWS, D), bf16),
        ],
        in_specs=[pl.BlockSpec(memory_space=pl.ANY)] * 8 + [whole(1, 32), whole(1, 32), whole(1, 3), whole(1, 1)],
        out_specs=vmem_specs(5),
        scratch_shapes=[pltpu.VMEM((ROWS, D), bf16)] * 2
        + [pltpu.VMEM((32, HD), bf16)]
        + sem_pair(21)
        + sem_pair(ROWS_SEMS)
        + sem_pair(WEIGHT_SEMS)
        + sem_pair(WEIGHT_SEMS)
        + [pltpu.SemaphoreType.DMA((8,))],
        compiler_params=params(3, vmem=60),
        name="start",
    )(*args)


def spread_plan(x, q, kv, sems):
    z, z_up, z_down, z_far, to_z_up, to_z_down = ring("z")
    y, y_up, y_down, y_far, to_y_up, to_y_down = ring("y")
    far = {"z": z_far}
    copies, firsts, queries, nears, fars = [], [], [], [], []
    both = pl.ds(1, 2)
    peers = [(z_up, to_z_up, z_down), (z_down, to_z_down, z_up), (z_far, far, z_far)]
    for place, peer, _ in peers:
        firsts.append(started(copies, x.at[place, both], kv.at[z, y], *sems.take(), peer))
    kv[z, y] = x[z, both]

    def along(place):
        ref = kv.at[place, y]
        nears.append(
            (place, started(copies, ref, ref, *sems.take(), to_y_up), started(copies, ref, ref, *sems.take(), to_y_down))
        )

    along(z)
    for place, peer, _ in peers:
        queries.append(started(copies, x.at[place, 0], q.at[z], *sems.take(), peer))
    q[z] = x[z, 0]
    yield
    for k, (_, _, source) in enumerate(peers):
        firsts[k].wait_recv()
        along(source)
        yield
    for copy in queries:
        copy.wait_recv()
    yield
    for place, a, b in nears:
        a.wait_recv()
        ref = kv.at[place, y_down, 0]
        fars.append(started(copies, ref, ref, *sems.take(), to_y_up))
        b.wait_recv()
        ref = kv.at[place, y_up, 1]
        fars.append(started(copies, ref, ref, *sems.take(), to_y_down))
        yield
    for copy in fars:
        copy.wait_recv()
    yield
    for copy in copies:
        copy.wait_send()


def ring_sum(at, axis, buffers, sems, put, late=False):
    one, two, passed = buffers
    me, up, down, far, to_up, to_down = ring(axis)
    copies = []
    a = started(copies, at(far, 0), one.at[0], *sems.take(), to_up)
    b = started(copies, at(far, 1), one.at[1], *sems.take(), to_down)
    if late:
        yield
    plain = [started(copies, at(up, 1), two.at[0, 1], *sems.take(), to_up)]
    if not late:
        plain.append(started(copies, at(down, 0), two.at[1, 0], *sems.take(), to_down))
        yield
    a.wait_recv()
    passed[0] = added(at(up, 0)[...], one[0]).astype(bf16)
    plain.append(started(copies, passed.at[0], two.at[0, 0], *sems.take(), to_up))
    if late:
        yield
        plain.append(started(copies, at(down, 0), two.at[1, 0], *sems.take(), to_down))
    b.wait_recv()
    passed[1] = added(at(down, 1)[...], one[1]).astype(bf16)
    plain.append(started(copies, passed.at[1], two.at[1, 1], *sems.take(), to_down))
    yield
    for copy in plain:
        copy.wait_recv()
    for part in range(2):
        put(part, added(at(me, part)[...], two[0, part], two[1, part]))
    yield
    for copy in copies:
        copy.wait_send()


RING_SEMS = 6


def ring_buffers(n, part):
    return [pltpu.VMEM((n, 2, *part), bf16), pltpu.VMEM((n, 2, 2, *part), bf16), pltpu.VMEM((n, 2, *part), bf16)]


def collect_plan(dq, dkv, o, total, buffers, sems):
    z, peers = z_peers()
    peers = peers + [(z, None)]
    copies, rings = [], []
    for k, (place, peer) in enumerate(peers):

        def at(i, part, place=place):
            return dkv.at[place, i, part]

        def put(part, value, k=k):
            if k < 3:
                total[k, part] = value.astype(bf16)
            else:
                o[z, 1 + part] = value.astype(bf16)

        rings.append(ring_sum(at, "y", [b.at[k] for b in buffers], sems, put, True))
    for _ in range(3):
        for r in rings:
            next(r)
        yield
    for place, peer in peers[:3]:
        started(copies, dq.at[place], o.at[z, 0], *sems.take(), peer)
    o[z, 0] = dq[z]
    for k, r in enumerate(rings):
        next(r)
        if k < 3:
            started(copies, total.at[k], o.at[z, pl.ds(1, 2)], *sems.take(), peers[k][1])
    yield
    for copy in copies:
        copy.wait()
    run(*rings)


def grads_plan(g, shard, first, second, low, legs, buffers, sems):
    rings = []
    for j in range(4):

        def at(i, part, j=j):
            z, y = (j, i) if first == "y" else (i, j)
            return g.at[pl.ds(pl.multiple_of(((4 * z + y) * 4 + low + part) * 32, 32), 32)]

        def put(part, value, j=j):
            legs[j, part] = value.astype(bf16)

        rings.append(ring_sum(at, first, [b.at[j] for b in buffers], sems, put))
    for _ in range(3):
        for r in rings:
            next(r)
        yield

    def put_last(part, value):
        shard[low + part] = value.astype(bf16)

    rings.append(ring_sum(lambda i, part: legs.at[i, part], second, [b.at[4] for b in buffers], sems, put_last))
    for _ in range(3):
        next(rings[-1])
        yield
    run(*rings)


def reach(facts, block, rows):
    t = block * rows + lax.broadcasted_iota(jnp.int32, (rows, 1), 0)
    one, two, three, padding = (facts[:, k : k + 1].astype(jnp.int32) for k in range(2, 6))
    begin = jnp.where(t >= three, three, jnp.where(t >= two, two, one))
    living = t < LEN - padding
    end = jnp.minimum((t // FRAME + 1) * FRAME, LEN - padding)
    return t, begin, jnp.where(living, begin, t), jnp.where(living, end, t + 1)


def dot_t(a, b):
    return lax.dot_general(a, b, (((1,), (1,)), ((), ())), preferred_element_type=f32)


def dot_l(a, b):
    return lax.dot_general(a, b, (((0,), (0,)), ((), ())), preferred_element_type=f32)


def column_scores(facts, q, kv, i, column):
    n = (i + 1) * BLOCK
    _, _, low, high = reach(facts[pl.ds(lax.axis_index("z") // 2, 1)], 4 * i + lax.axis_index("y"), BLOCK)
    k = kv[0 : i + 1, column, 0].reshape(n, HD)
    at = lax.broadcasted_iota(jnp.int32, (1, n), 1)
    at = (at // BLOCK) * (4 * BLOCK) + at % BLOCK + column * BLOCK
    return k, jnp.where((at >= low) & (at < high), dot_t(q[i], k) * scale, -1e30)


def attend_tile(facts, q, kv, top, total, acc, i, column, first):
    _, s = column_scores(facts, q, kv, i, column)
    v = kv[0 : i + 1, column, 1].reshape((i + 1) * BLOCK, HD)
    now = jnp.max(s, -1, keepdims=True)
    if not first:
        before = top[i][:, :1]
        now = jnp.maximum(before, now)
    p = jnp.exp(s - now)
    plus = jnp.sum(p, -1, keepdims=True)
    out = jnp.dot(p.astype(bf16), v, preferred_element_type=f32)
    if not first:
        shrink = jnp.exp(before - now)
        plus = plus + total[i][:, :1] * shrink
        out = out + acc[i] * shrink
    top[i] = jnp.broadcast_to(now, (BLOCK, HD))
    total[i] = jnp.broadcast_to(plus, (BLOCK, HD))
    acc[i] = out


def attend_back_tile(facts, q, kv, do, lse, inner, dq, acc, i, column, first):
    k, s = column_scores(facts, q, kv, i, column)
    n = i + 1
    v = kv[0:n, column, 1].reshape(n * BLOCK, HD)
    p = jnp.exp(s - lse[i][:, :1])
    ds = (p * (dot_t(do[i], v) - inner[i][:, :1])).astype(bf16)
    dv = dot_l(p.astype(bf16), do[i]).reshape(n, BLOCK, HD)
    dk = dot_l(ds, q[i]).reshape(n, BLOCK, HD)
    part = jnp.dot(ds, k, preferred_element_type=f32)
    if i == 3:
        acc[:, 0], acc[:, 1] = dk, dv
    else:
        acc[0:n, 0] += dk
        acc[0:n, 1] += dv
    dq[i] = part if first else dq[i] + part


def attend_back_kernel(
    facts, q, kv, o, lse, do, part, grads_up, out, summed, shard, acc, dq, dq_low, dkv, inner, total, *scratch
):
    _, _, _, z_far, z_up, z_down = ring("z")
    y, up, down, far, y_up, y_down = ring("y")
    greet([*tensor_place()[3:], z_up, z_down, {"z": z_far}, y_up, y_down])
    fed = sum_plan(part, summed, scratch[5:11], Sems(*scratch[11:13]))
    legs = [
        grads_plan(grads_up, shard, "z", "y", 0, scratch[13], scratch[15:18], Sems(*scratch[21:23])),
        grads_plan(grads_up, shard, "y", "z", 2, scratch[14], scratch[18:21], Sems(*scratch[23:25])),
    ]
    for leg in legs:
        next(leg)
    grads = collect_plan(dq_low, dkv, out, total, scratch[:3], Sems(*scratch[3:5]))
    next(fed)
    for i in range(4):
        value = jnp.sum(o[i] * do[i].astype(f32), -1, keepdims=True)
        inner[i] = jnp.broadcast_to(value, (BLOCK, HD))
    for column in (far, up, down, y):
        for i in (3, 2, 1, 0):
            attend_back_tile(facts, q, kv, do, lse, inner, dq, acc, i, column, column is far)
            if i == 2 and column is not far:
                for leg in legs:
                    next(leg)
        for k in range(4):
            dkv[k, column, 0] = (acc[k, 0] * scale).astype(bf16)
            dkv[k, column, 1] = acc[k, 1].astype(bf16)
        if column is y:
            dq_low[...] = (dq[...] * scale).astype(bf16)
        next(grads)
        next(fed, None)
    run(grads, fed, *legs)


def attend_back(facts, q, kv, o, lse, do, part, grads_up):
    return pl.pallas_call(
        attend_back_kernel,
        out_shape=[
            jax.ShapeDtypeStruct((4, 3, BLOCK, HD), bf16),
            jax.ShapeDtypeStruct((ROWS, D), f32),
            jax.ShapeDtypeStruct((4, 32, 1024), bf16),
        ],
        in_specs=vmem_specs(8),
        out_specs=vmem_specs(3),
        scratch_shapes=[
            pltpu.VMEM((4, 2, BLOCK, HD), f32),
            pltpu.VMEM((4, BLOCK, HD), f32),
            pltpu.VMEM((4, BLOCK, HD), bf16),
            pltpu.VMEM((4, 4, 2, BLOCK, HD), bf16),
            pltpu.VMEM((4, BLOCK, HD), f32),
            pltpu.VMEM((3, 2, BLOCK, HD), bf16),
        ]
        + ring_buffers(4, (BLOCK, HD))
        + sem_pair(4 * RING_SEMS + 6)
        + SUM_BUFFERS
        + sem_pair(SUM_SEMS)
        + [pltpu.VMEM((4, 2, 32, 1024), bf16)] * 2
        + ring_buffers(5, (32, 1024)) * 2
        + sem_pair(5 * RING_SEMS) * 2,
        compiler_params=params(6, vmem=56),
        name="attend_back",
    )(facts, q, kv, o, lse, do, part, grads_up)


def norm(value):
    centre = value - jnp.mean(value, -1, keepdims=True)
    r = lax.rsqrt(jnp.mean(centre * centre, -1, keepdims=True) + epsilon)
    return centre * r, r


def norm_back(grad, n, r, gain):
    e = grad * gain
    return r * (e - jnp.mean(e, -1, keepdims=True) - n * jnp.mean(e * n, -1, keepdims=True))


def one_hot(rows, places):
    at = lax.broadcasted_iota(jnp.int32, (rows, HD), 0)
    lane = lax.broadcasted_iota(jnp.int32, (rows, HD), 1)
    hot = at < 0
    for k, place in enumerate(places):
        hot = hot | ((at == k) & (lane == place))
    return jnp.where(hot, 1.0, 0.0).astype(bf16)


def tables(facts, seq, c):
    block = (4 * lax.axis_index("z") + lax.axis_index("y")) * 2 + c
    t, begin, _, _ = reach(facts[seq : seq + 1], block, ROWS)
    lane = lax.broadcasted_iota(jnp.int32, (1, HD), 1)
    i = jnp.where(lane < HD // 2, lane, lane - HD // 2).astype(f32)
    angles = (t - begin).astype(f32) * jnp.exp(i * (-2.0 * LOG_BASE / HD))
    return jnp.cos(angles), jnp.where(lane < HD // 2, -1.0, 1.0) * jnp.sin(angles)


def project_kernel(
    x, w_hbm, cot, n1, n1_t, gains, facts, q, kv, rows, o, lse, mixed, w, qkv, top, total, acc, *sems
):
    load = pltpu.make_async_copy(w_hbm, w, sems[4].at[0])
    load.start()
    _, _, _, z_far, z_up, z_down = ring("z")
    y, up, down, far, y_up, y_down = ring("y")
    greet([*tensor_place()[3:], z_up, z_down, {"z": z_far}, y_up, y_down])
    gather = rows_plan(cot, rows, Sems(*sems[2:4]))
    next(gather)
    load.wait()
    side = w[:, 1024:1152]
    gains[...] = dot_t(one_hot(8, (0, 1)), side)
    facts[...] = jnp.zeros_like(facts)
    facts[0:1] = side[0:1].astype(f32)
    facts[1:2] = side[64:65].astype(f32)
    for seq in range(2):
        for c in range(2):
            r = pl.ds((2 * seq + c) * ROWS, ROWS)
            n, _ = norm(x[r].astype(f32))
            n1[r] = (n * gains[0:1]).astype(bf16)
            lin = jnp.dot(n1[r], w[:, :768], preferred_element_type=f32)
            cosine, sine = tables(facts, seq, c)
            for kind in range(3):
                for h in range(2):
                    v = lin[:, (2 * kind + h) * HD : (2 * kind + h + 1) * HD]
                    if kind < 2:
                        v = v * cosine + pltpu.roll(v, HD // 2, 1) * sine
                    qkv[2 * seq + h, kind, c * ROWS : (c + 1) * ROWS] = v.astype(bf16)
    keys = spread_plan(qkv, q, kv, Sems(*sems[:2]))

    def work():
        for k in range(4):
            some = slice(512 * k, 512 * (k + 1))
            n1_t[some] = n1[:, some].T
            yield
        for i in range(4):
            attend_tile(facts, q, kv, top, total, acc, i, y, True)
            yield

    pieces = work()
    next(keys)
    next(gather)
    for _ in range(4):
        next(pieces)
        next(keys)
    next(gather)
    for _ in range(4):
        next(pieces)
        next(keys)
    next(gather, None)
    for column in (down, up):
        for i in range(4):
            attend_tile(facts, q, kv, top, total, acc, i, column, False)
    run(keys, gather)
    for i in range(4):
        attend_tile(facts, q, kv, top, total, acc, i, far, False)
    for i in range(4):
        out = acc[i] / total[i]
        o[i] = out
        mixed[i] = out.astype(bf16)
        lse[i] = top[i] + jnp.log(total[i])


def project(x, w, cot):
    block = (4, BLOCK, HD)
    return pl.pallas_call(
        project_kernel,
        out_shape=[
            jax.ShapeDtypeStruct((512, D), bf16),
            jax.ShapeDtypeStruct((D, 512), bf16),
            jax.ShapeDtypeStruct((8, D), f32),
            jax.ShapeDtypeStruct((8, HD), f32),
            jax.ShapeDtypeStruct(block, bf16),
            jax.ShapeDtypeStruct((4, 4, 2, BLOCK, HD), bf16),
            jax.ShapeDtypeStruct((4, ROWS, D), bf16),
            jax.ShapeDtypeStruct(block, f32),
            jax.ShapeDtypeStruct(block, f32),
            jax.ShapeDtypeStruct(block, bf16),
        ],
        in_specs=vmem_specs(1) + [pl.BlockSpec(memory_space=pl.ANY)] + vmem_specs(1),
        out_specs=vmem_specs(10),
        scratch_shapes=[pltpu.VMEM((D, 1152), bf16), pltpu.VMEM((4, 3, BLOCK, HD), bf16)]
        + [pltpu.VMEM(block, f32)] * 3
        + sem_pair(22)
        + sem_pair(ROWS_SEMS)
        + [pltpu.SemaphoreType.DMA((1,))],
        compiler_params=params(4, vmem=56),
        name="project",
    )(x, w, cot)


def sum_norm_plan(x, all_rows, make, buffers, sems, idle=lambda: None):
    from_core, s_here, s_send, from_across, t_send, from_copy = buffers
    d, c, m, core, across, copy_of = tensor_place()
    me, far = 2 * d + c, 2 * (1 - d) + c
    step = ROWS // CHUNKS
    rows = [pl.ds(k * step, step) for k in range(CHUNKS)]
    copies, zero, one, two = [], [], [], []
    for r in rows:
        zero.append(started(copies, x.at[:, 1 - c, r], from_core.at[:, r], *sems.take(), core))
    yield
    for k, r in enumerate(rows):
        zero[k].wait_recv()
        s_send[r] = added(x[1 - d, c, r], from_core[1 - d, r]).astype(bf16)
        one.append(started(copies, s_send.at[r], from_across.at[r], *sems.take(), across))
        s_here[r] = added(x[d, c, r], from_core[d, r])
    idle()
    for k, r in enumerate(rows):
        idle()
        one[k].wait_recv()
        t_send[r] = added(s_here[r], from_across[r]).astype(bf16)
        two.append(started(copies, t_send.at[r], from_copy.at[r], *sems.take(), copy_of))
    yield
    nears, firsts, seconds, lasts = [], [], [], []
    idle()
    for k, r in enumerate(rows):
        idle()
        two[k].wait_recv()
        all_rows[me, r] = make(r, added(t_send[r], from_copy[r])).astype(bf16)
        nears.append(started(copies, all_rows.at[me, r], all_rows.at[me, r], *sems.take(), core))
        half = pl.ds(pl.multiple_of(k * step + m * (step // 2), step // 2), step // 2)
        firsts.append(started(copies, all_rows.at[me, half], all_rows.at[me, half], *sems.take(), across))
    yield

    def onward(half, peer):
        return started(copies, all_rows.at[far, half], all_rows.at[far, half], *sems.take(), peer)

    idle()
    for k in range(CHUNKS):
        idle()
        firsts[k].wait_recv()
        half = pl.ds(pl.multiple_of(k * step + (1 - m) * (step // 2), step // 2), step // 2)
        seconds.append(onward(half, copy_of))
        lasts.append(onward(half, core))
    yield
    idle()
    for k in range(CHUNKS):
        idle()
        seconds[k].wait_recv()
        half = pl.ds(pl.multiple_of(k * step + m * (step // 2), step // 2), step // 2)
        lasts.append(onward(half, core))
    yield
    for copy in nears + lasts:
        copy.wait_recv()
    yield
    for copy in copies:
        copy.wait_send()


SUM_NORM_SEMS = 8 * CHUNKS
OUT_COLUMNS = pl.BlockSpec((D, 256), lambda i: (0, 3))


def z_peers():
    z, z_up, z_down, z_far, to_z_up, to_z_down = ring("z")
    return z, [(z_up, to_z_up), (z_down, to_z_down), (z_far, {"z": z_far})]


def mix_kernel(o, w, x, gains, mixed, middle, n2, turned, part, *scratch):
    z, peers = z_peers()
    c = lax.axis_index("c")
    greet([*tensor_place()[3:], *[peer for _, peer in peers]])
    turns, copies = Sems(*scratch[8:]), []
    for place, peer in peers:
        started(copies, o.at[place], turned.at[z], *turns.take(), peer)
    turned[z] = o[z]
    for copy in copies:
        copy.wait()
    for seq in range(2):
        for h in range(2):
            mixed[seq * BLOCK : (seq + 1) * BLOCK, h * HD : (h + 1) * HD] = turned[2 * seq + h]

    def partial(to):
        for seq in range(2):
            rows = pl.ds(pl.multiple_of(seq * BLOCK + to * ROWS, ROWS), ROWS)
            part[seq, to] = dot_t(mixed[rows], w[...]).astype(bf16)

    def make(r, total):
        value = x[r].astype(f32) + total
        middle[r] = value
        return norm(value)[0] * gains[1:2]

    partial(1 - c)
    plan = sum_norm_plan(part, n2, make, scratch[:6], Sems(*scratch[6:8]))
    next(plan)
    partial(c)
    run(plan)


def mix(o, first, x, gains):
    return pl.pallas_call(
        mix_kernel,
        grid=(1,),
        out_shape=[
            jax.ShapeDtypeStruct((512, 256), bf16),
            jax.ShapeDtypeStruct((ROWS, D), f32),
            jax.ShapeDtypeStruct((4, ROWS, D), bf16),
        ],
        in_specs=vmem_specs(1) + [OUT_COLUMNS] + vmem_specs(2),
        out_specs=vmem_specs(3),
        scratch_shapes=[pltpu.VMEM((4, BLOCK, HD), bf16), pltpu.VMEM((2, 2, ROWS, D), bf16)]
        + SUM_BUFFERS
        + sem_pair(SUM_NORM_SEMS)
        + sem_pair(3),
        compiler_params=params(1),
        name="mix",
    )(o, first, x, gains)


def feed_kernel(
    n2,
    cot_all,
    middle,
    cot,
    gains,
    w,
    weights,
    mixed,
    fed,
    grads_up,
    grad_out,
    grad_middle,
    turned,
    gain_two,
    shard,
    up,
    down,
    n2_t,
    cot_t,
    grads_down,
    branch,
    active,
    grad_hidden,
    part,
    grad_mixed,
    *scratch,
):
    z, peers = z_peers()
    c = lax.axis_index("c")
    local = scratch[10]
    _, _, _, _, z_up, z_down = ring("z")
    _, _, _, _, y_up, y_down = ring("y")
    loads = [
        pltpu.make_async_copy(weights.at[:, pl.ds(1024, 1024)], down, local.at[0]),
        pltpu.make_async_copy(weights.at[:, pl.ds(0, 1024)], up, local.at[1]),
    ]
    for copy in loads:
        copy.start()
    gain_two[...] = jnp.zeros_like(gain_two)
    greet([*tensor_place()[3:], *[peer for _, peer in peers], y_up, y_down])
    for copy in loads:
        copy.wait()

    def partial(to):
        n = n2[:, to].reshape(2 * ROWS, D)
        g = cot_all[:, to].reshape(2 * ROWS, D)
        for j in range(4):
            some = slice(256 * j, 256 * (j + 1))
            grad_active = jnp.dot(g, down[:, some], preferred_element_type=f32)
            hidden = jnp.dot(n, up[:, some], preferred_element_type=f32)
            half = 0.5 * (1.0 + lax.erf(hidden * 0.5**0.5))
            slope = half + hidden * jnp.exp(-0.5 * hidden * hidden) * (0.5 / jnp.pi) ** 0.5
            active[:, to, :, some] = (hidden * half).astype(bf16).reshape(2, ROWS, 256)
            grad_hidden[:, to, :, some] = (grad_active * slope).astype(bf16).reshape(2, ROWS, 256)
        value = grad_hidden[:, to].reshape(2 * ROWS, 1024)
        for k in range(4):
            some = slice(512 * k, 512 * (k + 1))
            part[:, to, :, some] = dot_t(value, up[some]).astype(bf16).reshape(2, ROWS, 512)

    legs = [
        grads_plan(grads_down, shard, "z", "y", 0, scratch[11], scratch[13:16], Sems(*scratch[19:21])),
        grads_plan(grads_down, shard, "y", "z", 2, scratch[12], scratch[16:19], Sems(*scratch[21:23])),
    ]

    def turn_cot(k):
        some = slice(512 * k, 512 * (k + 1))
        cot_t[some] = cot_all[:, :, :, some].reshape(512, 512).T

    def turn_n2(k):
        some = slice(512 * k, 512 * (k + 1))
        n2_t[some] = n2[:, :, :, some].reshape(512, 512).T

    def down_piece(j):
        some = slice(256 * j, 256 * (j + 1))
        value = active[:, :, :, some].reshape(512, 256)
        grads_down[:, some] = jnp.dot(cot_t[...], value, preferred_element_type=f32).astype(bf16)

    def up_piece(j):
        some = slice(256 * j, 256 * (j + 1))
        value = grad_hidden[:, :, :, some].reshape(512, 256)
        grads_up[:, some] = jnp.dot(n2_t[...], value, preferred_element_type=f32).astype(bf16)

    def fed_piece(k):
        some = slice(512 * k, 512 * (k + 1))
        value = dot_t(active[...].reshape(512, 1024), down[some])
        fed[:, :, :, some] = value.astype(bf16).reshape(2, 2, ROWS, 512)

    def leg_step():
        for leg in legs:
            next(leg, None)

    def work():
        for k in range(2):
            turn_cot(2 * k)
            turn_cot(2 * k + 1)
            yield
        for k in range(2):
            down_piece(2 * k)
            down_piece(2 * k + 1)
            if k:
                leg_step()
            yield
        for k in range(4):
            turn_n2(k)
        yield
        for j in range(4):
            up_piece(j)
            yield
        leg_step()
        yield
        for k in range(4):
            fed_piece(k)
            yield
        leg_step()
        yield

    pieces = work()

    def make(r, total):
        n, rate = norm(middle[r])
        gain_two[0:1] += 0.5 * jnp.sum(total * n, 0, keepdims=True)
        value = cot[r].astype(f32) + norm_back(total, n, rate, gains[1:2])
        grad_middle[r] = value
        return value

    partial(1 - c)
    plan = sum_norm_plan(part, branch, make, scratch[:6], Sems(*scratch[6:8]), lambda: next(pieces, None))
    next(plan)
    partial(c)
    run(plan)
    for k in range(4):
        value = jnp.dot(branch[k], w[...], preferred_element_type=f32).astype(bf16)
        for h in range(2):
            grad_mixed[2 * (k // 2) + h, (k % 2) * ROWS : (k % 2 + 1) * ROWS] = value[:, h * HD : (h + 1) * HD]
    turns, copies = Sems(*scratch[8:10]), []
    for place, peer in peers:
        started(copies, grad_mixed.at[place], turned.at[z], *turns.take(), peer)
    turned[z] = grad_mixed[z]
    for _ in pieces:
        pass
    leg_step()
    for k in range(4):
        some = slice(512 * k, 512 * (k + 1))
        grad_out[some] = dot_l(branch[:, :, some].reshape(512, 512), mixed[...]).astype(bf16)
    for copy in copies:
        copy.wait()
    run(*legs)


def feed(n2, cot_all, middle, cot, gains, first, weights, mixed):
    whole = lambda *shape: pl.BlockSpec(shape, lambda i: (0,) * len(shape))
    anywhere = pl.BlockSpec(memory_space=pl.ANY)
    rows = (2, 2, ROWS, D)
    return pl.pallas_call(
        feed_kernel,
        grid=(1,),
        out_shape=[
            jax.ShapeDtypeStruct(rows, bf16),
            jax.ShapeDtypeStruct((D, 1024), bf16),
            jax.ShapeDtypeStruct((D, 256), bf16),
            jax.ShapeDtypeStruct((ROWS, D), f32),
            jax.ShapeDtypeStruct((4, BLOCK, HD), bf16),
            jax.ShapeDtypeStruct((8, D), f32),
            jax.ShapeDtypeStruct((4, 32, 1024), bf16),
        ],
        in_specs=vmem_specs(5) + [OUT_COLUMNS, anywhere] + vmem_specs(1),
        out_specs=vmem_specs(7),
        scratch_shapes=[
            pltpu.VMEM((D, 1024), bf16),
            pltpu.VMEM((D, 1024), bf16),
            pltpu.VMEM((D, 512), bf16),
            pltpu.VMEM((D, 512), bf16),
            pltpu.VMEM((D, 1024), bf16),
            pltpu.VMEM((4, ROWS, D), bf16),
            pltpu.VMEM((2, 2, ROWS, 1024), bf16),
            pltpu.VMEM((2, 2, ROWS, 1024), bf16),
            pltpu.VMEM(rows, bf16),
            pltpu.VMEM((4, BLOCK, HD), bf16),
        ]
        + SUM_BUFFERS
        + sem_pair(SUM_NORM_SEMS)
        + sem_pair(3)
        + [pltpu.SemaphoreType.DMA((2,))]
        + [pltpu.VMEM((4, 2, 32, 1024), bf16)] * 2
        + ring_buffers(5, (32, 1024)) * 2
        + sem_pair(5 * RING_SEMS) * 2,
        compiler_params=params(2, vmem=60),
        name="feed",
    )(n2.reshape(rows), cot_all.reshape(rows), middle, cot, gains, first, weights, mixed)


def end_kernel(
    grads, w_hbm, n1, n1_t, grad_out, gains, facts, gain_two, down, up, o, gain, summed, down_all, up_all, *scratch
):
    w, lin, last, side, part, shard, side_shard, side_all, mine, theirs = scratch[:10]
    legs_a, legs_b, side_a, side_b = scratch[10:14]
    rings = [scratch[14 + 3 * k : 17 + 3 * k] for k in range(4)]
    sums = scratch[26:32]
    sems = [Sems(*scratch[32 + 2 * k : 34 + 2 * k]) for k in range(6)]
    load = pltpu.make_async_copy(w_hbm, w, scratch[44].at[0])
    load.start()
    d, c, m, core, across, copy_of = tensor_place()
    _, _, _, _, z_up, z_down = ring("z")
    _, _, _, _, y_up, y_down = ring("y")
    greet([core, across, copy_of, *swap_peers(), z_up, z_down, y_up, y_down])
    swap_feed = swap_plan(
        [(lambda q: down.at[q], lambda me: down_all.at[me]), (lambda q: up.at[q], lambda me: up_all.at[me])], sems[0]
    )
    next(swap_feed)
    for seq in range(2):
        for half in range(2):
            rows = pl.ds((2 * seq + half) * ROWS, ROWS)
            cosine, sine = tables(facts, seq, half)
            for kind in range(3):
                for h in range(2):
                    v = grads[2 * seq + h, kind, half * ROWS : (half + 1) * ROWS]
                    if kind < 2:
                        v = v.astype(f32)
                        v = (v * cosine - pltpu.roll(v, HD // 2, 1) * sine).astype(bf16)
                    lin[rows, (2 * kind + h) * HD : (2 * kind + h + 1) * HD] = v
    blocks = [slice(512 * k, 512 * (k + 1)) for k in range(4)]
    for some in blocks:
        last[some, 0:768] = jnp.dot(n1_t[some], lin[...], preferred_element_type=f32).astype(bf16)
        last[some, 768:1024] = grad_out[some]
    legs = [
        grads_plan(last, shard, "z", "y", 0, legs_a, rings[0], sems[1]),
        grads_plan(last, shard, "y", "z", 2, legs_b, rings[1], sems[2]),
    ]
    for leg in legs:
        next(leg)
    load.wait()
    hot = one_hot(8, (0, 1))
    for some in blocks:
        p = dot_t(lin[...], w[some, 0:768])
        part[:, :, :, some] = p.astype(bf16).reshape(2, 2, ROWS, 512)
        gain_one = jnp.sum(p * n1[:, some].astype(f32), 0, keepdims=True) / gains[0:1, some]
        both = jnp.concatenate([gain_one, gain_two[0:1, some], jnp.zeros((6, 512), f32)], 0)
        side[some] = dot_l(both.astype(bf16), hot).astype(bf16)

    def gains_plan():
        halves = [
            grads_plan(side, side_shard, "z", "y", 0, side_a, rings[2], sems[3]),
            grads_plan(side, side_shard, "y", "z", 2, side_b, rings[3], sems[4]),
        ]
        for _ in range(6):
            for half in halves:
                next(half)
            yield
        run(*halves)
        swap = swap_plan([(lambda q: side_shard.at[q], lambda me: side_all.at[me])], sems[0])
        next(swap)
        yield
        run(swap)
        mine[...] = added(side_all[0], side_all[1], side_all[2], side_all[3])
        copy = remote(mine, theirs, *sems[0].take(), copy_of)
        copy.start()
        yield
        copy.wait()
        gain[...] = mine[...] + theirs[...]

    total = sum_plan(part, summed, sums, sems[5])
    by_gain = gains_plan()
    next(total)
    next(by_gain)
    for plan in (total, by_gain, *legs, total, by_gain, *legs, by_gain, swap_feed, total, *legs, by_gain, *legs, by_gain):
        next(plan, None)
    run(*legs, by_gain, total)
    run(swap_plan([(lambda q: shard.at[q], lambda me: o.at[me])], sems[0]), swap_feed)


def end(grads, w, n1, n1_t, grad_out, gains, facts, gain_two, down, up):
    block, narrow = (32, 1024), (32, HD)
    return pl.pallas_call(
        end_kernel,
        out_shape=[
            jax.ShapeDtypeStruct((4, *block), bf16),
            jax.ShapeDtypeStruct(narrow, f32),
            jax.ShapeDtypeStruct((ROWS, D), f32),
            jax.ShapeDtypeStruct((4, *block), bf16),
            jax.ShapeDtypeStruct((4, *block), bf16),
        ],
        in_specs=vmem_specs(1) + [pl.BlockSpec(memory_space=pl.ANY)] + vmem_specs(8),
        out_specs=vmem_specs(5),
        scratch_shapes=[
            pltpu.VMEM((D, 1152), bf16),
            pltpu.VMEM((512, 768), bf16),
            pltpu.VMEM((D, 1024), bf16),
            pltpu.VMEM((D, HD), bf16),
            pltpu.VMEM((2, 2, ROWS, D), bf16),
            pltpu.VMEM((4, *block), bf16),
            pltpu.VMEM((4, *narrow), bf16),
            pltpu.VMEM((4, *narrow), bf16),
            pltpu.VMEM(narrow, f32),
            pltpu.VMEM(narrow, f32),
        ]
        + [pltpu.VMEM((4, 2, *block), bf16)] * 2
        + [pltpu.VMEM((4, 2, *narrow), bf16)] * 2
        + ring_buffers(5, block) * 2
        + ring_buffers(5, narrow) * 2
        + SUM_BUFFERS
        + sem_pair(13)
        + sem_pair(5 * RING_SEMS) * 4
        + sem_pair(SUM_SEMS)
        + [pltpu.SemaphoreType.DMA((1,))],
        compiler_params=params(7, vmem=60),
        name="end",
    )(grads, w, n1, n1_t, grad_out, gains, facts, gain_two, down, up)


def finish_kernel(
    last, grad_down, grad_up, gain, summed, x, grad_middle, gains, middle, fed, out, g_in, g_q, g_k, g_v, g_out, g_up, g_down, g_one, g_two, total
):
    total[...] = middle[...] + fed[...]
    to_outer(lambda k: total[:, k * HD : (k + 1) * HD], out, bf16)
    n, rate = norm(x[...].astype(f32))
    total[...] = grad_middle[...] + norm_back(summed[...], n, rate, gains[0:1])
    to_outer(lambda k: total[:, k * HD : (k + 1) * HD], g_in, f32)
    for q in range(4):
        for k, o in enumerate((g_q, g_k, g_v)):
            o[:, q * 256 : (q + 1) * 256] = last[q, :, k * 256 : (k + 1) * 256].astype(f32)
        g_out[:, q * 256 : (q + 1) * 256] = last[q, :, 768:1024].astype(f32)
        g_down[:, q * 1024 : (q + 1) * 1024] = grad_down[q].astype(f32)
        g_up[:, q * 1024 : (q + 1) * 1024] = grad_up[q].astype(f32)
    gain_t = gain[...].T
    g_one[...] = gain_t[0]
    g_two[...] = gain_t[1]


def finish(*args):
    def shape(*dims, kind=f32):
        return jax.ShapeDtypeStruct(dims, kind)

    return pl.pallas_call(
        finish_kernel,
        out_shape=[
            shape(ROWS, D, kind=bf16),
            shape(ROWS, D),
            shape(32, 1024),
            shape(32, 1024),
            shape(32, 1024),
            shape(32, 1024),
            shape(32, 4096),
            shape(32, 4096),
            shape(32),
            shape(32),
        ],
        in_specs=vmem_specs(10),
        out_specs=vmem_specs(10),
        scratch_shapes=[pltpu.VMEM((ROWS, D), f32)],
        compiler_params=params(),
        name="finish",
    )(*args)


def gather_weights(x):
    return lax.all_gather(x, ZY, axis=0, tiled=True)


def local(
    inputs,
    clip_starts,
    pad_lengths,
    w_query,
    w_key,
    w_value,
    w_out,
    w_up,
    w_down,
    gain_first,
    gain_second,
    cotangent,
):
    first, second, x_all, x_here, incoming = start(
        w_query,
        w_key,
        w_value,
        w_out.T,
        w_up,
        w_down.T,
        inputs[0],
        cotangent[0],
        gain_first[None],
        gain_second[None],
        clip_starts,
        pad_lengths[None],
    )
    first = first.reshape(D, -1)
    second = gather_weights(second.reshape(HD, -1))
    normed_one, normed_one_t, gains, facts, q, kv, incoming_all, o, lse, attended = project(
        x_all.reshape(512, D), first, incoming
    )
    mixed, middle, normed_two = mix(attended, first, x_here, gains)
    part_out, grad_up, grad_out, grad_middle, grad_mixed, gain_two, down_shard = feed(
        normed_two, incoming_all, middle, incoming, gains, first, second, mixed
    )
    grads, fed, up_shard = attend_back(facts, q, kv, o, lse, grad_mixed, part_out, grad_up)
    last, gain_grads, summed, grad_down, grad_up = end(
        grads, first, normed_one, normed_one_t, grad_out, gains, facts, gain_two, down_shard, up_shard
    )
    output, grad_input, *rest = finish(
        last, grad_down, grad_up, gain_grads, summed, x_here, grad_middle, gains, middle, fed
    )
    g_query, g_key, g_value, g_out, g_up, g_down, g_one, g_two = rest
    return (output[None], grad_input[None], g_query, g_key, g_value, g_out.T, g_up, g_down.T, g_one, g_two)


def solution(mesh):
    split = Mesh(mesh.devices.reshape(2, 4, 4, 2, 2), ("dp", "z", "y", "c", "mp"))
    seq = ("z", "y", "c")
    weights = ("dp", "z", "y", "c")
    tokens = P("dp", seq, None)
    wide, tall = P(weights, "mp"), P("mp", weights)
    return jax.shard_map(
        local,
        mesh=split,
        in_specs=(tokens, P("dp", None), P("dp"), wide, wide, wide, tall, wide, tall, P(weights), P(weights), tokens),
        out_specs=(tokens, tokens, wide, wide, wide, tall, wide, tall, P(weights), P(weights)),
        check_vma=False,
    )
```

```python
import functools

import jax
import jax.numpy as jnp
from jax import lax
from jax.experimental import pallas as pl
from jax.experimental.pallas import tpu as pltpu
from jax.sharding import Mesh
from jax.sharding import PartitionSpec as P

MESH = pl.DeviceIdType.MESH
HD = 128
FRAME = 32
LEN = 4096
D = 2048
ROWS = 128
BLOCK = 256
ZY = ("z", "y")
epsilon = 1e-05
scale = HD**-0.5
LOG_BASE = 9.210340371976184
f32 = jnp.float32
bf16 = jnp.bfloat16


def params(collective_id=None, vmem=48, **kw):
    if collective_id is not None:
        kw = dict(collective_id=collective_id, has_side_effects=True, **kw)
    return pltpu.CompilerParams(vmem_limit_bytes=vmem * 2**20, **kw)


def vmem_specs(n):
    return [pl.BlockSpec(memory_space=pltpu.VMEM)] * n


def greet(peers):
    barrier = pltpu.get_barrier_semaphore()
    for peer in peers:
        pl.semaphore_signal(barrier, inc=1, device_id=peer, device_id_type=MESH)
    pl.semaphore_wait(barrier, len(peers))


def remote(src, dst, send, recv, peer):
    return pltpu.make_async_remote_copy(
        src_ref=src, dst_ref=dst, send_sem=send, recv_sem=recv, device_id=peer, device_id_type=MESH
    )


def started(copies, src, dst, send, recv, peer):
    copy = remote(src, dst, send, recv, peer)
    copy.start()
    copies.append(copy)
    return copy


class Sems:
    def __init__(self, send, recv):
        self.send, self.recv, self.used = send, recv, 0

    def take(self):
        k = self.used
        self.used += 1
        return self.send.at[k], self.recv.at[k]


def sem_pair(n):
    return [pltpu.SemaphoreType.DMA((n,)), pltpu.SemaphoreType.DMA((n,))]


def tensor_place():
    d, c, m = lax.axis_index("dp"), lax.axis_index("c"), lax.axis_index("mp")
    return d, c, m, {"c": 1 - c}, {"dp": 1 - d, "mp": 1 - m}, {"mp": 1 - m}


def ring(axis, size=4):
    me = lax.axis_index(axis)
    up, down, far = (lax.rem(me + k, size) for k in (1, size - 1, 2))
    return me, up, down, far, {axis: up}, {axis: down}


def added(*values):
    total = values[0].astype(f32)
    for v in values[1:]:
        total = total + v.astype(f32)
    return total


def run(*protocols):
    live = list(protocols)
    while live:
        for p in list(live):
            try:
                next(p)
            except StopIteration:
                live.remove(p)


def swap_plan(pairs, sems):
    d, c = lax.axis_index("dp"), lax.axis_index("c")
    me = 2 * d + c
    copies = []
    for a, b in [(d, 1 - c), (1 - d, c), (1 - d, 1 - c)]:
        for src, dst in pairs:
            started(copies, src(2 * a + b), dst(me), *sems.take(), {"dp": a, "c": b})
    for src, dst in pairs:
        dst(me)[...] = src(me)[...]
    yield
    for copy in copies:
        copy.wait_recv()
    yield
    for copy in copies:
        copy.wait_send()


def quarter(ref):
    wide = ref.shape[1] // 4
    return lambda q: ref.at[:, pl.ds(pl.multiple_of(q * wide, wide), wide)]


def swap_peers():
    d, c = lax.axis_index("dp"), lax.axis_index("c")
    return [{"dp": 1 - d}, {"dp": 1 - d, "c": 1 - c}]


CHUNKS = 4
HALF = ROWS // 2


def rows_plan(x, o, sems):
    d, c, m, core, across, copy_of = tensor_place()
    me, far = 2 * d + c, 2 * (1 - d) + c
    copies, firsts, seconds = [], [], []
    step = HALF // 2
    mine = [pl.ds(m * HALF + k * step, step) for k in range(2)]
    other = [pl.ds((1 - m) * HALF + k * step, step) for k in range(2)]
    for rows in mine:
        firsts.append(started(copies, x.at[rows], o.at[me, rows], *sems.take(), across))
    near = started(copies, x, o.at[me], *sems.take(), core)
    o[me] = x[...]
    yield
    for k, rows in enumerate(other):
        firsts[k].wait_recv()
        seconds.append(started(copies, o.at[far, rows], o.at[far, rows], *sems.take(), copy_of))
    yield
    lasts = []
    for rows in other:
        lasts.append(started(copies, o.at[far, rows], o.at[far, rows], *sems.take(), core))
    for k, rows in enumerate(mine):
        seconds[k].wait_recv()
        lasts.append(started(copies, o.at[far, rows], o.at[far, rows], *sems.take(), core))
    yield
    near.wait_recv()
    for copy in lasts:
        copy.wait_recv()
    for copy in copies:
        copy.wait_send()


ROWS_SEMS = 9


def sum_plan(x, o, buffers, sems):
    from_core, s_here, s_send, from_across, t_send, from_copy = buffers
    d, c, m, core, across, copy_of = tensor_place()
    step = ROWS // CHUNKS
    rows = [pl.ds(k * step, step) for k in range(CHUNKS)]
    copies, zero, one, two = [], [], [], []
    for r in rows:
        zero.append(started(copies, x.at[:, 1 - c, r], from_core.at[:, r], *sems.take(), core))
    yield
    for k, r in enumerate(rows):
        zero[k].wait_recv()
        s_send[r] = added(x[1 - d, c, r], from_core[1 - d, r]).astype(bf16)
        one.append(started(copies, s_send.at[r], from_across.at[r], *sems.take(), across))
        s_here[r] = added(x[d, c, r], from_core[d, r])
    yield
    for k, r in enumerate(rows):
        one[k].wait_recv()
        t_send[r] = added(s_here[r], from_across[r]).astype(bf16)
        two.append(started(copies, t_send.at[r], from_copy.at[r], *sems.take(), copy_of))
    yield
    for k, r in enumerate(rows):
        two[k].wait_recv()
        o[r] = added(t_send[r], from_copy[r])
    for copy in copies:
        copy.wait_send()


SUM_SEMS = 3 * CHUNKS
SUM_BUFFERS = [
    pltpu.VMEM((2, ROWS, D), bf16),
    pltpu.VMEM((ROWS, D), f32),
    pltpu.VMEM((ROWS, D), bf16),
    pltpu.VMEM((ROWS, D), bf16),
    pltpu.VMEM((ROWS, D), bf16),
    pltpu.VMEM((ROWS, D), bf16),
]


def weights_plan(w, first, second, low, sems):
    i0, i_up, i_down, i_far, to_i_up, to_i_down = ring(first)
    j0, j_up, j_down, j_far, to_j_up, to_j_down = ring(second)

    def at(i, j, part, n):
        return w.at[(j, i) if first == "y" else (i, j)].at[pl.ds(low + part, n)]

    copies = []

    def send(ref, peer):
        return started(copies, ref, ref, *sems.take(), peer)

    def along(i):
        return i, send(at(i, j0, 0, 2), to_j_up), send(at(i, j0, 0, 2), to_j_down)

    from_down, from_up = send(at(i0, j0, 0, 2), to_i_up), send(at(i0, j0, 0, 2), to_i_down)
    second_leg = [along(i0)]
    yield
    from_down.wait_recv()
    far_low = send(at(i_down, j0, 0, 1), to_i_up)
    from_up.wait_recv()
    far_high = send(at(i_up, j0, 1, 1), to_i_down)
    second_leg.append(along(i_down))
    yield
    second_leg.append(along(i_up))
    yield
    onward = []

    def relay(leg):
        i, a, b = leg
        a.wait_recv()
        onward.append(send(at(i, j_down, 0, 1), to_j_up))
        b.wait_recv()
        onward.append(send(at(i, j_up, 1, 1), to_j_down))

    relay(second_leg[0])
    yield
    far_low.wait_recv()
    far_high.wait_recv()
    second_leg.append(along(i_far))
    for leg in second_leg[1:]:
        yield
        relay(leg)
    yield
    for copy in onward:
        copy.wait_recv()
    for copy in copies:
        copy.wait_send()


WEIGHT_SEMS = 20


def to_inner(x, o):
    for k in range(16):
        low, high = x[:, k * 64 : (k + 1) * 64], x[:, D // 2 + k * 64 : D // 2 + (k + 1) * 64]
        o[:, k * HD : (k + 1) * HD] = jnp.concatenate([low, high], 1)


def to_outer(x, o, kind):
    for k in range(0, 16, 2):
        one, two = x(k), x(k + 1)
        o[:, k * 64 : k * 64 + HD] = jnp.concatenate([one[:, :64], two[:, :64]], 1).astype(kind)
        o[:, D // 2 + k * 64 : D // 2 + k * 64 + HD] = jnp.concatenate([one[:, 64:], two[:, 64:]], 1).astype(kind)


def side_of(one, two, starts, padding):
    lane = lax.broadcasted_iota(jnp.int32, (32, HD), 1)
    same = lax.broadcasted_iota(jnp.int32, (32, 32), 0) == lax.broadcasted_iota(jnp.int32, (32, 32), 1)

    def column(row):
        return jnp.sum(jnp.where(same, row[...].astype(f32), 0.0), 1, keepdims=True)

    value = jnp.where(lane == 0, column(one), 0.0)
    value = jnp.where(lane == 1, column(two), value)
    for k in range(3):
        value = jnp.where(lane == 2 + k, starts[:, k : k + 1].astype(f32), value)
    return jnp.where(lane == 5, padding[...].astype(f32), value).astype(bf16)


def spread_plan(x, q, kv, sems):
    z, z_up, z_down, z_far, to_z_up, to_z_down = ring("z")
    y, y_up, y_down, y_far, to_y_up, to_y_down = ring("y")
    far = {"z": z_far}
    copies, firsts, queries, nears, fars = [], [], [], [], []
    both = pl.ds(1, 2)
    peers = [(z_up, to_z_up, z_down), (z_down, to_z_down, z_up), (z_far, far, z_far)]
    for place, peer, _ in peers:
        firsts.append(started(copies, x.at[place, both], kv.at[z, y], *sems.take(), peer))
    kv[z, y] = x[z, both]

    def along(place):
        ref = kv.at[place, y]
        nears.append(
            (place, started(copies, ref, ref, *sems.take(), to_y_up), started(copies, ref, ref, *sems.take(), to_y_down))
        )

    along(z)
    for place, peer, _ in peers:
        queries.append(started(copies, x.at[place, 0], q.at[z], *sems.take(), peer))
    q[z] = x[z, 0]
    yield
    for k, (_, _, source) in enumerate(peers):
        firsts[k].wait_recv()
        along(source)
        yield
    for copy in queries:
        copy.wait_recv()
    yield
    for place, a, b in nears:
        a.wait_recv()
        ref = kv.at[place, y_down, 0]
        fars.append(started(copies, ref, ref, *sems.take(), to_y_up))
        b.wait_recv()
        ref = kv.at[place, y_up, 1]
        fars.append(started(copies, ref, ref, *sems.take(), to_y_down))
        yield
    for copy in fars:
        copy.wait_recv()
    yield
    for copy in copies:
        copy.wait_send()


def ring_sum(at, axis, buffers, sems, put, late=False):
    one, two, passed = buffers
    me, up, down, far, to_up, to_down = ring(axis)
    copies = []
    a = started(copies, at(far, 0), one.at[0], *sems.take(), to_up)
    b = started(copies, at(far, 1), one.at[1], *sems.take(), to_down)
    if late:
        yield
    plain = [started(copies, at(up, 1), two.at[0, 1], *sems.take(), to_up)]
    if not late:
        plain.append(started(copies, at(down, 0), two.at[1, 0], *sems.take(), to_down))
        yield
    a.wait_recv()
    passed[0] = added(at(up, 0)[...], one[0]).astype(bf16)
    plain.append(started(copies, passed.at[0], two.at[0, 0], *sems.take(), to_up))
    if late:
        yield
        plain.append(started(copies, at(down, 0), two.at[1, 0], *sems.take(), to_down))
    b.wait_recv()
    passed[1] = added(at(down, 1)[...], one[1]).astype(bf16)
    plain.append(started(copies, passed.at[1], two.at[1, 1], *sems.take(), to_down))
    yield
    for copy in plain:
        copy.wait_recv()
    for part in range(2):
        put(part, added(at(me, part)[...], two[0, part], two[1, part]))
    yield
    for copy in copies:
        copy.wait_send()


RING_SEMS = 6


def ring_buffers(n, part):
    return [pltpu.VMEM((n, 2, *part), bf16), pltpu.VMEM((n, 2, 2, *part), bf16), pltpu.VMEM((n, 2, *part), bf16)]


def collect_plan(dq, dkv, o, total, buffers, sems):
    z, peers = z_peers()
    peers = peers + [(z, None)]
    copies, rings = [], []
    for k, (place, peer) in enumerate(peers):

        def at(i, part, place=place):
            return dkv.at[place, i, part]

        def put(part, value, k=k):
            if k < 3:
                total[k, part] = value.astype(bf16)
            else:
                o[z, 1 + part] = value.astype(bf16)

        rings.append(ring_sum(at, "y", [b.at[k] for b in buffers], sems, put, True))
    for _ in range(3):
        for r in rings:
            next(r)
        yield
    for place, peer in peers[:3]:
        started(copies, dq.at[place], o.at[z, 0], *sems.take(), peer)
    o[z, 0] = dq[z]
    for k, r in enumerate(rings):
        next(r)
        if k < 3:
            started(copies, total.at[k], o.at[z, pl.ds(1, 2)], *sems.take(), peers[k][1])
    yield
    for copy in copies:
        copy.wait()
    run(*rings)


def grads_plan(g, shard, first, second, low, legs, buffers, sems, late=False):
    rings = []
    for j in range(4):

        def at(i, part, j=j):
            z, y = (j, i) if first == "y" else (i, j)
            return g.at[pl.ds(pl.multiple_of(((4 * z + y) * 4 + low + part) * 32, 32), 32)]

        def put(part, value, j=j):
            legs[j, part] = value.astype(bf16)

        rings.append(ring_sum(at, first, [b.at[j] for b in buffers], sems, put, late))
    for _ in range(4 if late else 3):
        for r in rings:
            next(r)
        yield

    def put_last(part, value):
        shard[low + part] = value.astype(bf16)

    rings.append(ring_sum(lambda i, part: legs.at[i, part], second, [b.at[4] for b in buffers], sems, put_last))
    for _ in range(3):
        next(rings[-1])
        yield
    run(*rings)


def reach(facts, block, rows):
    t = block * rows + lax.broadcasted_iota(jnp.int32, (rows, 1), 0)
    one, two, three, padding = (facts[:, k : k + 1].astype(jnp.int32) for k in range(2, 6))
    begin = jnp.where(t >= three, three, jnp.where(t >= two, two, one))
    living = t < LEN - padding
    end = jnp.minimum((t // FRAME + 1) * FRAME, LEN - padding)
    return t, begin, jnp.where(living, begin, t), jnp.where(living, end, t + 1)


def dot_t(a, b):
    return lax.dot_general(a, b, (((1,), (1,)), ((), ())), preferred_element_type=f32)


def dot_l(a, b):
    return lax.dot_general(a, b, (((0,), (0,)), ((), ())), preferred_element_type=f32)


def column_scores(facts, q, kv, i, column):
    n = (i + 1) * BLOCK
    _, _, low, high = reach(facts[pl.ds(lax.axis_index("z") // 2, 1)], 4 * i + lax.axis_index("y"), BLOCK)
    k = kv[0 : i + 1, column, 0].reshape(n, HD)
    at = lax.broadcasted_iota(jnp.int32, (1, n), 1)
    at = (at // BLOCK) * (4 * BLOCK) + at % BLOCK + column * BLOCK
    return k, jnp.where((at >= low) & (at < high), dot_t(q[i], k) * scale, -1e30)


def attend_tile(facts, q, kv, top, total, acc, i, column, first):
    _, s = column_scores(facts, q, kv, i, column)
    v = kv[0 : i + 1, column, 1].reshape((i + 1) * BLOCK, HD)
    now = jnp.max(s, -1, keepdims=True)
    if not first:
        before = top[i][:, :1]
        now = jnp.maximum(before, now)
    p = jnp.exp(s - now)
    plus = jnp.sum(p, -1, keepdims=True)
    out = jnp.dot(p.astype(bf16), v, preferred_element_type=f32)
    if not first:
        shrink = jnp.exp(before - now)
        plus = plus + total[i][:, :1] * shrink
        out = out + acc[i] * shrink
    top[i] = jnp.broadcast_to(now, (BLOCK, HD))
    total[i] = jnp.broadcast_to(plus, (BLOCK, HD))
    acc[i] = out


def attend_back_tile(facts, q, kv, do, lse, inner, dq, acc, i, column, first):
    k, s = column_scores(facts, q, kv, i, column)
    n = i + 1
    v = kv[0:n, column, 1].reshape(n * BLOCK, HD)
    p = jnp.exp(s - lse[i][:, :1])
    ds = (p * (dot_t(do[i], v) - inner[i][:, :1])).astype(bf16)
    dv = dot_l(p.astype(bf16), do[i]).reshape(n, BLOCK, HD)
    dk = dot_l(ds, q[i]).reshape(n, BLOCK, HD)
    part = jnp.dot(ds, k, preferred_element_type=f32)
    if i == 3:
        acc[:, 0], acc[:, 1] = dk, dv
    else:
        acc[0:n, 0] += dk
        acc[0:n, 1] += dv
    dq[i] = part if first else dq[i] + part


def attend_back_kernel(
    facts, q, kv, o, lse, do, part, grads_up, out, summed, shard, acc, dq, dq_low, dkv, inner, total, *scratch
):
    _, _, _, z_far, z_up, z_down = ring("z")
    y, up, down, far, y_up, y_down = ring("y")
    greet([*tensor_place()[3:], z_up, z_down, {"z": z_far}, y_up, y_down])
    fed = sum_plan(part, summed, scratch[5:11], Sems(*scratch[11:13]))
    legs = [
        grads_plan(grads_up, shard, "z", "y", 0, scratch[13], scratch[15:18], Sems(*scratch[21:23])),
        grads_plan(grads_up, shard, "y", "z", 2, scratch[14], scratch[18:21], Sems(*scratch[23:25])),
    ]
    for leg in legs:
        next(leg)
    grads = collect_plan(dq_low, dkv, out, total, scratch[:3], Sems(*scratch[3:5]))
    next(fed)
    for i in range(4):
        value = jnp.sum(o[i] * do[i].astype(f32), -1, keepdims=True)
        inner[i] = jnp.broadcast_to(value, (BLOCK, HD))
    for column in (far, up, down, y):
        for i in (3, 2, 1, 0):
            attend_back_tile(facts, q, kv, do, lse, inner, dq, acc, i, column, column is far)
            if i == 2 and column is not far:
                for leg in legs:
                    next(leg)
        for k in range(4):
            dkv[k, column, 0] = (acc[k, 0] * scale).astype(bf16)
            dkv[k, column, 1] = acc[k, 1].astype(bf16)
        if column is y:
            dq_low[...] = (dq[...] * scale).astype(bf16)
        next(grads)
        next(fed, None)
    run(grads, fed, *legs)


def attend_back(facts, q, kv, o, lse, do, part, grads_up):
    return pl.pallas_call(
        attend_back_kernel,
        out_shape=[
            jax.ShapeDtypeStruct((4, 3, BLOCK, HD), bf16),
            jax.ShapeDtypeStruct((ROWS, D), f32),
            jax.ShapeDtypeStruct((4, 32, 1024), bf16),
        ],
        in_specs=vmem_specs(8),
        out_specs=vmem_specs(3),
        scratch_shapes=[
            pltpu.VMEM((4, 2, BLOCK, HD), f32),
            pltpu.VMEM((4, BLOCK, HD), f32),
            pltpu.VMEM((4, BLOCK, HD), bf16),
            pltpu.VMEM((4, 4, 2, BLOCK, HD), bf16),
            pltpu.VMEM((4, BLOCK, HD), f32),
            pltpu.VMEM((3, 2, BLOCK, HD), bf16),
        ]
        + ring_buffers(4, (BLOCK, HD))
        + sem_pair(4 * RING_SEMS + 6)
        + SUM_BUFFERS
        + sem_pair(SUM_SEMS)
        + [pltpu.VMEM((4, 2, 32, 1024), bf16)] * 2
        + ring_buffers(5, (32, 1024)) * 2
        + sem_pair(5 * RING_SEMS) * 2,
        compiler_params=params(6, vmem=56),
        name="attend_back",
    )(facts, q, kv, o, lse, do, part, grads_up)


def norm(value):
    centre = value - jnp.mean(value, -1, keepdims=True)
    r = lax.rsqrt(jnp.mean(centre * centre, -1, keepdims=True) + epsilon)
    return centre * r, r


def norm_back(grad, n, r, gain):
    e = grad * gain
    return r * (e - jnp.mean(e, -1, keepdims=True) - n * jnp.mean(e * n, -1, keepdims=True))


def one_hot(rows, places):
    at = lax.broadcasted_iota(jnp.int32, (rows, HD), 0)
    lane = lax.broadcasted_iota(jnp.int32, (rows, HD), 1)
    hot = at < 0
    for k, place in enumerate(places):
        hot = hot | ((at == k) & (lane == place))
    return jnp.where(hot, 1.0, 0.0).astype(bf16)


def tables(facts, c):
    block = (4 * lax.axis_index("z") + lax.axis_index("y")) * 2 + c
    t, begin, _, _ = reach(facts, block, ROWS)
    lane = lax.broadcasted_iota(jnp.int32, (1, HD), 1)
    i = jnp.where(lane < HD // 2, lane, lane - HD // 2).astype(f32)
    angles = (t - begin).astype(f32) * jnp.exp(i * (-2.0 * LOG_BASE / HD))
    return jnp.cos(angles), jnp.where(lane < HD // 2, -1.0, 1.0) * jnp.sin(angles)


def sum_norm_plan(x, produce, all_rows, make, buffers, sems, idle=lambda: None):
    from_core, s_here, s_send, from_across, t_send, from_copy = buffers
    d, c, m, core, across, copy_of = tensor_place()
    me, far = 2 * d + c, 2 * (1 - d) + c
    step = ROWS // CHUNKS
    rows = [pl.ds(k * step, step) for k in range(CHUNKS)]
    copies, zero, one, two = [], [], [], []
    for h in range(2):
        produce(h)
        for r in rows[2 * h : 2 * h + 2]:
            zero.append(started(copies, x.at[:, 1 - c, r], from_core.at[:, r], *sems.take(), core))
        for k in range(2 * h, 2 * h + 2):
            r = rows[k]
            zero[k].wait_recv()
            s_send[r] = added(x[1 - d, c, r], from_core[1 - d, r]).astype(bf16)
            one.append(started(copies, s_send.at[r], from_across.at[r], *sems.take(), across))
            s_here[r] = added(x[d, c, r], from_core[d, r])
    idle()
    for k, r in enumerate(rows):
        idle()
        one[k].wait_recv()
        t_send[r] = added(s_here[r], from_across[r]).astype(bf16)
        two.append(started(copies, t_send.at[r], from_copy.at[r], *sems.take(), copy_of))
    yield
    nears, firsts, seconds, lasts = [], [], [], []
    idle()
    for k, r in enumerate(rows):
        idle()
        two[k].wait_recv()
        all_rows[me, r] = make(r, added(t_send[r], from_copy[r])).astype(bf16)
        nears.append(started(copies, all_rows.at[me, r], all_rows.at[me, r], *sems.take(), core))
        half = pl.ds(pl.multiple_of(k * step + m * (step // 2), step // 2), step // 2)
        firsts.append(started(copies, all_rows.at[me, half], all_rows.at[me, half], *sems.take(), across))
    yield

    def onward(half, peer):
        return started(copies, all_rows.at[far, half], all_rows.at[far, half], *sems.take(), peer)

    idle()
    for k in range(CHUNKS):
        idle()
        firsts[k].wait_recv()
        half = pl.ds(pl.multiple_of(k * step + (1 - m) * (step // 2), step // 2), step // 2)
        seconds.append(onward(half, copy_of))
        lasts.append(onward(half, core))
    yield
    idle()
    for k in range(CHUNKS):
        idle()
        seconds[k].wait_recv()
        half = pl.ds(pl.multiple_of(k * step + m * (step // 2), step // 2), step // 2)
        lasts.append(onward(half, core))
    yield
    for copy in nears + lasts:
        copy.wait_recv()
    yield
    for copy in copies:
        copy.wait_send()


SUM_NORM_SEMS = 8 * CHUNKS
OUT_COLUMNS = pl.BlockSpec((D, 256), lambda i: (0, 3))


def z_peers():
    z, z_up, z_down, z_far, to_z_up, to_z_down = ring("z")
    return z, [(z_up, to_z_up), (z_down, to_z_down), (z_far, {"z": z_far})]


def front_kernel(
    wq,
    wk,
    wv,
    wo,
    wu,
    wd,
    x_hbm,
    cot_hbm,
    one,
    two,
    starts,
    padding,
    w_hbm,
    x_here,
    cot,
    tabs,
    n1,
    n1_t,
    gains,
    facts,
    q,
    kv,
    rows,
    o,
    lse,
    mixed,
    middle,
    n2,
    weights_hbm,
    *scratch,
):
    w, weights, qkv, top, total, acc, low, turned, part, x_raw, cot_raw, side, x = scratch[:13]
    sums, scratch = scratch[13:19], scratch[19:]
    local = scratch[0]
    sems = [Sems(*scratch[1 + 2 * k : 3 + 2 * k]) for k in range(10)]
    keys_sems, rows_sems, norm_sems, turn_sems, leg_a, leg_b, swaps, x_sems, first_a, first_b = sems
    d, c = lax.axis_index("dp"), lax.axis_index("c")
    me = 2 * d + c
    z, peers = z_peers()
    y, up, down, far, y_up, y_down = ring("y")
    here, there = w.at[z, y, me], weights.at[z, y, me]
    firsts = [(wq, 0, 256), (wk, 256, 256), (wv, 512, 256), (wo, 768, 256)]
    rests = [(wu, 0, 1024), (wd, 1024, 1024)]
    loads = [pltpu.make_async_copy(x_hbm, x_raw, local.at[0]), pltpu.make_async_copy(cot_hbm, cot_raw, local.at[1])]
    for k, (src, left, n) in enumerate(firsts):
        loads.append(pltpu.make_async_copy(quarter(src)(me), here.at[:, pl.ds(left, n)], local.at[2 + k]))
    for k, (src, left, n) in enumerate(rests):
        loads.append(pltpu.make_async_copy(quarter(src)(me), there.at[:, pl.ds(left, n)], local.at[6 + k]))
    for copy in loads:
        copy.start()
    side[...] = side_of(one, two, starts, padding)
    here[:, 1024:1152] = side[...]
    greet([*tensor_place()[3:], *swap_peers(), *[peer for _, peer in peers], y_up, y_down])

    def swap(pairs, dst):
        copies = []
        for a, b in [(d, 1 - c), (1 - d, c), (1 - d, 1 - c)]:
            for src, left, n in pairs:
                started(copies, src(2 * a + b), dst.at[:, pl.ds(left, n)], *swaps.take(), {"dp": a, "c": b})
        return copies

    swap_first = swap([(quarter(src), left, n) for src, left, n in firsts] + [(lambda q: side, 1024, HD)], here)
    loads[0].wait()
    to_inner(x_raw, x_here)
    gather_x = rows_plan(x_here, x, x_sems)
    next(gather_x)
    for copy in loads[2:6]:
        copy.wait()
    for copy in swap_first:
        copy.wait_recv()
    legs = [weights_plan(w, "y", "z", 0, first_a), weights_plan(w, "z", "y", 2, first_b)]
    for leg in legs:
        next(leg)
    swap_rest = swap([(quarter(src), left, n) for src, left, n in rests], there)
    for seq in range(2):
        fact = w[z, y, 2 * seq, 0:1, 1024:1152].astype(f32)
        for half in range(2):
            tabs[0, 2 * seq + half], tabs[1, 2 * seq + half] = tables(fact, half)
    loads[1].wait()
    to_inner(cot_raw, cot)
    run(*legs, gather_x)
    store = pltpu.make_async_copy(w, w_hbm, local.at[8])
    store.start()
    for copy in loads[6:] + swap_rest:
        copy.wait()
    for copy in swap_first:
        copy.wait_send()

    def columns(left, right):
        return w[:, :, :, :, left:right].reshape(D, right - left)

    gather = rows_plan(cot, rows, rows_sems)
    next(gather)
    legs = [weights_plan(weights, "y", "z", 0, leg_a), weights_plan(weights, "z", "y", 2, leg_b)]

    def leg_step():
        for leg in legs:
            next(leg, None)

    leg_step()
    side = columns(1024, 1152)
    gains[...] = dot_t(one_hot(8, (0, 1)), side)
    facts[...] = jnp.zeros_like(facts)
    facts[0:1] = side[0:1].astype(f32)
    facts[1:2] = side[64:65].astype(f32)
    for block in range(4):
        seq, half = block // 2, block % 2
        r = pl.ds(block * ROWS, ROWS)
        n, _ = norm(x[block].astype(f32))
        n1[r] = (n * gains[0:1]).astype(bf16)
        lin = jnp.dot(n1[r], columns(0, 768), preferred_element_type=f32)
        for kind in range(3):
            for h in range(2):
                v = lin[:, (2 * kind + h) * HD : (2 * kind + h + 1) * HD]
                if kind < 2:
                    v = v * tabs[0, block] + pltpu.roll(v, HD // 2, 1) * tabs[1, block]
                qkv[2 * seq + h, kind, half * ROWS : (half + 1) * ROWS] = v.astype(bf16)
    keys = spread_plan(qkv, q, kv, keys_sems)

    def work():
        for k in range(4):
            some = slice(512 * k, 512 * (k + 1))
            n1_t[some] = n1[:, some].T
            yield
        for i in range(4):
            attend_tile(facts, q, kv, top, total, acc, i, y, True)
            yield

    pieces = work()
    next(keys)
    next(gather)
    for _ in range(4):
        next(pieces)
        next(keys)
    next(gather)
    for _ in range(4):
        next(pieces)
        next(keys)
    next(gather, None)
    leg_step()
    for column in (down, up):
        for i in range(4):
            attend_tile(facts, q, kv, top, total, acc, i, column, False)
    run(keys, gather)
    for i in range(4):
        attend_tile(facts, q, kv, top, total, acc, i, far, False)
    for i in range(4):
        low[i] = (acc[i] / total[i]).astype(bf16)
    copies = []
    for place, peer in peers:
        started(copies, low.at[place], turned.at[z], *turn_sems.take(), peer)
    turned[z] = low[z]
    for i in range(4):
        o[i] = acc[i] / total[i]
        lse[i] = top[i] + jnp.log(total[i])
    leg_step()
    for copy in copies:
        copy.wait()
    for seq in range(2):
        for h in range(2):
            mixed[seq, :, :, h * HD : (h + 1) * HD] = turned[2 * seq + h].reshape(2, ROWS, HD)

    def partial(h):
        r = slice(HALF * h, HALF * (h + 1))
        value = dot_t(mixed[:, :, r].reshape(2 * ROWS, 256), columns(768, 1024))
        part[:, :, r] = value.astype(bf16).reshape(2, 2, HALF, D)

    def make(r, value):
        value = x_here[r].astype(f32) + value
        middle[r] = value
        return norm(value)[0] * gains[1:2]

    def legs_work():
        for _ in range(5):
            for _ in range(2):
                yield
            leg_step()
            yield
        run(*legs)
        pltpu.make_async_copy(weights, weights_hbm, local.at[9]).start()
        yield

    rest = legs_work()
    run(sum_norm_plan(part, partial, n2, make, sums, norm_sems, lambda: next(rest, None)))
    for _ in rest:
        pass
    pltpu.make_async_copy(weights, weights_hbm, local.at[9]).wait()
    store.wait()


def front(*args):
    block = (4, BLOCK, HD)
    shape = jax.ShapeDtypeStruct
    anywhere = pl.BlockSpec(memory_space=pl.ANY)
    whole = lambda *dims: pl.BlockSpec(dims, lambda i: (0,) * len(dims))
    first, second = (4, 4, 4, 32, 1152), (4, 4, 4, 32, 2048)
    return pl.pallas_call(
        front_kernel,
        grid=(1,),
        out_shape=[
            shape(first, bf16),
            shape((ROWS, D), bf16),
            shape((ROWS, D), bf16),
            shape((2, 4, ROWS, HD), f32),
            shape((512, D), bf16),
            shape((D, 512), bf16),
            shape((8, D), f32),
            shape((8, HD), f32),
            shape(block, bf16),
            shape((4, 4, 2, BLOCK, HD), bf16),
            shape((4, ROWS, D), bf16),
            shape(block, f32),
            shape(block, f32),
            shape((2, 2, ROWS, 256), bf16),
            shape((ROWS, D), f32),
            shape((4, ROWS, D), bf16),
            shape(second, bf16),
        ],
        in_specs=[anywhere] * 8 + [whole(1, 32), whole(1, 32), whole(1, 3), whole(1, 1)],
        out_specs=[anywhere] + vmem_specs(15) + [anywhere],
        scratch_shapes=[
            pltpu.VMEM(first, bf16),
            pltpu.VMEM(second, bf16),
            pltpu.VMEM((4, 3, BLOCK, HD), bf16),
        ]
        + [pltpu.VMEM(block, f32)] * 3
        + [pltpu.VMEM(block, bf16)] * 2
        + [pltpu.VMEM((2, 2, ROWS, D), bf16)]
        + [pltpu.VMEM((ROWS, D), bf16)] * 2
        + [pltpu.VMEM((32, HD), bf16), pltpu.VMEM((4, ROWS, D), bf16)]
        + SUM_BUFFERS
        + [pltpu.SemaphoreType.DMA((10,))]
        + sem_pair(22)
        + sem_pair(ROWS_SEMS)
        + sem_pair(SUM_NORM_SEMS)
        + sem_pair(3)
        + sem_pair(WEIGHT_SEMS) * 2
        + sem_pair(21)
        + sem_pair(ROWS_SEMS)
        + sem_pair(WEIGHT_SEMS) * 2,
        compiler_params=params(4, vmem=60),
        name="front",
    )(*args)


def feed_kernel(
    n2,
    cot_all,
    middle,
    cot,
    gains,
    w,
    weights,
    mixed,
    fed,
    grads_up,
    grad_out,
    grad_middle,
    turned,
    gain_two,
    shard,
    up,
    down,
    n2_t,
    cot_t,
    grads_down,
    branch,
    active,
    grad_hidden,
    part,
    grad_mixed,
    *scratch,
):
    z, peers = z_peers()
    local = scratch[10]
    _, _, _, _, z_up, z_down = ring("z")
    _, _, _, _, y_up, y_down = ring("y")
    loads = [
        pltpu.make_async_copy(weights.at[:, pl.ds(1024, 1024)], down, local.at[0]),
        pltpu.make_async_copy(weights.at[:, pl.ds(0, 1024)], up, local.at[1]),
    ]
    for copy in loads:
        copy.start()
    gain_two[...] = jnp.zeros_like(gain_two)
    greet([*tensor_place()[3:], *[peer for _, peer in peers], y_up, y_down])
    for copy in loads:
        copy.wait()

    def partial(h):
        rows = slice(HALF * h, HALF * (h + 1))
        n = n2[:, :, rows].reshape(2 * ROWS, D)
        g = cot_all[:, :, rows].reshape(2 * ROWS, D)
        for j in range(4):
            some = slice(256 * j, 256 * (j + 1))
            grad_active = jnp.dot(g, down[:, some], preferred_element_type=f32)
            hidden = jnp.dot(n, up[:, some], preferred_element_type=f32)
            half = 0.5 * (1.0 + lax.erf(hidden * 0.5**0.5))
            slope = half + hidden * jnp.exp(-0.5 * hidden * hidden) * (0.5 / jnp.pi) ** 0.5
            active[:, :, rows, some] = (hidden * half).astype(bf16).reshape(2, 2, HALF, 256)
            grad_hidden[:, :, rows, some] = (grad_active * slope).astype(bf16).reshape(2, 2, HALF, 256)
        value = grad_hidden[:, :, rows].reshape(2 * ROWS, 1024)
        for k in range(4):
            some = slice(512 * k, 512 * (k + 1))
            part[:, :, rows, some] = dot_t(value, up[some]).astype(bf16).reshape(2, 2, HALF, 512)

    legs = [
        grads_plan(grads_down, shard, "z", "y", 0, scratch[11], scratch[13:16], Sems(*scratch[19:21])),
        grads_plan(grads_down, shard, "y", "z", 2, scratch[12], scratch[16:19], Sems(*scratch[21:23])),
    ]

    def turn_cot(k):
        some = slice(512 * k, 512 * (k + 1))
        cot_t[some] = cot_all[:, :, :, some].reshape(512, 512).T

    def turn_n2(k):
        some = slice(512 * k, 512 * (k + 1))
        n2_t[some] = n2[:, :, :, some].reshape(512, 512).T

    def down_piece(j):
        some = slice(256 * j, 256 * (j + 1))
        value = active[:, :, :, some].reshape(512, 256)
        grads_down[:, some] = jnp.dot(cot_t[...], value, preferred_element_type=f32).astype(bf16)

    def up_piece(j):
        some = slice(256 * j, 256 * (j + 1))
        value = grad_hidden[:, :, :, some].reshape(512, 256)
        grads_up[:, some] = jnp.dot(n2_t[...], value, preferred_element_type=f32).astype(bf16)

    def fed_piece(k):
        some = slice(512 * k, 512 * (k + 1))
        value = dot_t(active[...].reshape(512, 1024), down[some])
        fed[:, :, :, some] = value.astype(bf16).reshape(2, 2, ROWS, 512)

    def leg_step():
        for leg in legs:
            next(leg, None)

    def work():
        for k in range(2):
            turn_cot(2 * k)
            turn_cot(2 * k + 1)
            yield
        for k in range(2):
            down_piece(2 * k)
            down_piece(2 * k + 1)
            if k:
                leg_step()
            yield
        for k in range(4):
            turn_n2(k)
        yield
        for j in range(4):
            up_piece(j)
            yield
        leg_step()
        yield
        for k in range(4):
            fed_piece(k)
            yield
        leg_step()
        yield

    pieces = work()

    def make(r, total):
        n, rate = norm(middle[r])
        gain_two[0:1] += 0.5 * jnp.sum(total * n, 0, keepdims=True)
        value = cot[r].astype(f32) + norm_back(total, n, rate, gains[1:2])
        grad_middle[r] = value
        return value

    run(sum_norm_plan(part, partial, branch, make, scratch[:6], Sems(*scratch[6:8]), lambda: next(pieces, None)))
    for k in range(4):
        value = jnp.dot(branch[k], w[...], preferred_element_type=f32).astype(bf16)
        for h in range(2):
            grad_mixed[2 * (k // 2) + h, (k % 2) * ROWS : (k % 2 + 1) * ROWS] = value[:, h * HD : (h + 1) * HD]
    turns, copies = Sems(*scratch[8:10]), []
    for place, peer in peers:
        started(copies, grad_mixed.at[place], turned.at[z], *turns.take(), peer)
    turned[z] = grad_mixed[z]
    for _ in pieces:
        pass
    leg_step()
    for k in range(4):
        some = slice(512 * k, 512 * (k + 1))
        grad_out[some] = dot_l(branch[:, :, some].reshape(512, 512), mixed[...]).astype(bf16)
    for copy in copies:
        copy.wait()
    run(*legs)


def feed(n2, cot_all, middle, cot, gains, first, weights, mixed):
    whole = lambda *shape: pl.BlockSpec(shape, lambda i: (0,) * len(shape))
    anywhere = pl.BlockSpec(memory_space=pl.ANY)
    rows = (2, 2, ROWS, D)
    return pl.pallas_call(
        feed_kernel,
        grid=(1,),
        out_shape=[
            jax.ShapeDtypeStruct(rows, bf16),
            jax.ShapeDtypeStruct((D, 1024), bf16),
            jax.ShapeDtypeStruct((D, 256), bf16),
            jax.ShapeDtypeStruct((ROWS, D), f32),
            jax.ShapeDtypeStruct((4, BLOCK, HD), bf16),
            jax.ShapeDtypeStruct((8, D), f32),
            jax.ShapeDtypeStruct((4, 32, 1024), bf16),
        ],
        in_specs=vmem_specs(5) + [OUT_COLUMNS, anywhere] + vmem_specs(1),
        out_specs=vmem_specs(7),
        scratch_shapes=[
            pltpu.VMEM((D, 1024), bf16),
            pltpu.VMEM((D, 1024), bf16),
            pltpu.VMEM((D, 512), bf16),
            pltpu.VMEM((D, 512), bf16),
            pltpu.VMEM((D, 1024), bf16),
            pltpu.VMEM((4, ROWS, D), bf16),
            pltpu.VMEM((2, 2, ROWS, 1024), bf16),
            pltpu.VMEM((2, 2, ROWS, 1024), bf16),
            pltpu.VMEM(rows, bf16),
            pltpu.VMEM((4, BLOCK, HD), bf16),
        ]
        + SUM_BUFFERS
        + sem_pair(SUM_NORM_SEMS)
        + sem_pair(3)
        + [pltpu.SemaphoreType.DMA((2,))]
        + [pltpu.VMEM((4, 2, 32, 1024), bf16)] * 2
        + ring_buffers(5, (32, 1024)) * 2
        + sem_pair(5 * RING_SEMS) * 2,
        compiler_params=params(2, vmem=60),
        name="feed",
    )(n2.reshape(rows), cot_all.reshape(rows), middle, cot, gains, first, weights, mixed)


def end_kernel(
    grads, w_hbm, n1, n1_t, grad_out, gains, tabs, gain_two, down, up, o, gain, summed, down_all, up_all, *scratch
):
    w, lin, last, side, part, shard, side_shard, side_all, mine, theirs = scratch[:10]
    legs_a, legs_b, side_a, side_b = scratch[10:14]
    rings = [scratch[14 + 3 * k : 17 + 3 * k] for k in range(4)]
    sums = scratch[26:32]
    sems = [Sems(*scratch[32 + 2 * k : 34 + 2 * k]) for k in range(7)]
    load = pltpu.make_async_copy(w_hbm, w, scratch[46].at[0])
    load.start()
    d, c, m, core, across, copy_of = tensor_place()
    _, _, _, _, z_up, z_down = ring("z")
    _, _, _, _, y_up, y_down = ring("y")
    greet([core, across, copy_of, *swap_peers(), z_up, z_down, y_up, y_down])
    swap_feed = swap_plan(
        [(lambda q: down.at[q], lambda me: down_all.at[me]), (lambda q: up.at[q], lambda me: up_all.at[me])], sems[0]
    )
    next(swap_feed)
    for seq in range(2):
        for half in range(2):
            rows = pl.ds((2 * seq + half) * ROWS, ROWS)
            cosine, sine = tabs[0, 2 * seq + half], tabs[1, 2 * seq + half]
            for kind in range(3):
                for h in range(2):
                    v = grads[2 * seq + h, kind, half * ROWS : (half + 1) * ROWS]
                    if kind < 2:
                        v = v.astype(f32)
                        v = (v * cosine - pltpu.roll(v, HD // 2, 1) * sine).astype(bf16)
                    lin[rows, (2 * kind + h) * HD : (2 * kind + h + 1) * HD] = v
    blocks = [slice(512 * k, 512 * (k + 1)) for k in range(4)]
    for some in blocks:
        last[some, 0:768] = jnp.dot(n1_t[some], lin[...], preferred_element_type=f32).astype(bf16)
        last[some, 768:1024] = grad_out[some]
    legs = [
        grads_plan(last, shard, "z", "y", 0, legs_a, rings[0], sems[1], True),
        grads_plan(last, shard, "y", "z", 2, legs_b, rings[1], sems[2], True),
    ]
    for leg in legs:
        next(leg)
    load.wait()
    hot = one_hot(8, (0, 1))
    for some in blocks:
        p = dot_t(lin[...], w[some, 0:768])
        part[:, :, :, some] = p.astype(bf16).reshape(2, 2, ROWS, 512)
        gain_one = jnp.sum(p * n1[:, some].astype(f32), 0, keepdims=True) / gains[0:1, some]
        both = jnp.concatenate([gain_one, gain_two[0:1, some], jnp.zeros((6, 512), f32)], 0)
        side[some] = dot_l(both.astype(bf16), hot).astype(bf16)

    def gains_plan():
        halves = [
            grads_plan(side, side_shard, "z", "y", 0, side_a, rings[2], sems[3]),
            grads_plan(side, side_shard, "y", "z", 2, side_b, rings[3], sems[4]),
        ]
        for _ in range(6):
            for half in halves:
                next(half)
            yield
        run(*halves)
        swap = swap_plan([(lambda q: side_shard.at[q], lambda me: side_all.at[me])], sems[0])
        next(swap)
        yield
        run(swap)
        mine[...] = added(side_all[0], side_all[1], side_all[2], side_all[3])
        copy = remote(mine, theirs, *sems[0].take(), copy_of)
        copy.start()
        yield
        copy.wait()
        gain[...] = mine[...] + theirs[...]

    total = sum_plan(part, summed, sums, sems[5])
    by_gain = gains_plan()
    next(total)
    next(by_gain)
    swap_last = swap_plan([(lambda q: shard.at[q], lambda me: o.at[me])], sems[6])
    for plan in (
        *legs,
        *legs,
        total,
        by_gain,
        *legs,
        total,
        by_gain,
        *legs,
        by_gain,
        *legs,
        by_gain,
        *legs,
        swap_last,
        by_gain,
        total,
    ):
        next(plan, None)
    run(by_gain, total, swap_feed, swap_last, *legs)


def end(grads, w, n1, n1_t, grad_out, gains, tabs, gain_two, down, up):
    block, narrow = (32, 1024), (32, HD)
    return pl.pallas_call(
        end_kernel,
        out_shape=[
            jax.ShapeDtypeStruct((4, *block), bf16),
            jax.ShapeDtypeStruct(narrow, f32),
            jax.ShapeDtypeStruct((ROWS, D), f32),
            jax.ShapeDtypeStruct((4, *block), bf16),
            jax.ShapeDtypeStruct((4, *block), bf16),
        ],
        in_specs=vmem_specs(1) + [pl.BlockSpec(memory_space=pl.ANY)] + vmem_specs(8),
        out_specs=vmem_specs(5),
        scratch_shapes=[
            pltpu.VMEM((D, 1152), bf16),
            pltpu.VMEM((512, 768), bf16),
            pltpu.VMEM((D, 1024), bf16),
            pltpu.VMEM((D, HD), bf16),
            pltpu.VMEM((2, 2, ROWS, D), bf16),
            pltpu.VMEM((4, *block), bf16),
            pltpu.VMEM((4, *narrow), bf16),
            pltpu.VMEM((4, *narrow), bf16),
            pltpu.VMEM(narrow, f32),
            pltpu.VMEM(narrow, f32),
        ]
        + [pltpu.VMEM((4, 2, *block), bf16)] * 2
        + [pltpu.VMEM((4, 2, *narrow), bf16)] * 2
        + ring_buffers(5, block) * 2
        + ring_buffers(5, narrow) * 2
        + SUM_BUFFERS
        + sem_pair(10)
        + sem_pair(5 * RING_SEMS) * 4
        + sem_pair(SUM_SEMS)
        + sem_pair(3)
        + [pltpu.SemaphoreType.DMA((1,))],
        compiler_params=params(7, vmem=60),
        name="end",
    )(grads, w, n1, n1_t, grad_out, gains, tabs, gain_two, down, up)


def finish_kernel(
    *refs,
):
    given, (out, g_in, g_q, g_k, g_v, g_out, g_up, g_down, g_one, g_two), refs = refs[:10], refs[10:20], refs[20:]
    last, grad_down, grad_up, gain, summed, x, grad_middle, gains, middle, fed, total, sems = refs
    loads = [pltpu.make_async_copy(a, b, sems.at[k]) for k, (a, b) in enumerate(zip(given, refs[:10]))]
    for copy in loads:
        copy.start()
    for copy in loads:
        copy.wait()
    total[...] = middle[...] + fed[...]
    to_outer(lambda k: total[:, k * HD : (k + 1) * HD], out, bf16)
    n, rate = norm(x[...].astype(f32))
    total[...] = grad_middle[...] + norm_back(summed[...], n, rate, gains[0:1])
    to_outer(lambda k: total[:, k * HD : (k + 1) * HD], g_in, f32)
    for q in range(4):
        for k, o in enumerate((g_q, g_k, g_v)):
            o[:, q * 256 : (q + 1) * 256] = last[q, :, k * 256 : (k + 1) * 256].astype(f32)
        g_out[:, q * 256 : (q + 1) * 256] = last[q, :, 768:1024].astype(f32)
        g_down[:, q * 1024 : (q + 1) * 1024] = grad_down[q].astype(f32)
        g_up[:, q * 1024 : (q + 1) * 1024] = grad_up[q].astype(f32)
    gain_t = gain[...].T
    g_one[...] = gain_t[0]
    g_two[...] = gain_t[1]


def finish(*args):
    def shape(*dims, kind=f32):
        return jax.ShapeDtypeStruct(dims, kind)

    return pl.pallas_call(
        finish_kernel,
        out_shape=[
            shape(ROWS, D, kind=bf16),
            shape(ROWS, D),
            shape(32, 1024),
            shape(32, 1024),
            shape(32, 1024),
            shape(32, 1024),
            shape(32, 4096),
            shape(32, 4096),
            shape(32),
            shape(32),
        ],
        in_specs=[pl.BlockSpec(memory_space=pl.ANY)] * 10,
        out_specs=vmem_specs(10),
        scratch_shapes=[pltpu.VMEM(a.shape, a.dtype) for a in args]
        + [pltpu.VMEM((ROWS, D), f32), pltpu.SemaphoreType.DMA((10,))],
        compiler_params=params(vmem=60),
        name="finish",
    )(*args)


def local(
    inputs,
    clip_starts,
    pad_lengths,
    w_query,
    w_key,
    w_value,
    w_out,
    w_up,
    w_down,
    gain_first,
    gain_second,
    cotangent,
):
    (
        first,
        x_here,
        incoming,
        tabs,
        normed_one,
        normed_one_t,
        gains,
        facts,
        q,
        kv,
        incoming_all,
        o,
        lse,
        mixed,
        middle,
        normed_two,
        second,
    ) = front(
        w_query,
        w_key,
        w_value,
        w_out.T,
        w_up,
        w_down.T,
        inputs[0],
        cotangent[0],
        gain_first[None],
        gain_second[None],
        clip_starts,
        pad_lengths[None],
    )
    first = first.reshape(D, -1)
    part_out, grad_up, grad_out, grad_middle, grad_mixed, gain_two, down_shard = feed(
        normed_two, incoming_all, middle, incoming, gains, first, second.reshape(D, D), mixed.reshape(512, 256)
    )
    grads, fed, up_shard = attend_back(facts, q, kv, o, lse, grad_mixed, part_out, grad_up)
    last, gain_grads, summed, grad_down, grad_up = end(
        grads, first, normed_one, normed_one_t, grad_out, gains, tabs, gain_two, down_shard, up_shard
    )
    output, grad_input, *rest = finish(
        last, grad_down, grad_up, gain_grads, summed, x_here, grad_middle, gains, middle, fed
    )
    g_query, g_key, g_value, g_out, g_up, g_down, g_one, g_two = rest
    return (output[None], grad_input[None], g_query, g_key, g_value, g_out.T, g_up, g_down.T, g_one, g_two)


def solution(mesh):
    split = Mesh(mesh.devices.reshape(2, 4, 4, 2, 2), ("dp", "z", "y", "c", "mp"))
    seq = ("z", "y", "c")
    weights = ("dp", "z", "y", "c")
    tokens = P("dp", seq, None)
    wide, tall = P(weights, "mp"), P("mp", weights)
    return jax.shard_map(
        local,
        mesh=split,
        in_specs=(tokens, P("dp", None), P("dp"), wide, wide, wide, tall, wide, tall, P(weights), P(weights), tokens),
        out_specs=(tokens, tokens, wide, wide, wide, tall, wide, tall, P(weights), P(weights)),
        check_vma=False,
    )
```

```python
import functools

import jax
import jax.numpy as jnp
from jax import lax
from jax.experimental import pallas as pl
from jax.experimental.pallas import tpu as pltpu
from jax.sharding import Mesh
from jax.sharding import PartitionSpec as P

MESH = pl.DeviceIdType.MESH
HD = 128
FRAME = 32
LEN = 4096
D = 2048
ROWS = 128
BLOCK = 256
ZY = ("z", "y")
epsilon = 1e-05
scale = HD**-0.5
LOG_BASE = 9.210340371976184
f32 = jnp.float32
bf16 = jnp.bfloat16


def params(collective_id=None, vmem=48, **kw):
    if collective_id is not None:
        kw = dict(collective_id=collective_id, has_side_effects=True, **kw)
    return pltpu.CompilerParams(vmem_limit_bytes=vmem * 2**20, **kw)


def vmem_specs(n):
    return [pl.BlockSpec(memory_space=pltpu.VMEM)] * n


def greet(peers):
    barrier = pltpu.get_barrier_semaphore()
    for peer in peers:
        pl.semaphore_signal(barrier, inc=1, device_id=peer, device_id_type=MESH)
    pl.semaphore_wait(barrier, len(peers))


def remote(src, dst, send, recv, peer):
    return pltpu.make_async_remote_copy(
        src_ref=src, dst_ref=dst, send_sem=send, recv_sem=recv, device_id=peer, device_id_type=MESH
    )


def started(copies, src, dst, send, recv, peer):
    copy = remote(src, dst, send, recv, peer)
    copy.start()
    copies.append(copy)
    return copy


class Sems:
    def __init__(self, send, recv):
        self.send, self.recv, self.used = send, recv, 0

    def take(self):
        k = self.used
        self.used += 1
        return self.send.at[k], self.recv.at[k]


def sem_pair(n):
    return [pltpu.SemaphoreType.DMA((n,)), pltpu.SemaphoreType.DMA((n,))]


def tensor_place():
    d, c, m = lax.axis_index("dp"), lax.axis_index("c"), lax.axis_index("mp")
    return d, c, m, {"c": 1 - c}, {"dp": 1 - d, "mp": 1 - m}, {"mp": 1 - m}


def ring(axis, size=4):
    me = lax.axis_index(axis)
    up, down, far = (lax.rem(me + k, size) for k in (1, size - 1, 2))
    return me, up, down, far, {axis: up}, {axis: down}


def added(*values):
    total = values[0].astype(f32)
    for v in values[1:]:
        total = total + v.astype(f32)
    return total


def run(*protocols):
    live = list(protocols)
    while live:
        for p in list(live):
            try:
                next(p)
            except StopIteration:
                live.remove(p)


def swap_plan(pairs, sems):
    d, c = lax.axis_index("dp"), lax.axis_index("c")
    me = 2 * d + c
    copies = []
    for a, b in [(d, 1 - c), (1 - d, c), (1 - d, 1 - c)]:
        for src, dst in pairs:
            started(copies, src(2 * a + b), dst(me), *sems.take(), {"dp": a, "c": b})
    for src, dst in pairs:
        dst(me)[...] = src(me)[...]
    yield
    for copy in copies:
        copy.wait_recv()
    yield
    for copy in copies:
        copy.wait_send()


def quarter(ref):
    wide = ref.shape[1] // 4
    return lambda q: ref.at[:, pl.ds(pl.multiple_of(q * wide, wide), wide)]


class Stores:
    def __init__(self, buffers, outputs, sems):
        self.pairs, self.sems, self.copies = list(zip(buffers, outputs)), sems, []

    def __call__(self, *places):
        for k in places:
            copy = pltpu.make_async_copy(*self.pairs[k], self.sems.at[k])
            copy.start()
            self.copies.append(copy)

    def wait(self):
        for copy in self.copies:
            copy.wait()


def swap_peers():
    d, c = lax.axis_index("dp"), lax.axis_index("c")
    return [{"dp": 1 - d}, {"dp": 1 - d, "c": 1 - c}]


CHUNKS = 4
HALF = ROWS // 2


def rows_plan(x, o, sems):
    d, c, m, core, across, copy_of = tensor_place()
    me, far = 2 * d + c, 2 * (1 - d) + c
    copies, firsts, seconds = [], [], []
    step = HALF // 2
    mine = [pl.ds(m * HALF + k * step, step) for k in range(2)]
    other = [pl.ds((1 - m) * HALF + k * step, step) for k in range(2)]
    for rows in mine:
        firsts.append(started(copies, x.at[rows], o.at[me, rows], *sems.take(), across))
    near = started(copies, x, o.at[me], *sems.take(), core)
    o[me] = x[...]
    yield
    for k, rows in enumerate(other):
        firsts[k].wait_recv()
        seconds.append(started(copies, o.at[far, rows], o.at[far, rows], *sems.take(), copy_of))
    yield
    lasts = []
    for rows in other:
        lasts.append(started(copies, o.at[far, rows], o.at[far, rows], *sems.take(), core))
    for k, rows in enumerate(mine):
        seconds[k].wait_recv()
        lasts.append(started(copies, o.at[far, rows], o.at[far, rows], *sems.take(), core))
    yield
    near.wait_recv()
    for copy in lasts:
        copy.wait_recv()
    for copy in copies:
        copy.wait_send()


ROWS_SEMS = 9


def sum_plan(x, o, buffers, sems):
    from_core, s_here, s_send, from_across, t_send, from_copy = buffers
    d, c, m, core, across, copy_of = tensor_place()
    step = ROWS // CHUNKS
    rows = [pl.ds(k * step, step) for k in range(CHUNKS)]
    copies, zero, one, two = [], [], [], []
    for r in rows:
        zero.append(started(copies, x.at[:, 1 - c, r], from_core.at[:, r], *sems.take(), core))
    yield
    for k, r in enumerate(rows):
        zero[k].wait_recv()
        s_send[r] = x[1 - d, c, r] + from_core[1 - d, r]
        one.append(started(copies, s_send.at[r], from_across.at[r], *sems.take(), across))
        s_here[r] = x[d, c, r] + from_core[d, r]
    yield
    for k, r in enumerate(rows):
        one[k].wait_recv()
        t_send[r] = s_here[r] + from_across[r]
        two.append(started(copies, t_send.at[r], from_copy.at[r], *sems.take(), copy_of))
    yield
    for k, r in enumerate(rows):
        two[k].wait_recv()
        o[r] = added(t_send[r], from_copy[r])
    for copy in copies:
        copy.wait_send()


SUM_SEMS = 3 * CHUNKS
SUM_BUFFERS = [
    pltpu.VMEM((2, ROWS, D), bf16),
    pltpu.VMEM((ROWS, D), bf16),
    pltpu.VMEM((ROWS, D), bf16),
    pltpu.VMEM((ROWS, D), bf16),
    pltpu.VMEM((ROWS, D), bf16),
    pltpu.VMEM((ROWS, D), bf16),
]


def weights_plan(w, first, second, low, sems):
    i0, i_up, i_down, i_far, to_i_up, to_i_down = ring(first)
    j0, j_up, j_down, j_far, to_j_up, to_j_down = ring(second)

    def at(i, j, part, n):
        return w.at[(j, i) if first == "y" else (i, j)].at[pl.ds(low + part, n)]

    copies = []

    def send(ref, peer):
        return started(copies, ref, ref, *sems.take(), peer)

    def along(i):
        return i, send(at(i, j0, 0, 2), to_j_up), send(at(i, j0, 0, 2), to_j_down)

    from_down, from_up = send(at(i0, j0, 0, 2), to_i_up), send(at(i0, j0, 0, 2), to_i_down)
    second_leg = [along(i0)]
    yield
    from_down.wait_recv()
    far_low = send(at(i_down, j0, 0, 1), to_i_up)
    from_up.wait_recv()
    far_high = send(at(i_up, j0, 1, 1), to_i_down)
    second_leg.append(along(i_down))
    yield
    second_leg.append(along(i_up))
    yield
    onward = []

    def relay(leg):
        i, a, b = leg
        a.wait_recv()
        onward.append(send(at(i, j_down, 0, 1), to_j_up))
        b.wait_recv()
        onward.append(send(at(i, j_up, 1, 1), to_j_down))

    far_low.wait_recv()
    far_high.wait_recv()
    second_leg.append(along(i_far))
    for leg in second_leg:
        yield
        relay(leg)
    yield
    for copy in onward:
        copy.wait_recv()
    for copy in copies:
        copy.wait_send()


WEIGHT_SEMS = 20


def to_inner(x, o):
    for k in range(16):
        low, high = x[:, k * 64 : (k + 1) * 64], x[:, D // 2 + k * 64 : D // 2 + (k + 1) * 64]
        o[:, k * HD : (k + 1) * HD] = jnp.concatenate([low, high], 1)


def to_outer(x, o, kind):
    for k in range(0, 16, 2):
        one, two = x(k), x(k + 1)
        o[:, k * 64 : k * 64 + HD] = jnp.concatenate([one[:, :64], two[:, :64]], 1).astype(kind)
        o[:, D // 2 + k * 64 : D // 2 + k * 64 + HD] = jnp.concatenate([one[:, 64:], two[:, 64:]], 1).astype(kind)


def side_of(one, two, starts, padding):
    lane = lax.broadcasted_iota(jnp.int32, (32, HD), 1)
    same = lax.broadcasted_iota(jnp.int32, (32, 32), 0) == lax.broadcasted_iota(jnp.int32, (32, 32), 1)

    def column(row):
        return jnp.sum(jnp.where(same, row[...].astype(f32), 0.0), 1, keepdims=True)

    value = jnp.where(lane == 0, column(one), 0.0)
    value = jnp.where(lane == 1, column(two), value)
    for k in range(3):
        value = jnp.where(lane == 2 + k, starts[:, k : k + 1].astype(f32), value)
    return jnp.where(lane == 5, padding[...].astype(f32), value).astype(bf16)


def spread_plan(x, q, kv, sems):
    z, z_up, z_down, z_far, to_z_up, to_z_down = ring("z")
    y, y_up, y_down, y_far, to_y_up, to_y_down = ring("y")
    far = {"z": z_far}
    copies, firsts, queries, nears, fars = [], [], [], [], []
    both = pl.ds(1, 2)
    peers = [(z_up, to_z_up, z_down), (z_down, to_z_down, z_up), (z_far, far, z_far)]
    for place, peer, _ in peers:
        firsts.append(started(copies, x.at[place, both], kv.at[z, y], *sems.take(), peer))
    kv[z, y] = x[z, both]

    def along(place):
        ref = kv.at[place, y]
        nears.append(
            (place, started(copies, ref, ref, *sems.take(), to_y_up), started(copies, ref, ref, *sems.take(), to_y_down))
        )

    along(z)
    for place, peer, _ in peers:
        queries.append(started(copies, x.at[place, 0], q.at[z], *sems.take(), peer))
    q[z] = x[z, 0]
    yield
    for k, (_, _, source) in enumerate(peers):
        firsts[k].wait_recv()
        along(source)
        yield
    for copy in queries:
        copy.wait_recv()
    yield
    for place, a, b in nears:
        a.wait_recv()
        ref = kv.at[place, y_down, 0]
        fars.append(started(copies, ref, ref, *sems.take(), to_y_up))
        b.wait_recv()
        ref = kv.at[place, y_up, 1]
        fars.append(started(copies, ref, ref, *sems.take(), to_y_down))
        yield
    for copy in fars:
        copy.wait_recv()
    yield
    for copy in copies:
        copy.wait_send()


def ring_sum(at, axis, buffers, sems, put, late=False):
    one, two, passed = buffers
    me, up, down, far, to_up, to_down = ring(axis)
    copies = []
    a = started(copies, at(far, 0), one.at[0], *sems.take(), to_up)
    b = started(copies, at(far, 1), one.at[1], *sems.take(), to_down)
    if late:
        yield
    plain = [started(copies, at(up, 1), two.at[0, 1], *sems.take(), to_up)]
    if late:
        yield
    plain.append(started(copies, at(down, 0), two.at[1, 0], *sems.take(), to_down))
    if not late:
        yield
    a.wait_recv()
    passed[0] = at(up, 0)[...] + one[0]
    plain.append(started(copies, passed.at[0], two.at[0, 0], *sems.take(), to_up))
    b.wait_recv()
    passed[1] = at(down, 1)[...] + one[1]
    plain.append(started(copies, passed.at[1], two.at[1, 1], *sems.take(), to_down))
    yield
    for copy in plain:
        copy.wait_recv()
    for part in range(2):
        put(part, added(at(me, part)[...], two[0, part], two[1, part]))
    yield
    for copy in copies:
        copy.wait_send()


RING_SEMS = 6


def ring_buffers(n, part):
    return [pltpu.VMEM((n, 2, *part), bf16), pltpu.VMEM((n, 2, 2, *part), bf16), pltpu.VMEM((n, 2, *part), bf16)]


def collect_plan(dq, dkv, o, total, buffers, sems):
    z, peers = z_peers()
    peers = peers + [(z, None)]
    copies, rings = [], []
    for k, (place, peer) in enumerate(peers):

        def at(i, part, place=place):
            return dkv.at[place, i, part]

        def put(part, value, k=k):
            if k < 3:
                total[k, part] = value.astype(bf16)
            else:
                o[z, 1 + part] = value.astype(bf16)

        rings.append(ring_sum(at, "y", [b.at[k] for b in buffers], sems, put, True))
    for _ in range(3):
        for r in rings:
            next(r)
        yield
    for place, peer in peers[:3]:
        started(copies, dq.at[place], o.at[z, 0], *sems.take(), peer)
    o[z, 0] = dq[z]
    for k, r in enumerate(rings):
        next(r)
        if k < 3:
            started(copies, total.at[k], o.at[z, pl.ds(1, 2)], *sems.take(), peers[k][1])
    yield
    for copy in copies:
        copy.wait()
    run(*rings)


def first_leg(g, first, low, legs, buffers, sems, late=False):
    rings = []
    for j in range(4):

        def at(i, part, j=j):
            z, y = (j, i) if first == "y" else (i, j)
            return g.at[pl.ds(pl.multiple_of(((4 * z + y) * 4 + low + part) * 32, 32), 32)]

        def put(part, value, j=j):
            legs[j, part] = value.astype(bf16)

        rings.append(ring_sum(at, first, [b.at[j] for b in buffers], sems, put, late))
    for _ in range(4 if late else 3):
        for r in rings:
            next(r)
        yield
    run(*rings)


def second_leg(legs, shard, second, low, buffers, sems):
    def put(part, value):
        shard[low + part] = value.astype(bf16)

    return ring_sum(lambda i, part: legs.at[i, part], second, [b.at[b.shape[0] - 1] for b in buffers], sems, put)


def grads_plan(g, shard, first, second, low, legs, buffers, sems, late=False):
    leg = first_leg(g, first, low, legs, buffers, sems, late)
    for _ in range(4 if late else 3):
        next(leg)
        yield
    last = second_leg(legs, shard, second, low, buffers, sems)
    for _ in range(3):
        next(last)
        yield
    run(leg, last)


def reach(facts, block, rows):
    t = block * rows + lax.broadcasted_iota(jnp.int32, (rows, 1), 0)
    one, two, three, padding = (facts[:, k : k + 1].astype(jnp.int32) for k in range(2, 6))
    begin = jnp.where(t >= three, three, jnp.where(t >= two, two, one))
    living = t < LEN - padding
    end = jnp.minimum((t // FRAME + 1) * FRAME, LEN - padding)
    return t, begin, jnp.where(living, begin, t), jnp.where(living, end, t + 1)


def dot_t(a, b):
    return lax.dot_general(a, b, (((1,), (1,)), ((), ())), preferred_element_type=f32)


def dot_l(a, b):
    return lax.dot_general(a, b, (((0,), (0,)), ((), ())), preferred_element_type=f32)


def column_scores(facts, q, kv, i, column):
    n = (i + 1) * BLOCK
    _, _, low, high = reach(facts[pl.ds(lax.axis_index("z") // 2, 1)], 4 * i + lax.axis_index("y"), BLOCK)
    k = kv[0 : i + 1, column, 0].reshape(n, HD)
    at = lax.broadcasted_iota(jnp.int32, (1, n), 1)
    at = (at // BLOCK) * (4 * BLOCK) + at % BLOCK + column * BLOCK
    s = dot_t(q[i], k) * scale
    before, own = s[:, : i * BLOCK], s[:, i * BLOCK :]
    here = at[:, i * BLOCK :]
    own = jnp.where((here >= low) & (here < high), own, -1e30)
    if i:
        own = jnp.concatenate([jnp.where(at[:, : i * BLOCK] >= low, before, -1e30), own], 1)
    return k, own


def attend_tile(facts, q, kv, top, total, acc, i, column, first):
    _, s = column_scores(facts, q, kv, i, column)
    v = kv[0 : i + 1, column, 1].reshape((i + 1) * BLOCK, HD)
    now = jnp.max(s, -1, keepdims=True)
    if not first:
        before = top[i][:, :1]
        now = jnp.maximum(before, now)
    p = jnp.exp(s - now)
    plus = jnp.sum(p, -1, keepdims=True)
    out = jnp.dot(p.astype(bf16), v, preferred_element_type=f32)
    if not first:
        shrink = jnp.exp(before - now)
        plus = plus + total[i][:, :1] * shrink
        out = out + acc[i] * shrink
    top[i] = jnp.broadcast_to(now, (BLOCK, HD))
    total[i] = jnp.broadcast_to(plus, (BLOCK, HD))
    acc[i] = out


def attend_back_tile(facts, q, kv, do, lse, inner, dq, acc, i, column, first):
    k, s = column_scores(facts, q, kv, i, column)
    n = i + 1
    v = kv[0:n, column, 1].reshape(n * BLOCK, HD)
    p = jnp.exp(s - lse[i][:, :1])
    ds = (p * (dot_t(do[i], v) - inner[i][:, :1])).astype(bf16)
    dv = dot_l(p.astype(bf16), do[i]).reshape(n, BLOCK, HD)
    dk = dot_l(ds, q[i]).reshape(n, BLOCK, HD)
    part = jnp.dot(ds, k, preferred_element_type=f32)
    if i == 3:
        acc[:, 0], acc[:, 1] = dk, dv
    else:
        acc[0:n, 0] += dk
        acc[0:n, 1] += dv
    dq[i] = part if first else dq[i] + part


def norm(value):
    centre = value - jnp.mean(value, -1, keepdims=True)
    r = lax.rsqrt(jnp.mean(centre * centre, -1, keepdims=True) + epsilon)
    return centre * r, r


def norm_back(grad, n, r, gain):
    e = grad * gain
    return r * (e - jnp.mean(e, -1, keepdims=True) - n * jnp.mean(e * n, -1, keepdims=True))


def one_hot(rows, places):
    at = lax.broadcasted_iota(jnp.int32, (rows, HD), 0)
    lane = lax.broadcasted_iota(jnp.int32, (rows, HD), 1)
    hot = at < 0
    for k, place in enumerate(places):
        hot = hot | ((at == k) & (lane == place))
    return jnp.where(hot, 1.0, 0.0).astype(bf16)


def tables(facts, c):
    block = (4 * lax.axis_index("z") + lax.axis_index("y")) * 2 + c
    t, begin, _, _ = reach(facts, block, ROWS)
    lane = lax.broadcasted_iota(jnp.int32, (1, HD), 1)
    i = jnp.where(lane < HD // 2, lane, lane - HD // 2).astype(f32)
    angles = (t - begin).astype(f32) * jnp.exp(i * (-2.0 * LOG_BASE / HD))
    return jnp.cos(angles), jnp.where(lane < HD // 2, -1.0, 1.0) * jnp.sin(angles)


def sum_norm_plan(x, produce, all_rows, make, buffers, sems, idle=lambda: None):
    from_core, s_here, s_send, from_across, t_send, from_copy = buffers
    d, c, m, core, across, copy_of = tensor_place()
    me, far = 2 * d + c, 2 * (1 - d) + c
    step = ROWS // CHUNKS
    rows = [pl.ds(k * step, step) for k in range(CHUNKS)]
    copies, zero, one, two = [], [], [], []
    for h in range(2):
        produce(h)
        for r in rows[2 * h : 2 * h + 2]:
            zero.append(started(copies, x.at[:, 1 - c, r], from_core.at[:, r], *sems.take(), core))
        for k in range(2 * h, 2 * h + 2):
            r = rows[k]
            zero[k].wait_recv()
            s_send[r] = x[1 - d, c, r] + from_core[1 - d, r]
            one.append(started(copies, s_send.at[r], from_across.at[r], *sems.take(), across))
            s_here[r] = x[d, c, r] + from_core[d, r]
    idle()
    for k, r in enumerate(rows):
        idle()
        one[k].wait_recv()
        t_send[r] = s_here[r] + from_across[r]
        two.append(started(copies, t_send.at[r], from_copy.at[r], *sems.take(), copy_of))
    yield
    nears, firsts, seconds, lasts = [], [], [], []
    idle()
    for k, r in enumerate(rows):
        idle()
        two[k].wait_recv()
        all_rows[me, r] = make(r, added(t_send[r], from_copy[r])).astype(bf16)
        nears.append(started(copies, all_rows.at[me, r], all_rows.at[me, r], *sems.take(), core))
        half = pl.ds(pl.multiple_of(k * step + m * (step // 2), step // 2), step // 2)
        firsts.append(started(copies, all_rows.at[me, half], all_rows.at[me, half], *sems.take(), across))
    yield

    def onward(half, peer):
        return started(copies, all_rows.at[far, half], all_rows.at[far, half], *sems.take(), peer)

    idle()
    for k in range(CHUNKS):
        idle()
        firsts[k].wait_recv()
        half = pl.ds(pl.multiple_of(k * step + (1 - m) * (step // 2), step // 2), step // 2)
        seconds.append(onward(half, copy_of))
        lasts.append(onward(half, core))
    yield
    idle()
    for k in range(CHUNKS):
        idle()
        seconds[k].wait_recv()
        half = pl.ds(pl.multiple_of(k * step + m * (step // 2), step // 2), step // 2)
        lasts.append(onward(half, core))
    yield
    for copy in nears + lasts:
        copy.wait_recv()
    yield
    for copy in copies:
        copy.wait_send()


SUM_NORM_SEMS = 8 * CHUNKS
OUT_COLUMNS = pl.BlockSpec((D, 256), lambda i: (0, 3))


def z_peers():
    z, z_up, z_down, z_far, to_z_up, to_z_down = ring("z")
    return z, [(z_up, to_z_up), (z_down, to_z_down), (z_far, {"z": z_far})]


def front_kernel(
    wq,
    wk,
    wv,
    wo,
    wu,
    wd,
    x_hbm,
    cot_hbm,
    one,
    two,
    starts,
    padding,
    w_hbm,
    *scratch,
):
    outputs, weights_hbm, scratch = scratch[:15], scratch[15], scratch[16:]
    x_here, cot, tabs, n1, n1_t, gains, facts, q, kv, rows, o, lse, mixed, middle, n2 = scratch[:15]
    keep = Stores(scratch[:15], outputs, scratch[15])
    scratch = scratch[16:]
    w, weights, qkv, top, total, acc, low, turned, part, x_raw, cot_raw, side, x, lin = scratch[:14]
    sums, scratch = scratch[14:20], scratch[20:]
    local = scratch[0]
    sems = [Sems(*scratch[1 + 2 * k : 3 + 2 * k]) for k in range(10)]
    keys_sems, rows_sems, norm_sems, turn_sems, leg_a, leg_b, swaps, x_sems, first_a, first_b = sems
    d, c = lax.axis_index("dp"), lax.axis_index("c")
    me = 2 * d + c
    z, peers = z_peers()
    y, up, down, far, y_up, y_down = ring("y")
    here, there = w.at[z, y, me], weights.at[z, y, me]
    firsts = [(wq, 0, 256), (wk, 256, 256), (wv, 512, 256), (wo, 768, 256)]
    rests = [(wu, 0, 1024), (wd, 1024, 1024)]
    loads = [pltpu.make_async_copy(x_hbm, x_raw, local.at[0]), pltpu.make_async_copy(cot_hbm, cot_raw, local.at[1])]
    for k, (src, left, n) in enumerate(firsts):
        loads.append(pltpu.make_async_copy(quarter(src)(me), here.at[:, pl.ds(left, n)], local.at[2 + k]))
    for k, (src, left, n) in enumerate(rests):
        loads.append(pltpu.make_async_copy(quarter(src)(me), there.at[:, pl.ds(left, n)], local.at[6 + k]))
    for copy in loads:
        copy.start()
    side[...] = side_of(one, two, starts, padding)
    here[:, 1024:1152] = side[...]
    greet([*tensor_place()[3:], *swap_peers(), *[peer for _, peer in peers], y_up, y_down])

    def swap(pairs, dst):
        copies = []
        for a, b in [(d, 1 - c), (1 - d, c), (1 - d, 1 - c)]:
            for src, left, n in pairs:
                started(copies, src(2 * a + b), dst.at[:, pl.ds(left, n)], *swaps.take(), {"dp": a, "c": b})
        return copies

    swap_first = swap([(quarter(src), left, n) for src, left, n in firsts] + [(lambda q: side, 1024, HD)], here)
    loads[0].wait()
    to_inner(x_raw, x_here)
    gather_x = rows_plan(x_here, x, x_sems)
    next(gather_x)
    for copy in loads[2:6]:
        copy.wait()
    for copy in swap_first:
        copy.wait_recv()
    legs = [weights_plan(w, "y", "z", 0, first_a), weights_plan(w, "z", "y", 2, first_b)]
    for leg in legs:
        next(leg)
    swap_rest = swap([(quarter(src), left, n) for src, left, n in rests], there)
    for seq in range(2):
        fact = w[z, y, 2 * seq, 0:1, 1024:1152].astype(f32)
        for half in range(2):
            tabs[0, 2 * seq + half], tabs[1, 2 * seq + half] = tables(fact, half)
    loads[1].wait()
    to_inner(cot_raw, cot)
    run(*legs, gather_x)
    store = pltpu.make_async_copy(w, w_hbm, local.at[8])
    store.start()
    keep(0, 1, 2)
    for copy in loads[6:] + swap_rest:
        copy.wait()
    for copy in swap_first:
        copy.wait_send()

    def columns(left, right):
        return w[:, :, :, :, left:right].reshape(D, right - left)

    gather = rows_plan(cot, rows, rows_sems)
    next(gather)
    legs = [weights_plan(weights, "y", "z", 0, leg_a), weights_plan(weights, "z", "y", 2, leg_b)]

    def leg_step():
        for leg in legs:
            next(leg, None)

    leg_step()
    side = columns(1024, 1152)
    gains[...] = dot_t(one_hot(8, (0, 1)), side)
    facts[...] = jnp.zeros_like(facts)
    facts[0:1] = side[0:1].astype(f32)
    facts[1:2] = side[64:65].astype(f32)
    for block in range(4):
        r = pl.ds(block * ROWS, ROWS)
        n1[r] = (norm(x[block].astype(f32))[0] * gains[0:1]).astype(bf16)
    lin[...] = jnp.dot(n1[...], columns(0, 768), preferred_element_type=f32)
    for block in range(4):
        seq, half = block // 2, block % 2
        r = pl.ds(block * ROWS, ROWS)
        for kind in range(3):
            for h in range(2):
                v = lin[r, (2 * kind + h) * HD : (2 * kind + h + 1) * HD]
                if kind < 2:
                    v = v * tabs[0, block] + pltpu.roll(v, HD // 2, 1) * tabs[1, block]
                qkv[2 * seq + h, kind, half * ROWS : (half + 1) * ROWS] = v.astype(bf16)
    keys = spread_plan(qkv, q, kv, keys_sems)
    keep(3, 5, 6)

    def work():
        for k in range(4):
            some = slice(512 * k, 512 * (k + 1))
            n1_t[some] = n1[:, some].T
            yield
        for i in range(4):
            attend_tile(facts, q, kv, top, total, acc, i, y, True)
            yield

    pieces = work()
    next(keys)
    next(gather)
    for _ in range(4):
        next(pieces)
        next(keys)
    next(gather)
    for _ in range(4):
        next(pieces)
        next(keys)
    next(gather, None)
    leg_step()
    for column in (down, up):
        for i in range(4):
            attend_tile(facts, q, kv, top, total, acc, i, column, False)
    run(keys, gather)
    keep(4, 7, 8, 9)
    for i in range(4):
        attend_tile(facts, q, kv, top, total, acc, i, far, False)
    for i in range(4):
        low[i] = (acc[i] / total[i]).astype(bf16)
    copies = []
    for place, peer in peers:
        started(copies, low.at[place], turned.at[z], *turn_sems.take(), peer)
    turned[z] = low[z]
    for i in range(4):
        o[i] = acc[i] / total[i]
        lse[i] = top[i] + jnp.log(total[i])
    keep(10, 11)
    leg_step()
    for copy in copies:
        copy.wait()
    for seq in range(2):
        for h in range(2):
            mixed[seq, :, :, h * HD : (h + 1) * HD] = turned[2 * seq + h].reshape(2, ROWS, HD)
    keep(12)

    def partial(h):
        r = slice(HALF * h, HALF * (h + 1))
        value = dot_t(mixed[:, :, r].reshape(2 * ROWS, 256), columns(768, 1024))
        part[:, :, r] = value.astype(bf16).reshape(2, 2, HALF, D)

    def make(r, value):
        value = x_here[r].astype(f32) + value
        middle[r] = value
        return norm(value)[0] * gains[1:2]

    def legs_work():
        for pause in (0, 0, 0, 2, 5, 3):
            for _ in range(pause):
                yield
            if pause != 3:
                leg_step()
        yield
        run(*legs)
        pltpu.make_async_copy(weights, weights_hbm, local.at[9]).start()
        yield

    rest = legs_work()
    run(sum_norm_plan(part, partial, n2, make, sums, norm_sems, lambda: next(rest, None)))
    keep(13, 14)
    for _ in rest:
        pass
    keep.wait()
    pltpu.make_async_copy(weights, weights_hbm, local.at[9]).wait()
    store.wait()


def front(*args):
    block = (4, BLOCK, HD)
    shape = jax.ShapeDtypeStruct
    anywhere = pl.BlockSpec(memory_space=pl.ANY)
    whole = lambda *dims: pl.BlockSpec(dims, lambda i: (0,) * len(dims))
    first, second = (4, 4, 4, 32, 1152), (4, 4, 4, 32, 2048)
    kept = [
        shape((ROWS, D), bf16),
        shape((ROWS, D), bf16),
        shape((2, 4, ROWS, HD), f32),
        shape((512, D), bf16),
        shape((D, 512), bf16),
        shape((8, D), f32),
        shape((8, HD), f32),
        shape(block, bf16),
        shape((4, 4, 2, BLOCK, HD), bf16),
        shape((4, ROWS, D), bf16),
        shape(block, f32),
        shape(block, f32),
        shape((2, 2, ROWS, 256), bf16),
        shape((ROWS, D), f32),
        shape((4, ROWS, D), bf16),
    ]
    return pl.pallas_call(
        front_kernel,
        grid=(1,),
        out_shape=[shape(first, bf16), *kept, shape(second, bf16)],
        in_specs=[anywhere] * 8 + [whole(1, 32), whole(1, 32), whole(1, 3), whole(1, 1)],
        out_specs=[anywhere] * 17,
        scratch_shapes=[pltpu.VMEM(a.shape, a.dtype) for a in kept]
        + [pltpu.SemaphoreType.DMA((15,))]
        + [
            pltpu.VMEM(first, bf16),
            pltpu.VMEM(second, bf16),
            pltpu.VMEM((4, 3, BLOCK, HD), bf16),
        ]
        + [pltpu.VMEM(block, f32)] * 3
        + [pltpu.VMEM(block, bf16)] * 2
        + [pltpu.VMEM((2, 2, ROWS, D), bf16)]
        + [pltpu.VMEM((ROWS, D), bf16)] * 2
        + [pltpu.VMEM((32, HD), bf16), pltpu.VMEM((4, ROWS, D), bf16), pltpu.VMEM((512, 768), f32)]
        + SUM_BUFFERS
        + [pltpu.SemaphoreType.DMA((10,))]
        + sem_pair(22)
        + sem_pair(ROWS_SEMS)
        + sem_pair(SUM_NORM_SEMS)
        + sem_pair(3)
        + sem_pair(WEIGHT_SEMS) * 2
        + sem_pair(21)
        + sem_pair(ROWS_SEMS)
        + sem_pair(WEIGHT_SEMS) * 2,
        compiler_params=params(4, vmem=60),
        name="front",
    )(*args)


def feed_kernel(n2_hbm, cot_all_hbm, middle_hbm, cot_hbm, gains, w, weights, mixed_hbm, *scratch):
    outputs, scratch = scratch[:9], scratch[9:]
    fed, grad_out, grad_middle, turned, gain_two, down_a, down_b, up_a, up_b = scratch[:9]
    keep = Stores(scratch[:9], outputs, scratch[9])
    n2, cot_all, middle, cot, mixed = scratch[10:15]
    up, down, n2_t, cot_t, grads_down, grads_up, branch, active, grad_hidden, part, grad_mixed = scratch[15:26]
    scratch = scratch[26:]
    z, peers = z_peers()
    local = scratch[10]
    _, _, _, _, z_up, z_down = ring("z")
    _, _, _, _, y_up, y_down = ring("y")
    loads = [
        pltpu.make_async_copy(cot_all_hbm, cot_all, local.at[0]),
        pltpu.make_async_copy(weights.at[:, pl.ds(1024, 1024)], down, local.at[1]),
        pltpu.make_async_copy(n2_hbm, n2, local.at[2]),
        pltpu.make_async_copy(weights.at[:, pl.ds(0, 1024)], up, local.at[3]),
        pltpu.make_async_copy(middle_hbm, middle, local.at[4]),
        pltpu.make_async_copy(cot_hbm, cot, local.at[5]),
        pltpu.make_async_copy(mixed_hbm, mixed, local.at[6]),
    ]
    for copy in loads:
        copy.start()
    gain_two[...] = jnp.zeros_like(gain_two)
    greet([*tensor_place()[3:], *[peer for _, peer in peers], y_up, y_down])
    loads[0].wait()
    for k in range(4):
        some = slice(512 * k, 512 * (k + 1))
        cot_t[some] = cot_all[:, :, :, some].reshape(512, 512).T
    for copy in loads[1:]:
        copy.wait()

    def partial(h):
        rows = slice(HALF * h, HALF * (h + 1))
        n = n2[:, :, rows].reshape(2 * ROWS, D)
        g = cot_all[:, :, rows].reshape(2 * ROWS, D)
        for j in range(4):
            some = slice(256 * j, 256 * (j + 1))
            grad_active = jnp.dot(g, down[:, some], preferred_element_type=f32)
            hidden = jnp.dot(n, up[:, some], preferred_element_type=f32)
            half = 0.5 * (1.0 + lax.erf(hidden * 0.5**0.5))
            slope = half + hidden * jnp.exp(-0.5 * hidden * hidden) * (0.5 / jnp.pi) ** 0.5
            active[:, :, rows, some] = (hidden * half).astype(bf16).reshape(2, 2, HALF, 256)
            grad_hidden[:, :, rows, some] = (grad_active * slope).astype(bf16).reshape(2, 2, HALF, 256)
        value = grad_hidden[:, :, rows].reshape(2 * ROWS, 1024)
        for k in range(4):
            some = slice(512 * k, 512 * (k + 1))
            part[:, :, rows, some] = dot_t(value, up[some]).astype(bf16).reshape(2, 2, HALF, 512)

    downs = [
        first_leg(grads_down, "z", 0, down_a, scratch[11:14], Sems(*scratch[23:25])),
        first_leg(grads_down, "y", 2, down_b, scratch[14:17], Sems(*scratch[25:27])),
    ]
    ups = [
        first_leg(grads_up, "z", 0, up_a, scratch[17:20], Sems(*scratch[27:29])),
        first_leg(grads_up, "y", 2, up_b, scratch[20:23], Sems(*scratch[29:31])),
    ]

    def turn_n2(k):
        some = slice(512 * k, 512 * (k + 1))
        n2_t[some] = n2[:, :, :, some].reshape(512, 512).T

    def down_piece(j):
        some = slice(256 * j, 256 * (j + 1))
        value = active[:, :, :, some].reshape(512, 256)
        grads_down[:, some] = jnp.dot(cot_t[...], value, preferred_element_type=f32).astype(bf16)

    def up_piece(j):
        some = slice(256 * j, 256 * (j + 1))
        value = grad_hidden[:, :, :, some].reshape(512, 256)
        grads_up[:, some] = jnp.dot(n2_t[...], value, preferred_element_type=f32).astype(bf16)

    def fed_piece(k):
        some = slice(512 * k, 512 * (k + 1))
        value = dot_t(active[...].reshape(512, 1024), down[some])
        fed[:, :, :, some] = value.astype(bf16).reshape(2, 2, ROWS, 512)

    def step(plans):
        for plan in plans:
            next(plan, None)

    def work():
        for k in range(2):
            down_piece(2 * k)
            down_piece(2 * k + 1)
            if k:
                step(downs)
            yield
        for k in range(4):
            turn_n2(k)
        yield
        for j in range(4):
            up_piece(j)
            if j == 3:
                step(ups)
            yield
        step(downs)
        yield
        for k in range(4):
            fed_piece(k)
            if k == 3:
                keep(0)
            yield
        step(ups)
        yield

    pieces = work()

    def make(r, total):
        n, rate = norm(middle[r])
        gain_two[0:1] += 0.5 * jnp.sum(total * n, 0, keepdims=True)
        value = cot[r].astype(f32) + norm_back(total, n, rate, gains[1:2])
        grad_middle[r] = value
        return value

    run(sum_norm_plan(part, partial, branch, make, scratch[:6], Sems(*scratch[6:8]), lambda: next(pieces, None)))
    for k in range(4):
        value = jnp.dot(branch[k], w[...], preferred_element_type=f32).astype(bf16)
        for h in range(2):
            grad_mixed[2 * (k // 2) + h, (k % 2) * ROWS : (k % 2 + 1) * ROWS] = value[:, h * HD : (h + 1) * HD]
    turns, copies = Sems(*scratch[8:10]), []
    for place, peer in peers:
        started(copies, grad_mixed.at[place], turned.at[z], *turns.take(), peer)
    turned[z] = grad_mixed[z]
    for _ in pieces:
        pass
    keep(2, 4)
    for k in range(4):
        some = slice(512 * k, 512 * (k + 1))
        grad_out[some] = dot_l(branch[:, :, some].reshape(512, 512), mixed[...]).astype(bf16)
    keep(1)
    for copy in copies:
        copy.wait()
    keep(3)
    run(*downs, *ups)
    keep(5, 6, 7, 8)
    keep.wait()


def feed(n2, cot_all, middle, cot, gains, first, weights, mixed):
    anywhere = pl.BlockSpec(memory_space=pl.ANY)
    rows = (2, 2, ROWS, D)
    shape, vmem = jax.ShapeDtypeStruct, pltpu.VMEM
    kept = [
        shape(rows, bf16),
        shape((D, 256), bf16),
        shape((ROWS, D), f32),
        shape((4, BLOCK, HD), bf16),
        shape((8, D), f32),
    ] + [shape((4, 2, 32, 1024), bf16)] * 4
    return pl.pallas_call(
        feed_kernel,
        grid=(1,),
        out_shape=kept,
        in_specs=[anywhere] * 4 + vmem_specs(1) + [OUT_COLUMNS] + [anywhere] * 2,
        out_specs=[anywhere] * 9,
        scratch_shapes=[vmem(a.shape, a.dtype) for a in kept]
        + [pltpu.SemaphoreType.DMA((9,))]
        + [vmem(rows, bf16), vmem(rows, bf16), vmem((ROWS, D), f32), vmem((ROWS, D), bf16), vmem((512, 256), bf16)]
        + [
            vmem((D, 1024), bf16),
            vmem((D, 1024), bf16),
            vmem((D, 512), bf16),
            vmem((D, 512), bf16),
            vmem((D, 1024), bf16),
            vmem((D, 1024), bf16),
            vmem((4, ROWS, D), bf16),
            vmem((2, 2, ROWS, 1024), bf16),
            vmem((2, 2, ROWS, 1024), bf16),
            vmem(rows, bf16),
            vmem((4, BLOCK, HD), bf16),
        ]
        + SUM_BUFFERS
        + sem_pair(SUM_NORM_SEMS)
        + sem_pair(3)
        + [pltpu.SemaphoreType.DMA((7,))]
        + ring_buffers(4, (32, 1024)) * 4
        + sem_pair(4 * RING_SEMS) * 4,
        compiler_params=params(2, vmem=62),
        name="feed",
    )(n2.reshape(rows), cot_all.reshape(rows), middle, cot, gains, first, weights, mixed)


def back_kernel(
    facts,
    q,
    kv,
    o,
    lse,
    do,
    fed_part,
    w_hbm,
    n1_hbm,
    n1_t_hbm,
    grad_out_hbm,
    gains,
    tabs,
    gain_two,
    down_a,
    down_b,
    up_a,
    up_b,
    fed,
    out,
    gain,
    summed,
    down_all,
    up_all,
    *scratch,
):
    acc, dq, dq_low, dkv, inner, total, grads, down_shard, w, n1, n1_t, grad_out, lin, last, side, part = scratch[:16]
    up_shard, shard, side_shard, side_all, mine, theirs = scratch[16:22]
    legs_a, legs_b, side_a, side_b = scratch[22:26]
    key_buffers = scratch[26:29]
    rings = [scratch[29 + 3 * k : 32 + 3 * k] for k in range(8)]
    fed_buffers, sums = scratch[53:59], scratch[59:65]
    sems = [Sems(*scratch[65 + 2 * k : 67 + 2 * k]) for k in range(13)]
    local = scratch[91]
    pairs = [(n1_t_hbm, n1_t), (grad_out_hbm, grad_out), (w_hbm.at[:, pl.ds(0, 768)], w), (n1_hbm, n1)]
    loads = [pltpu.make_async_copy(a, b, local.at[k]) for k, (a, b) in enumerate(pairs)]
    for copy in loads:
        copy.start()
    d, c, m, core, across, copy_of = tensor_place()
    z, z_up, z_down, z_far, to_z_up, to_z_down = ring("z")
    y, y_up, y_down, y_far, to_y_up, to_y_down = ring("y")
    greet([core, across, copy_of, *swap_peers(), to_z_up, to_z_down, {"z": z_far}, to_y_up, to_y_down])

    def step(*plans):
        for plan in plans:
            next(plan, None)

    fed_plan = sum_plan(fed_part, fed, fed_buffers, sems[0])
    feeds = [
        second_leg(down_a, down_shard, "y", 0, rings[4], sems[2]),
        second_leg(down_b, down_shard, "z", 2, rings[5], sems[3]),
        second_leg(up_a, up_shard, "y", 0, rings[6], sems[11]),
        second_leg(up_b, up_shard, "z", 2, rings[7], sems[12]),
    ]
    swap_feed = swap_plan(
        [(lambda q: down_shard.at[q], lambda me: down_all.at[me]), (lambda q: up_shard.at[q], lambda me: up_all.at[me])],
        sems[1],
    )
    keys = collect_plan(dq_low, dkv, grads, total, key_buffers, sems[4])
    step(fed_plan, *feeds)
    for i in range(4):
        value = jnp.sum(o[i] * do[i].astype(f32), -1, keepdims=True)
        inner[i] = jnp.broadcast_to(value, (BLOCK, HD))
    for column in (y_far, y_up, y_down, y):
        for i in (3, 2, 1, 0):
            attend_back_tile(facts, q, kv, do, lse, inner, dq, acc, i, column, column is y_far)
        for k in range(4):
            dkv[k, column, 0] = (acc[k, 0] * scale).astype(bf16)
            dkv[k, column, 1] = acc[k, 1].astype(bf16)
        if column is y:
            dq_low[...] = (dq[...] * scale).astype(bf16)
        step(keys)
        if column is not y_down:
            step(*feeds)
        if column is y_far or column is y:
            step(fed_plan)
    step(swap_feed)
    for copy in loads:
        copy.wait()
    run(keys)

    for block in range(4):
        seq, half = block // 2, block % 2
        for kind in range(3):
            for h in range(2):
                v = grads[2 * seq + h, kind, half * ROWS : (half + 1) * ROWS]
                if kind < 2:
                    v = v.astype(f32)
                    v = (v * tabs[0, block] - pltpu.roll(v, HD // 2, 1) * tabs[1, block]).astype(bf16)
                lin[block * ROWS : (block + 1) * ROWS, (2 * kind + h) * HD : (2 * kind + h + 1) * HD] = v
    blocks = [slice(512 * k, 512 * (k + 1)) for k in range(4)]
    for some in blocks:
        last[some, 0:768] = jnp.dot(n1_t[some], lin[...], preferred_element_type=f32).astype(bf16)
        last[some, 768:1024] = grad_out[some]
    lasts = [
        grads_plan(last, shard, "z", "y", 0, legs_a, rings[0], sems[5], True),
        grads_plan(last, shard, "y", "z", 2, legs_b, rings[1], sems[6], True),
    ]
    step(*lasts)
    hot = one_hot(8, (0, 1))
    for some in blocks:
        p = dot_t(lin[...], w[some])
        part[:, :, :, some] = p.astype(bf16).reshape(2, 2, ROWS, 512)
        gain_one = jnp.sum(p * n1[:, some].astype(f32), 0, keepdims=True) / gains[0:1, some]
        both = jnp.concatenate([gain_one, gain_two[0:1, some], jnp.zeros((6, 512), f32)], 0)
        side[some] = dot_l(both.astype(bf16), hot).astype(bf16)

    def gains_plan():
        halves = [
            grads_plan(side, side_shard, "z", "y", 0, side_a, rings[2], sems[7]),
            grads_plan(side, side_shard, "y", "z", 2, side_b, rings[3], sems[8]),
        ]
        for _ in range(6):
            for half in halves:
                next(half)
            yield
        run(*halves)
        swap = swap_plan([(lambda q: side_shard.at[q], lambda me: side_all.at[me])], sems[1])
        next(swap)
        yield
        run(swap)
        mine[...] = added(side_all[0], side_all[1], side_all[2], side_all[3])
        copy = remote(mine, theirs, *sems[1].take(), copy_of)
        copy.start()
        yield
        copy.wait()
        gain[...] = mine[...] + theirs[...]

    norms = sum_plan(part, summed, sums, sems[9])
    narrow = gains_plan()
    swap_last = swap_plan([(lambda q: shard.at[q], lambda me: out.at[me])], sems[10])
    step(norms, narrow, norms)
    step(*lasts)
    step(*lasts, narrow)
    step(narrow, *lasts, narrow)
    step(norms, *lasts, narrow)
    step(narrow, *lasts, narrow)
    step(narrow, *lasts, swap_last, fed_plan)
    run(narrow, swap_last, norms, *lasts, fed_plan, swap_feed, *feeds)


def back(facts, q, kv, o, lse, do, fed_part, w, n1, n1_t, grad_out, gains, tabs, gain_two, *feeds):
    block, narrow = (32, 1024), (32, HD)
    heads = (4, BLOCK, HD)
    shape, vmem = jax.ShapeDtypeStruct, pltpu.VMEM
    return pl.pallas_call(
        back_kernel,
        out_shape=[
            shape((ROWS, D), f32),
            shape((4, *block), bf16),
            shape(narrow, f32),
            shape((ROWS, D), f32),
            shape((4, *block), bf16),
            shape((4, *block), bf16),
        ],
        in_specs=vmem_specs(7) + [pl.BlockSpec(memory_space=pl.ANY)] * 4 + vmem_specs(7),
        out_specs=vmem_specs(6),
        scratch_shapes=[
            vmem((4, 2, BLOCK, HD), f32),
            vmem(heads, f32),
            vmem(heads, bf16),
            vmem((4, 4, 2, BLOCK, HD), bf16),
            vmem(heads, f32),
            vmem((3, 2, BLOCK, HD), bf16),
            vmem((4, 3, BLOCK, HD), bf16),
            vmem((4, *block), bf16),
            vmem((D, 768), bf16),
            vmem((512, D), bf16),
            vmem((D, 512), bf16),
            vmem((D, 256), bf16),
            vmem((512, 768), bf16),
            vmem((D, 1024), bf16),
            vmem((D, HD), bf16),
            vmem((2, 2, ROWS, D), bf16),
            vmem((4, *block), bf16),
            vmem((4, *block), bf16),
            vmem((4, *narrow), bf16),
            vmem((4, *narrow), bf16),
            vmem(narrow, f32),
            vmem(narrow, f32),
        ]
        + [vmem((4, 2, *block), bf16)] * 2
        + [vmem((4, 2, *narrow), bf16)] * 2
        + ring_buffers(4, (BLOCK, HD))
        + ring_buffers(5, block) * 2
        + ring_buffers(5, narrow) * 2
        + ring_buffers(1, block) * 4
        + SUM_BUFFERS * 2
        + sem_pair(SUM_SEMS)
        + sem_pair(10)
        + sem_pair(RING_SEMS) * 2
        + sem_pair(4 * RING_SEMS + 6)
        + sem_pair(5 * RING_SEMS) * 4
        + sem_pair(SUM_SEMS)
        + sem_pair(3)
        + sem_pair(RING_SEMS) * 2
        + [pltpu.SemaphoreType.DMA((4,))],
        compiler_params=params(6, vmem=62),
        name="back",
    )(facts, q, kv, o, lse, do, fed_part, w, n1, n1_t, grad_out, gains, tabs, gain_two, *feeds)


def finish_kernel(
    *refs,
):
    given, (out, g_in, g_q, g_k, g_v, g_out, g_up, g_down, g_one, g_two), refs = refs[:10], refs[10:20], refs[20:]
    last, grad_down, grad_up, gain, summed, x, grad_middle, gains, middle, fed, total, sems = refs
    loads = [pltpu.make_async_copy(a, b, sems.at[k]) for k, (a, b) in enumerate(zip(given, refs[:10]))]
    for copy in loads:
        copy.start()
    for copy in loads:
        copy.wait()
    total[...] = middle[...] + fed[...]
    to_outer(lambda k: total[:, k * HD : (k + 1) * HD], out, bf16)
    n, rate = norm(x[...].astype(f32))
    total[...] = grad_middle[...] + norm_back(summed[...], n, rate, gains[0:1])
    to_outer(lambda k: total[:, k * HD : (k + 1) * HD], g_in, f32)
    for q in range(4):
        for k, o in enumerate((g_q, g_k, g_v)):
            o[:, q * 256 : (q + 1) * 256] = last[q, :, k * 256 : (k + 1) * 256].astype(f32)
        g_out[:, q * 256 : (q + 1) * 256] = last[q, :, 768:1024].astype(f32)
        g_down[:, q * 1024 : (q + 1) * 1024] = grad_down[q].astype(f32)
        g_up[:, q * 1024 : (q + 1) * 1024] = grad_up[q].astype(f32)
    gain_t = gain[...].T
    g_one[...] = gain_t[0]
    g_two[...] = gain_t[1]


def finish(*args):
    def shape(*dims, kind=f32):
        return jax.ShapeDtypeStruct(dims, kind)

    return pl.pallas_call(
        finish_kernel,
        out_shape=[
            shape(ROWS, D, kind=bf16),
            shape(ROWS, D),
            shape(32, 1024),
            shape(32, 1024),
            shape(32, 1024),
            shape(32, 1024),
            shape(32, 4096),
            shape(32, 4096),
            shape(32),
            shape(32),
        ],
        in_specs=[pl.BlockSpec(memory_space=pl.ANY)] * 10,
        out_specs=vmem_specs(10),
        scratch_shapes=[pltpu.VMEM(a.shape, a.dtype) for a in args]
        + [pltpu.VMEM((ROWS, D), f32), pltpu.SemaphoreType.DMA((10,))],
        compiler_params=params(vmem=60),
        name="finish",
    )(*args)


def local(
    inputs,
    clip_starts,
    pad_lengths,
    w_query,
    w_key,
    w_value,
    w_out,
    w_up,
    w_down,
    gain_first,
    gain_second,
    cotangent,
):
    (
        first,
        x_here,
        incoming,
        tabs,
        normed_one,
        normed_one_t,
        gains,
        facts,
        q,
        kv,
        incoming_all,
        o,
        lse,
        mixed,
        middle,
        normed_two,
        second,
    ) = front(
        w_query,
        w_key,
        w_value,
        w_out.T,
        w_up,
        w_down.T,
        inputs[0],
        cotangent[0],
        gain_first[None],
        gain_second[None],
        clip_starts,
        pad_lengths[None],
    )
    first = first.reshape(D, -1)
    part_out, grad_out, grad_middle, grad_mixed, gain_two, *legs = feed(
        normed_two, incoming_all, middle, incoming, gains, first, second.reshape(D, D), mixed.reshape(512, 256)
    )
    fed, last, gain_grads, summed, grad_down, grad_up = back(
        facts,
        q,
        kv,
        o,
        lse,
        grad_mixed,
        part_out,
        first,
        normed_one,
        normed_one_t,
        grad_out,
        gains,
        tabs,
        gain_two,
        *legs,
    )
    output, grad_input, *rest = finish(
        last, grad_down, grad_up, gain_grads, summed, x_here, grad_middle, gains, middle, fed
    )
    g_query, g_key, g_value, g_out, g_up, g_down, g_one, g_two = rest
    return (output[None], grad_input[None], g_query, g_key, g_value, g_out.T, g_up, g_down.T, g_one, g_two)


def solution(mesh):
    split = Mesh(mesh.devices.reshape(2, 4, 4, 2, 2), ("dp", "z", "y", "c", "mp"))
    seq = ("z", "y", "c")
    weights = ("dp", "z", "y", "c")
    tokens = P("dp", seq, None)
    wide, tall = P(weights, "mp"), P("mp", weights)
    return jax.shard_map(
        local,
        mesh=split,
        in_specs=(tokens, P("dp", None), P("dp"), wide, wide, wide, tall, wide, tall, P(weights), P(weights), tokens),
        out_specs=(tokens, tokens, wide, wide, wide, tall, wide, tall, P(weights), P(weights)),
        check_vma=False,
    )
```

```python
import functools

import jax
import jax.numpy as jnp
from jax import lax
from jax.experimental import pallas as pl
from jax.experimental.pallas import tpu as pltpu
from jax.sharding import Mesh
from jax.sharding import PartitionSpec as P

MESH = pl.DeviceIdType.MESH
HD = 128
FRAME = 32
LEN = 4096
D = 2048
ROWS = 128
BLOCK = 256
ZY = ("z", "y")
epsilon = 1e-05
scale = HD**-0.5
LOG_BASE = 9.210340371976184
f32 = jnp.float32
bf16 = jnp.bfloat16


def params(collective_id=None, vmem=48, **kw):
    if collective_id is not None:
        kw = dict(collective_id=collective_id, has_side_effects=True, **kw)
    return pltpu.CompilerParams(vmem_limit_bytes=vmem * 2**20, **kw)


def vmem_specs(n):
    return [pl.BlockSpec(memory_space=pltpu.VMEM)] * n


def greet(peers):
    barrier = pltpu.get_barrier_semaphore()
    for peer in peers:
        pl.semaphore_signal(barrier, inc=1, device_id=peer, device_id_type=MESH)
    pl.semaphore_wait(barrier, len(peers))


def remote(src, dst, send, recv, peer):
    return pltpu.make_async_remote_copy(
        src_ref=src, dst_ref=dst, send_sem=send, recv_sem=recv, device_id=peer, device_id_type=MESH
    )


def started(copies, src, dst, send, recv, peer):
    copy = remote(src, dst, send, recv, peer)
    copy.start()
    copies.append(copy)
    return copy


class Sems:
    def __init__(self, send, recv):
        self.send, self.recv, self.used = send, recv, 0

    def take(self):
        k = self.used
        self.used += 1
        return self.send.at[k], self.recv.at[k]


def sem_pair(n):
    return [pltpu.SemaphoreType.DMA((n,)), pltpu.SemaphoreType.DMA((n,))]


def tensor_place():
    d, c, m = lax.axis_index("dp"), lax.axis_index("c"), lax.axis_index("mp")
    return d, c, m, {"c": 1 - c}, {"dp": 1 - d, "mp": 1 - m}, {"mp": 1 - m}


def ring(axis, size=4):
    me = lax.axis_index(axis)
    up, down, far = (lax.rem(me + k, size) for k in (1, size - 1, 2))
    return me, up, down, far, {axis: up}, {axis: down}


def added(*values):
    total = values[0].astype(f32)
    for v in values[1:]:
        total = total + v.astype(f32)
    return total


def run(*protocols):
    live = list(protocols)
    while live:
        for p in list(live):
            try:
                next(p)
            except StopIteration:
                live.remove(p)


def swap_plan(pairs, sems):
    d, c = lax.axis_index("dp"), lax.axis_index("c")
    me = 2 * d + c
    copies = []
    for a, b in [(d, 1 - c), (1 - d, c), (1 - d, 1 - c)]:
        for src, dst in pairs:
            started(copies, src(2 * a + b), dst(me), *sems.take(), {"dp": a, "c": b})
    for src, dst in pairs:
        dst(me)[...] = src(me)[...]
    yield
    for copy in copies:
        copy.wait_recv()
    yield
    for copy in copies:
        copy.wait_send()


def quarter(ref):
    wide = ref.shape[1] // 4
    return lambda q: ref.at[:, pl.ds(pl.multiple_of(q * wide, wide), wide)]


class Stores:
    def __init__(self, buffers, outputs, sems):
        self.pairs, self.sems, self.copies = list(zip(buffers, outputs)), sems, []

    def __call__(self, *places):
        for k in places:
            copy = pltpu.make_async_copy(*self.pairs[k], self.sems.at[k])
            copy.start()
            self.copies.append(copy)

    def wait(self):
        for copy in self.copies:
            copy.wait()


def swap_peers():
    d, c = lax.axis_index("dp"), lax.axis_index("c")
    return [{"dp": 1 - d}, {"dp": 1 - d, "c": 1 - c}]


CHUNKS = 4
FINE = 8
HALF = ROWS // 2


def rows_plan(x, o, sems):
    d, c, m, core, across, copy_of = tensor_place()
    me, far = 2 * d + c, 2 * (1 - d) + c
    copies, firsts, seconds = [], [], []
    step = HALF // 2
    mine = [pl.ds(m * HALF + k * step, step) for k in range(2)]
    other = [pl.ds((1 - m) * HALF + k * step, step) for k in range(2)]
    for rows in mine:
        firsts.append(started(copies, x.at[rows], o.at[me, rows], *sems.take(), across))
    near = started(copies, x, o.at[me], *sems.take(), core)
    o[me] = x[...]
    yield
    for k, rows in enumerate(other):
        firsts[k].wait_recv()
        seconds.append(started(copies, o.at[far, rows], o.at[far, rows], *sems.take(), copy_of))
    yield
    lasts = []
    for rows in other:
        lasts.append(started(copies, o.at[far, rows], o.at[far, rows], *sems.take(), core))
    for k, rows in enumerate(mine):
        seconds[k].wait_recv()
        lasts.append(started(copies, o.at[far, rows], o.at[far, rows], *sems.take(), core))
    yield
    near.wait_recv()
    for copy in lasts:
        copy.wait_recv()
    for copy in copies:
        copy.wait_send()


ROWS_SEMS = 9


def sum_plan(x, o, buffers, sems):
    from_core, s_here, s_send, from_across, t_send, from_copy = buffers
    d, c, m, core, across, copy_of = tensor_place()
    step = ROWS // CHUNKS
    rows = [pl.ds(k * step, step) for k in range(CHUNKS)]
    copies, zero, one, two = [], [], [], []
    for r in rows:
        zero.append(started(copies, x.at[:, 1 - c, r], from_core.at[:, r], *sems.take(), core))
    yield
    for k, r in enumerate(rows):
        zero[k].wait_recv()
        s_send[r] = x[1 - d, c, r] + from_core[1 - d, r]
        one.append(started(copies, s_send.at[r], from_across.at[r], *sems.take(), across))
        s_here[r] = x[d, c, r] + from_core[d, r]
    yield
    for k, r in enumerate(rows):
        one[k].wait_recv()
        t_send[r] = s_here[r] + from_across[r]
        two.append(started(copies, t_send.at[r], from_copy.at[r], *sems.take(), copy_of))
    yield
    for k, r in enumerate(rows):
        two[k].wait_recv()
        o[r] = added(t_send[r], from_copy[r])
    for copy in copies:
        copy.wait_send()


SUM_SEMS = 3 * CHUNKS
SUM_BUFFERS = [
    pltpu.VMEM((2, ROWS, D), bf16),
    pltpu.VMEM((ROWS, D), bf16),
    pltpu.VMEM((ROWS, D), bf16),
    pltpu.VMEM((ROWS, D), bf16),
    pltpu.VMEM((ROWS, D), bf16),
    pltpu.VMEM((ROWS, D), bf16),
]


def weights_plan(w, first, second, low, sems):
    i0, i_up, i_down, i_far, to_i_up, to_i_down = ring(first)
    j0, j_up, j_down, j_far, to_j_up, to_j_down = ring(second)

    def at(i, j, part, n):
        return w.at[(j, i) if first == "y" else (i, j)].at[pl.ds(low + part, n)]

    copies = []

    def send(ref, peer):
        return started(copies, ref, ref, *sems.take(), peer)

    def along(i):
        return i, send(at(i, j0, 0, 2), to_j_up), send(at(i, j0, 0, 2), to_j_down)

    from_down, from_up = send(at(i0, j0, 0, 2), to_i_up), send(at(i0, j0, 0, 2), to_i_down)
    second_leg = [along(i0)]
    yield
    from_down.wait_recv()
    far_low = send(at(i_down, j0, 0, 1), to_i_up)
    from_up.wait_recv()
    far_high = send(at(i_up, j0, 1, 1), to_i_down)
    second_leg.append(along(i_down))
    yield
    second_leg.append(along(i_up))
    yield
    onward = []

    def relay(leg):
        i, a, b = leg
        a.wait_recv()
        onward.append(send(at(i, j_down, 0, 1), to_j_up))
        b.wait_recv()
        onward.append(send(at(i, j_up, 1, 1), to_j_down))

    far_low.wait_recv()
    far_high.wait_recv()
    second_leg.append(along(i_far))
    for leg in second_leg:
        yield
        relay(leg)
    yield
    for copy in onward:
        copy.wait_recv()
    for copy in copies:
        copy.wait_send()


WEIGHT_SEMS = 20


def to_inner(x, o):
    for k in range(16):
        low, high = x[:, k * 64 : (k + 1) * 64], x[:, D // 2 + k * 64 : D // 2 + (k + 1) * 64]
        o[:, k * HD : (k + 1) * HD] = jnp.concatenate([low, high], 1)


def to_outer(x, o, kind):
    for k in range(0, 16, 2):
        one, two = x(k), x(k + 1)
        o[:, k * 64 : k * 64 + HD] = jnp.concatenate([one[:, :64], two[:, :64]], 1).astype(kind)
        o[:, D // 2 + k * 64 : D // 2 + k * 64 + HD] = jnp.concatenate([one[:, 64:], two[:, 64:]], 1).astype(kind)


def side_of(one, two, starts, padding):
    lane = lax.broadcasted_iota(jnp.int32, (32, HD), 1)
    same = lax.broadcasted_iota(jnp.int32, (32, 32), 0) == lax.broadcasted_iota(jnp.int32, (32, 32), 1)

    def column(row):
        return jnp.sum(jnp.where(same, row[...].astype(f32), 0.0), 1, keepdims=True)

    value = jnp.where(lane == 0, column(one), 0.0)
    value = jnp.where(lane == 1, column(two), value)
    for k in range(3):
        value = jnp.where(lane == 2 + k, starts[:, k : k + 1].astype(f32), value)
    return jnp.where(lane == 5, padding[...].astype(f32), value).astype(bf16)


def spread_plan(x, q, kv, sems):
    z, z_up, z_down, z_far, to_z_up, to_z_down = ring("z")
    y, y_up, y_down, y_far, to_y_up, to_y_down = ring("y")
    far = {"z": z_far}
    copies, firsts, queries, nears, fars = [], [], [], [], []
    both = pl.ds(1, 2)
    peers = [(z_up, to_z_up, z_down), (z_down, to_z_down, z_up), (z_far, far, z_far)]
    for place, peer, _ in peers:
        firsts.append(started(copies, x.at[place, both], kv.at[z, y], *sems.take(), peer))
    kv[z, y] = x[z, both]

    def along(place):
        ref = kv.at[place, y]
        nears.append(
            (place, started(copies, ref, ref, *sems.take(), to_y_up), started(copies, ref, ref, *sems.take(), to_y_down))
        )

    along(z)
    for place, peer, _ in peers:
        queries.append(started(copies, x.at[place, 0], q.at[z], *sems.take(), peer))
    q[z] = x[z, 0]
    yield
    for k, (_, _, source) in enumerate(peers):
        firsts[k].wait_recv()
        along(source)
        yield
    for copy in queries:
        copy.wait_recv()
    yield
    for place, a, b in nears:
        a.wait_recv()
        ref = kv.at[place, y_down, 0]
        fars.append(started(copies, ref, ref, *sems.take(), to_y_up))
        b.wait_recv()
        ref = kv.at[place, y_up, 1]
        fars.append(started(copies, ref, ref, *sems.take(), to_y_down))
        yield
    for copy in fars:
        copy.wait_recv()
    yield
    for copy in copies:
        copy.wait_send()


def ring_sum(at, axis, buffers, sems, put, late=False):
    one, two, passed = buffers
    me, up, down, far, to_up, to_down = ring(axis)
    copies = []
    a = started(copies, at(far, 0), one.at[0], *sems.take(), to_up)
    b = started(copies, at(far, 1), one.at[1], *sems.take(), to_down)
    if late:
        yield
    plain = [started(copies, at(up, 1), two.at[0, 1], *sems.take(), to_up)]
    if late:
        yield
    plain.append(started(copies, at(down, 0), two.at[1, 0], *sems.take(), to_down))
    if not late:
        yield
    a.wait_recv()
    passed[0] = at(up, 0)[...] + one[0]
    plain.append(started(copies, passed.at[0], two.at[0, 0], *sems.take(), to_up))
    b.wait_recv()
    passed[1] = at(down, 1)[...] + one[1]
    plain.append(started(copies, passed.at[1], two.at[1, 1], *sems.take(), to_down))
    yield
    for copy in plain:
        copy.wait_recv()
    for part in range(2):
        put(part, added(at(me, part)[...], two[0, part], two[1, part]))
    yield
    for copy in copies:
        copy.wait_send()


RING_SEMS = 6


def ring_buffers(n, part):
    return [pltpu.VMEM((n, 2, *part), bf16), pltpu.VMEM((n, 2, 2, *part), bf16), pltpu.VMEM((n, 2, *part), bf16)]


def collect_plan(dq, dkv, o, total, buffers, sems):
    z, peers = z_peers()
    peers = peers + [(z, None)]
    copies, rings = [], []
    for k, (place, peer) in enumerate(peers):

        def at(i, part, place=place):
            return dkv.at[place, i, part]

        def put(part, value, k=k):
            if k < 3:
                total[k, part] = value.astype(bf16)
            else:
                o[z, 1 + part] = value.astype(bf16)

        rings.append(ring_sum(at, "y", [b.at[k] for b in buffers], sems, put, True))
    for _ in range(3):
        for r in rings:
            next(r)
        yield
    for place, peer in peers[:3]:
        started(copies, dq.at[place], o.at[z, 0], *sems.take(), peer)
    o[z, 0] = dq[z]
    for k, r in enumerate(rings):
        next(r)
        if k < 3:
            started(copies, total.at[k], o.at[z, pl.ds(1, 2)], *sems.take(), peers[k][1])
    yield
    for copy in copies:
        copy.wait()
    run(*rings)


def first_leg(g, first, low, legs, buffers, sems, late=False):
    rings = []
    for j in range(4):

        def at(i, part, j=j):
            z, y = (j, i) if first == "y" else (i, j)
            return g.at[pl.ds(pl.multiple_of(((4 * z + y) * 4 + low + part) * 32, 32), 32)]

        def put(part, value, j=j):
            legs[j, part] = value.astype(bf16)

        rings.append(ring_sum(at, first, [b.at[j] for b in buffers], sems, put, late))
    for _ in range(4 if late else 3):
        for r in rings:
            next(r)
        yield
    run(*rings)


def second_leg(legs, shard, second, low, buffers, sems):
    def put(part, value):
        shard[low + part] = value.astype(bf16)

    return ring_sum(lambda i, part: legs.at[i, part], second, [b.at[b.shape[0] - 1] for b in buffers], sems, put)


def grads_plan(g, shard, first, second, low, legs, buffers, sems, late=False):
    leg = first_leg(g, first, low, legs, buffers, sems, late)
    for _ in range(4 if late else 3):
        next(leg)
        yield
    last = second_leg(legs, shard, second, low, buffers, sems)
    for _ in range(3):
        next(last)
        yield
    run(leg, last)


def reach(facts, block, rows):
    t = block * rows + lax.broadcasted_iota(jnp.int32, (rows, 1), 0)
    one, two, three, padding = (facts[:, k : k + 1].astype(jnp.int32) for k in range(2, 6))
    begin = jnp.where(t >= three, three, jnp.where(t >= two, two, one))
    living = t < LEN - padding
    end = jnp.minimum((t // FRAME + 1) * FRAME, LEN - padding)
    return t, begin, jnp.where(living, begin, t), jnp.where(living, end, t + 1)


def dot_t(a, b):
    return lax.dot_general(a, b, (((1,), (1,)), ((), ())), preferred_element_type=f32)


def dot_l(a, b):
    return lax.dot_general(a, b, (((0,), (0,)), ((), ())), preferred_element_type=f32)


def column_scores(facts, q, kv, i, column):
    n = (i + 1) * BLOCK
    _, _, low, high = reach(facts[pl.ds(lax.axis_index("z") // 2, 1)], 4 * i + lax.axis_index("y"), BLOCK)
    k = kv[0 : i + 1, column, 0].reshape(n, HD)
    at = lax.broadcasted_iota(jnp.int32, (1, n), 1)
    at = (at // BLOCK) * (4 * BLOCK) + at % BLOCK + column * BLOCK
    s = dot_t(q[i], k) * scale
    before, own = s[:, : i * BLOCK], s[:, i * BLOCK :]
    here = at[:, i * BLOCK :]
    own = jnp.where((here >= low) & (here < high), own, -1e30)
    if i:
        own = jnp.concatenate([jnp.where(at[:, : i * BLOCK] >= low, before, -1e30), own], 1)
    return k, own


def attend_tile(facts, q, kv, top, total, acc, i, column, first):
    _, s = column_scores(facts, q, kv, i, column)
    v = kv[0 : i + 1, column, 1].reshape((i + 1) * BLOCK, HD)
    now = jnp.max(s, -1, keepdims=True)
    if not first:
        before = top[i][:, :1]
        now = jnp.maximum(before, now)
    p = jnp.exp(s - now)
    plus = jnp.sum(p, -1, keepdims=True)
    out = jnp.dot(p.astype(bf16), v, preferred_element_type=f32)
    if not first:
        shrink = jnp.exp(before - now)
        plus = plus + total[i][:, :1] * shrink
        out = out + acc[i] * shrink
    top[i] = jnp.broadcast_to(now, (BLOCK, HD))
    total[i] = jnp.broadcast_to(plus, (BLOCK, HD))
    acc[i] = out


def attend_back_tile(facts, q, kv, do, lse, inner, dq, acc, i, column, first):
    k, s = column_scores(facts, q, kv, i, column)
    n = i + 1
    v = kv[0:n, column, 1].reshape(n * BLOCK, HD)
    p = jnp.exp(s - lse[i][:, :1])
    ds = (p * (dot_t(do[i], v) - inner[i][:, :1])).astype(bf16)
    dv = dot_l(p.astype(bf16), do[i]).reshape(n, BLOCK, HD)
    dk = dot_l(ds, q[i]).reshape(n, BLOCK, HD)
    part = jnp.dot(ds, k, preferred_element_type=f32)
    if i == 3:
        acc[:, 0], acc[:, 1] = dk, dv
    else:
        acc[0:n, 0] += dk
        acc[0:n, 1] += dv
    dq[i] = part if first else dq[i] + part


def norm(value):
    centre = value - jnp.mean(value, -1, keepdims=True)
    r = lax.rsqrt(jnp.mean(centre * centre, -1, keepdims=True) + epsilon)
    return centre * r, r


def norm_back(grad, n, r, gain):
    e = grad * gain
    return r * (e - jnp.mean(e, -1, keepdims=True) - n * jnp.mean(e * n, -1, keepdims=True))


def one_hot(rows, places):
    at = lax.broadcasted_iota(jnp.int32, (rows, HD), 0)
    lane = lax.broadcasted_iota(jnp.int32, (rows, HD), 1)
    hot = at < 0
    for k, place in enumerate(places):
        hot = hot | ((at == k) & (lane == place))
    return jnp.where(hot, 1.0, 0.0).astype(bf16)


def tables(facts, c):
    block = (4 * lax.axis_index("z") + lax.axis_index("y")) * 2 + c
    t, begin, _, _ = reach(facts, block, ROWS)
    lane = lax.broadcasted_iota(jnp.int32, (1, HD), 1)
    i = jnp.where(lane < HD // 2, lane, lane - HD // 2).astype(f32)
    angles = (t - begin).astype(f32) * jnp.exp(i * (-2.0 * LOG_BASE / HD))
    return jnp.cos(angles), jnp.where(lane < HD // 2, -1.0, 1.0) * jnp.sin(angles)


def sum_norm_plan(x, produce, all_rows, make, buffers, sems, idle=lambda: None):
    from_core, s_here, s_send, from_across, t_send, from_copy = buffers
    d, c, m, core, across, copy_of = tensor_place()
    me, far = 2 * d + c, 2 * (1 - d) + c
    step = ROWS // FINE
    rows = [pl.ds(k * step, step) for k in range(FINE)]
    halves = [pl.ds(pl.multiple_of(k * (D // 2), D // 2), D // 2) for k in (m, 1 - m)]
    copies, zero, one, two = [], [], [], []
    for h in range(2):
        produce(h)
        for r in rows[FINE // 2 * h : FINE // 2 * (h + 1)]:
            zero.append(started(copies, x.at[:, 1 - c, r], from_core.at[:, r], *sems.take(), core))
        for k in range(FINE // 2 * h, FINE // 2 * (h + 1)):
            r = rows[k]
            zero[k].wait_recv()
            s_send[r] = x[1 - d, c, r] + from_core[1 - d, r]
            one.append(started(copies, s_send.at[r], from_across.at[r], *sems.take(), across))
            s_here[r] = x[d, c, r] + from_core[d, r]
    idle()
    for k, r in enumerate(rows):
        if k % 2 == 0:
            idle()
        one[k].wait_recv()
        t_send[r] = s_here[r] + from_across[r]
        two.append(started(copies, t_send.at[r], from_copy.at[r], *sems.take(), copy_of))
    yield
    nears, firsts, seconds, lasts = [], [], [], []
    idle()
    for k, r in enumerate(rows):
        if k % 2 == 0:
            idle()
        two[k].wait_recv()
        all_rows[me, r] = make(r, added(t_send[r], from_copy[r])).astype(bf16)
        nears.append(started(copies, all_rows.at[me, r], all_rows.at[me, r], *sems.take(), core))
        ref = all_rows.at[me, r, halves[0]]
        firsts.append(started(copies, ref, ref, *sems.take(), across))
    yield

    def onward(r, half, peer):
        ref = all_rows.at[far, r, half]
        return started(copies, ref, ref, *sems.take(), peer)

    idle()
    for k, r in enumerate(rows):
        if k % 2 == 0:
            idle()
        firsts[k].wait_recv()
        seconds.append(onward(r, halves[1], copy_of))
        lasts.append(onward(r, halves[1], core))
    yield
    idle()
    for k, r in enumerate(rows):
        if k % 2 == 0:
            idle()
        seconds[k].wait_recv()
        lasts.append(onward(r, halves[0], core))
    yield
    for copy in nears + lasts:
        copy.wait_recv()
    yield
    for copy in copies:
        copy.wait_send()


SUM_NORM_SEMS = 8 * FINE
OUT_COLUMNS = pl.BlockSpec((D, 256), lambda i: (0, 3))


def z_peers():
    z, z_up, z_down, z_far, to_z_up, to_z_down = ring("z")
    return z, [(z_up, to_z_up), (z_down, to_z_down), (z_far, {"z": z_far})]


def front_kernel(
    wq,
    wk,
    wv,
    wo,
    wu,
    wd,
    x_hbm,
    cot_hbm,
    one,
    two,
    starts,
    padding,
    w_hbm,
    *scratch,
):
    outputs, weights_hbm, scratch = scratch[:15], scratch[15], scratch[16:]
    x_here, cot, tabs, n1, n1_t, gains, facts, q, kv, rows, o, lse, mixed, middle, n2 = scratch[:15]
    keep = Stores(scratch[:15], outputs, scratch[15])
    scratch = scratch[16:]
    w, weights, qkv, top, total, acc, low, turned, part, x_raw, cot_raw, side, x, lin = scratch[:14]
    sums, scratch = scratch[14:20], scratch[20:]
    local = scratch[0]
    sems = [Sems(*scratch[1 + 2 * k : 3 + 2 * k]) for k in range(10)]
    keys_sems, rows_sems, norm_sems, turn_sems, leg_a, leg_b, swaps, x_sems, first_a, first_b = sems
    d, c = lax.axis_index("dp"), lax.axis_index("c")
    me = 2 * d + c
    z, peers = z_peers()
    y, up, down, far, y_up, y_down = ring("y")
    here, there = w.at[z, y, me], weights.at[z, y, me]
    firsts = [(wq, 0, 256), (wk, 256, 256), (wv, 512, 256), (wo, 768, 256)]
    rests = [(wu, 0, 1024), (wd, 1024, 1024)]
    loads = [pltpu.make_async_copy(x_hbm, x_raw, local.at[0]), pltpu.make_async_copy(cot_hbm, cot_raw, local.at[1])]
    for k, (src, left, n) in enumerate(firsts):
        loads.append(pltpu.make_async_copy(quarter(src)(me), here.at[:, pl.ds(left, n)], local.at[2 + k]))
    for k, (src, left, n) in enumerate(rests):
        loads.append(pltpu.make_async_copy(quarter(src)(me), there.at[:, pl.ds(left, n)], local.at[6 + k]))
    for copy in loads:
        copy.start()
    side[...] = side_of(one, two, starts, padding)
    here[:, 1024:1152] = side[...]
    greet([*tensor_place()[3:], *swap_peers(), *[peer for _, peer in peers], y_up, y_down])

    def swap(pairs, dst):
        copies = []
        for a, b in [(d, 1 - c), (1 - d, c), (1 - d, 1 - c)]:
            for src, left, n in pairs:
                started(copies, src(2 * a + b), dst.at[:, pl.ds(left, n)], *swaps.take(), {"dp": a, "c": b})
        return copies

    swap_first = swap([(quarter(src), left, n) for src, left, n in firsts] + [(lambda q: side, 1024, HD)], here)
    loads[0].wait()
    to_inner(x_raw, x_here)
    gather_x = rows_plan(x_here, x, x_sems)
    next(gather_x)
    for copy in loads[2:6]:
        copy.wait()
    for copy in swap_first:
        copy.wait_recv()
    legs = [weights_plan(w, "y", "z", 0, first_a), weights_plan(w, "z", "y", 2, first_b)]
    for leg in legs:
        next(leg)
    swap_rest = swap([(quarter(src), left, n) for src, left, n in rests], there)
    for seq in range(2):
        fact = w[z, y, 2 * seq, 0:1, 1024:1152].astype(f32)
        for half in range(2):
            tabs[0, 2 * seq + half], tabs[1, 2 * seq + half] = tables(fact, half)
    loads[1].wait()
    to_inner(cot_raw, cot)
    run(*legs, gather_x)
    store = pltpu.make_async_copy(w, w_hbm, local.at[8])
    store.start()
    keep(0, 1, 2)
    for copy in loads[6:] + swap_rest:
        copy.wait()
    for copy in swap_first:
        copy.wait_send()

    def columns(left, right):
        return w[:, :, :, :, left:right].reshape(D, right - left)

    gather = rows_plan(cot, rows, rows_sems)
    next(gather)
    legs = [weights_plan(weights, "y", "z", 0, leg_a), weights_plan(weights, "z", "y", 2, leg_b)]

    def leg_step():
        for leg in legs:
            next(leg, None)

    leg_step()
    side = columns(1024, 1152)
    gains[...] = dot_t(one_hot(8, (0, 1)), side)
    facts[...] = jnp.zeros_like(facts)
    facts[0:1] = side[0:1].astype(f32)
    facts[1:2] = side[64:65].astype(f32)
    for block in range(4):
        r = pl.ds(block * ROWS, ROWS)
        n1[r] = (norm(x[block].astype(f32))[0] * gains[0:1]).astype(bf16)
    lin[...] = jnp.dot(n1[...], columns(0, 768), preferred_element_type=f32)
    for block in range(4):
        seq, half = block // 2, block % 2
        r = pl.ds(block * ROWS, ROWS)
        for kind in range(3):
            for h in range(2):
                v = lin[r, (2 * kind + h) * HD : (2 * kind + h + 1) * HD]
                if kind < 2:
                    v = v * tabs[0, block] + pltpu.roll(v, HD // 2, 1) * tabs[1, block]
                qkv[2 * seq + h, kind, half * ROWS : (half + 1) * ROWS] = v.astype(bf16)
    keys = spread_plan(qkv, q, kv, keys_sems)
    keep(3, 5, 6)

    def work():
        for k in range(4):
            some = slice(512 * k, 512 * (k + 1))
            n1_t[some] = n1[:, some].T
            yield
        for i in range(4):
            attend_tile(facts, q, kv, top, total, acc, i, y, True)
            yield

    pieces = work()
    next(keys)
    next(gather)
    for _ in range(4):
        next(pieces)
        next(keys)
    next(gather)
    for _ in range(4):
        next(pieces)
        next(keys)
    next(gather, None)
    leg_step()
    for column in (down, up):
        for i in range(4):
            attend_tile(facts, q, kv, top, total, acc, i, column, False)
    run(keys, gather)
    keep(4, 7, 8, 9)
    for i in range(4):
        attend_tile(facts, q, kv, top, total, acc, i, far, False)
    for i in range(4):
        low[i] = (acc[i] / total[i]).astype(bf16)
    copies = []
    for place, peer in peers:
        started(copies, low.at[place], turned.at[z], *turn_sems.take(), peer)
    turned[z] = low[z]
    for i in range(4):
        o[i] = acc[i] / total[i]
        lse[i] = top[i] + jnp.log(total[i])
    keep(10, 11)
    leg_step()
    for copy in copies:
        copy.wait()
    for seq in range(2):
        for h in range(2):
            mixed[seq, :, :, h * HD : (h + 1) * HD] = turned[2 * seq + h].reshape(2, ROWS, HD)
    keep(12)

    def partial(h):
        r = slice(HALF * h, HALF * (h + 1))
        value = dot_t(mixed[:, :, r].reshape(2 * ROWS, 256), columns(768, 1024))
        part[:, :, r] = value.astype(bf16).reshape(2, 2, HALF, D)

    def make(r, value):
        value = x_here[r].astype(f32) + value
        middle[r] = value
        return norm(value)[0] * gains[1:2]

    def legs_work():
        for pause in (0, 0, 0, 2, 5, 3):
            for _ in range(pause):
                yield
            if pause != 3:
                leg_step()
        yield
        run(*legs)
        pltpu.make_async_copy(weights, weights_hbm, local.at[9]).start()
        yield

    rest = legs_work()
    run(sum_norm_plan(part, partial, n2, make, sums, norm_sems, lambda: next(rest, None)))
    keep(13, 14)
    for _ in rest:
        pass
    keep.wait()
    pltpu.make_async_copy(weights, weights_hbm, local.at[9]).wait()
    store.wait()


def front(*args):
    block = (4, BLOCK, HD)
    shape = jax.ShapeDtypeStruct
    anywhere = pl.BlockSpec(memory_space=pl.ANY)
    whole = lambda *dims: pl.BlockSpec(dims, lambda i: (0,) * len(dims))
    first, second = (4, 4, 4, 32, 1152), (4, 4, 4, 32, 2048)
    kept = [
        shape((ROWS, D), bf16),
        shape((ROWS, D), bf16),
        shape((2, 4, ROWS, HD), f32),
        shape((512, D), bf16),
        shape((D, 512), bf16),
        shape((8, D), f32),
        shape((8, HD), f32),
        shape(block, bf16),
        shape((4, 4, 2, BLOCK, HD), bf16),
        shape((4, ROWS, D), bf16),
        shape(block, f32),
        shape(block, f32),
        shape((2, 2, ROWS, 256), bf16),
        shape((ROWS, D), f32),
        shape((4, ROWS, D), bf16),
    ]
    return pl.pallas_call(
        front_kernel,
        grid=(1,),
        out_shape=[shape(first, bf16), *kept, shape(second, bf16)],
        in_specs=[anywhere] * 8 + [whole(1, 32), whole(1, 32), whole(1, 3), whole(1, 1)],
        out_specs=[anywhere] * 17,
        scratch_shapes=[pltpu.VMEM(a.shape, a.dtype) for a in kept]
        + [pltpu.SemaphoreType.DMA((15,))]
        + [
            pltpu.VMEM(first, bf16),
            pltpu.VMEM(second, bf16),
            pltpu.VMEM((4, 3, BLOCK, HD), bf16),
        ]
        + [pltpu.VMEM(block, f32)] * 3
        + [pltpu.VMEM(block, bf16)] * 2
        + [pltpu.VMEM((2, 2, ROWS, D), bf16)]
        + [pltpu.VMEM((ROWS, D), bf16)] * 2
        + [pltpu.VMEM((32, HD), bf16), pltpu.VMEM((4, ROWS, D), bf16), pltpu.VMEM((512, 768), f32)]
        + SUM_BUFFERS
        + [pltpu.SemaphoreType.DMA((10,))]
        + sem_pair(22)
        + sem_pair(ROWS_SEMS)
        + sem_pair(SUM_NORM_SEMS)
        + sem_pair(3)
        + sem_pair(WEIGHT_SEMS) * 2
        + sem_pair(21)
        + sem_pair(ROWS_SEMS)
        + sem_pair(WEIGHT_SEMS) * 2,
        compiler_params=params(4, vmem=60),
        name="front",
    )(*args)


def feed_kernel(n2_hbm, cot_all_hbm, middle_hbm, cot_hbm, gains, w, weights, mixed_hbm, *scratch):
    outputs, scratch = scratch[:9], scratch[9:]
    fed, grad_out, grad_middle, turned, gain_two, down_a, down_b, up_a, up_b = scratch[:9]
    keep = Stores(scratch[:9], outputs, scratch[9])
    n2, cot_all, middle, cot, mixed = scratch[10:15]
    up, down, n2_t, cot_t, grads_down, grads_up, branch, active, grad_hidden, part, grad_mixed = scratch[15:26]
    scratch = scratch[26:]
    z, peers = z_peers()
    local = scratch[10]
    _, _, _, _, z_up, z_down = ring("z")
    _, _, _, _, y_up, y_down = ring("y")
    loads = [
        pltpu.make_async_copy(cot_all_hbm, cot_all, local.at[0]),
        pltpu.make_async_copy(weights.at[:, pl.ds(1024, 1024)], down, local.at[1]),
        pltpu.make_async_copy(n2_hbm, n2, local.at[2]),
        pltpu.make_async_copy(weights.at[:, pl.ds(0, 1024)], up, local.at[3]),
        pltpu.make_async_copy(middle_hbm, middle, local.at[4]),
        pltpu.make_async_copy(cot_hbm, cot, local.at[5]),
        pltpu.make_async_copy(mixed_hbm, mixed, local.at[6]),
    ]
    for copy in loads:
        copy.start()
    gain_two[...] = jnp.zeros_like(gain_two)
    greet([*tensor_place()[3:], *[peer for _, peer in peers], y_up, y_down])
    loads[0].wait()
    for k in range(4):
        some = slice(512 * k, 512 * (k + 1))
        cot_t[some] = cot_all[:, :, :, some].reshape(512, 512).T
    for copy in loads[1:]:
        copy.wait()

    def activate(h):
        rows = slice(HALF * h, HALF * (h + 1))
        n = n2[:, :, rows].reshape(2 * ROWS, D)
        g = cot_all[:, :, rows].reshape(2 * ROWS, D)
        for j in range(4):
            some = slice(256 * j, 256 * (j + 1))
            grad_active = jnp.dot(g, down[:, some], preferred_element_type=f32)
            hidden = jnp.dot(n, up[:, some], preferred_element_type=f32)
            half = 0.5 * (1.0 + lax.erf(hidden * 0.5**0.5))
            slope = half + hidden * jnp.exp(-0.5 * hidden * hidden) * (0.5 / jnp.pi) ** 0.5
            active[:, :, rows, some] = (hidden * half).astype(bf16).reshape(2, 2, HALF, 256)
            grad_hidden[:, :, rows, some] = (grad_active * slope).astype(bf16).reshape(2, 2, HALF, 256)

    def partial(h):
        activate(h)
        if h == 1:
            for j in range(4):
                down_piece(j)
            step(downs)
        rows = slice(HALF * h, HALF * (h + 1))
        value = grad_hidden[:, :, rows].reshape(2 * ROWS, 1024)
        for k in range(4):
            some = slice(512 * k, 512 * (k + 1))
            part[:, :, rows, some] = dot_t(value, up[some]).astype(bf16).reshape(2, 2, HALF, 512)

    downs = [
        first_leg(grads_down, "z", 0, down_a, scratch[11:14], Sems(*scratch[23:25])),
        first_leg(grads_down, "y", 2, down_b, scratch[14:17], Sems(*scratch[25:27])),
    ]
    ups = [
        first_leg(grads_up, "z", 0, up_a, scratch[17:20], Sems(*scratch[27:29])),
        first_leg(grads_up, "y", 2, up_b, scratch[20:23], Sems(*scratch[29:31])),
    ]

    def turn_n2(k):
        some = slice(512 * k, 512 * (k + 1))
        n2_t[some] = n2[:, :, :, some].reshape(512, 512).T

    def down_piece(j):
        some = slice(256 * j, 256 * (j + 1))
        value = active[:, :, :, some].reshape(512, 256)
        grads_down[:, some] = jnp.dot(cot_t[...], value, preferred_element_type=f32).astype(bf16)

    def up_piece(j):
        some = slice(256 * j, 256 * (j + 1))
        value = grad_hidden[:, :, :, some].reshape(512, 256)
        grads_up[:, some] = jnp.dot(n2_t[...], value, preferred_element_type=f32).astype(bf16)

    def fed_piece(k):
        some = slice(512 * k, 512 * (k + 1))
        value = dot_t(active[...].reshape(512, 1024), down[some])
        fed[:, :, :, some] = value.astype(bf16).reshape(2, 2, ROWS, 512)

    def step(plans):
        for plan in plans:
            next(plan, None)

    def work():
        for k in range(4):
            turn_n2(k)
        yield
        for j in range(4):
            up_piece(j)
            if j == 3:
                step(ups)
            yield
        step(downs)
        yield
        for k in range(4):
            fed_piece(k)
            if k == 3:
                keep(0)
            yield
        step(ups)
        yield

    pieces = work()

    def make(r, total):
        n, rate = norm(middle[r])
        gain_two[0:1] += 0.5 * jnp.sum(total * n, 0, keepdims=True)
        value = cot[r].astype(f32) + norm_back(total, n, rate, gains[1:2])
        grad_middle[r] = value
        return value

    run(sum_norm_plan(part, partial, branch, make, scratch[:6], Sems(*scratch[6:8]), lambda: next(pieces, None)))
    for k in range(4):
        value = jnp.dot(branch[k], w[...], preferred_element_type=f32).astype(bf16)
        for h in range(2):
            grad_mixed[2 * (k // 2) + h, (k % 2) * ROWS : (k % 2 + 1) * ROWS] = value[:, h * HD : (h + 1) * HD]
    turns, copies = Sems(*scratch[8:10]), []
    for place, peer in peers:
        started(copies, grad_mixed.at[place], turned.at[z], *turns.take(), peer)
    turned[z] = grad_mixed[z]
    for _ in pieces:
        pass
    keep(2, 4)
    for k in range(4):
        some = slice(512 * k, 512 * (k + 1))
        grad_out[some] = dot_l(branch[:, :, some].reshape(512, 512), mixed[...]).astype(bf16)
    keep(1)
    for copy in copies:
        copy.wait()
    keep(3)
    run(*downs, *ups)
    keep(5, 6, 7, 8)
    keep.wait()


def feed(n2, cot_all, middle, cot, gains, first, weights, mixed):
    anywhere = pl.BlockSpec(memory_space=pl.ANY)
    rows = (2, 2, ROWS, D)
    shape, vmem = jax.ShapeDtypeStruct, pltpu.VMEM
    kept = [
        shape(rows, bf16),
        shape((D, 256), bf16),
        shape((ROWS, D), f32),
        shape((4, BLOCK, HD), bf16),
        shape((8, D), f32),
    ] + [shape((4, 2, 32, 1024), bf16)] * 4
    return pl.pallas_call(
        feed_kernel,
        grid=(1,),
        out_shape=kept,
        in_specs=[anywhere] * 4 + vmem_specs(1) + [OUT_COLUMNS] + [anywhere] * 2,
        out_specs=[anywhere] * 9,
        scratch_shapes=[vmem(a.shape, a.dtype) for a in kept]
        + [pltpu.SemaphoreType.DMA((9,))]
        + [vmem(rows, bf16), vmem(rows, bf16), vmem((ROWS, D), f32), vmem((ROWS, D), bf16), vmem((512, 256), bf16)]
        + [
            vmem((D, 1024), bf16),
            vmem((D, 1024), bf16),
            vmem((D, 512), bf16),
            vmem((D, 512), bf16),
            vmem((D, 1024), bf16),
            vmem((D, 1024), bf16),
            vmem((4, ROWS, D), bf16),
            vmem((2, 2, ROWS, 1024), bf16),
            vmem((2, 2, ROWS, 1024), bf16),
            vmem(rows, bf16),
            vmem((4, BLOCK, HD), bf16),
        ]
        + SUM_BUFFERS
        + sem_pair(SUM_NORM_SEMS)
        + sem_pair(3)
        + [pltpu.SemaphoreType.DMA((7,))]
        + ring_buffers(4, (32, 1024)) * 4
        + sem_pair(4 * RING_SEMS) * 4,
        compiler_params=params(2, vmem=62),
        name="feed",
    )(n2.reshape(rows), cot_all.reshape(rows), middle, cot, gains, first, weights, mixed)


def back_kernel(
    facts,
    q,
    kv,
    o,
    lse,
    do,
    fed_part,
    w_hbm,
    n1_hbm,
    n1_t_hbm,
    grad_out_hbm,
    gains,
    tabs,
    gain_two,
    down_a,
    down_b,
    up_a,
    up_b,
    fed,
    out,
    gain,
    summed,
    down_all,
    up_all,
    *scratch,
):
    acc, dq, dq_low, dkv, inner, total, grads, down_shard, w, n1, n1_t, grad_out, lin, last, side, part = scratch[:16]
    up_shard, shard, side_shard, side_all, mine, theirs = scratch[16:22]
    legs_a, legs_b, side_a, side_b = scratch[22:26]
    key_buffers = scratch[26:29]
    rings = [scratch[29 + 3 * k : 32 + 3 * k] for k in range(8)]
    fed_buffers, sums = scratch[53:59], scratch[59:65]
    sems = [Sems(*scratch[65 + 2 * k : 67 + 2 * k]) for k in range(13)]
    local = scratch[91]
    pairs = [(n1_t_hbm, n1_t), (grad_out_hbm, grad_out), (w_hbm.at[:, pl.ds(0, 768)], w), (n1_hbm, n1)]
    loads = [pltpu.make_async_copy(a, b, local.at[k]) for k, (a, b) in enumerate(pairs)]
    for copy in loads:
        copy.start()
    d, c, m, core, across, copy_of = tensor_place()
    z, z_up, z_down, z_far, to_z_up, to_z_down = ring("z")
    y, y_up, y_down, y_far, to_y_up, to_y_down = ring("y")
    greet([core, across, copy_of, *swap_peers(), to_z_up, to_z_down, {"z": z_far}, to_y_up, to_y_down])

    def step(*plans):
        for plan in plans:
            next(plan, None)

    fed_plan = sum_plan(fed_part, fed, fed_buffers, sems[0])
    feeds = [
        second_leg(down_a, down_shard, "y", 0, rings[4], sems[2]),
        second_leg(down_b, down_shard, "z", 2, rings[5], sems[3]),
        second_leg(up_a, up_shard, "y", 0, rings[6], sems[11]),
        second_leg(up_b, up_shard, "z", 2, rings[7], sems[12]),
    ]
    swap_feed = swap_plan(
        [(lambda q: down_shard.at[q], lambda me: down_all.at[me]), (lambda q: up_shard.at[q], lambda me: up_all.at[me])],
        sems[1],
    )
    keys = collect_plan(dq_low, dkv, grads, total, key_buffers, sems[4])
    step(fed_plan, *feeds)
    for i in range(4):
        value = jnp.sum(o[i] * do[i].astype(f32), -1, keepdims=True)
        inner[i] = jnp.broadcast_to(value, (BLOCK, HD))
    for column in (y_far, y_up, y_down, y):
        for i in (3, 2, 1, 0):
            attend_back_tile(facts, q, kv, do, lse, inner, dq, acc, i, column, column is y_far)
        for k in range(4):
            dkv[k, column, 0] = (acc[k, 0] * scale).astype(bf16)
            dkv[k, column, 1] = acc[k, 1].astype(bf16)
        if column is y:
            dq_low[...] = (dq[...] * scale).astype(bf16)
        step(keys)
        if column is y_far or column is y:
            step(fed_plan)
    step(*feeds)
    for copy in loads:
        copy.wait()
    run(keys)
    step(*feeds, swap_feed)

    for block in range(4):
        seq, half = block // 2, block % 2
        for kind in range(3):
            for h in range(2):
                v = grads[2 * seq + h, kind, half * ROWS : (half + 1) * ROWS]
                if kind < 2:
                    v = v.astype(f32)
                    v = (v * tabs[0, block] - pltpu.roll(v, HD // 2, 1) * tabs[1, block]).astype(bf16)
                lin[block * ROWS : (block + 1) * ROWS, (2 * kind + h) * HD : (2 * kind + h + 1) * HD] = v
    blocks = [slice(512 * k, 512 * (k + 1)) for k in range(4)]
    for some in blocks:
        last[some, 0:768] = jnp.dot(n1_t[some], lin[...], preferred_element_type=f32).astype(bf16)
        last[some, 768:1024] = grad_out[some]
    lasts = [
        grads_plan(last, shard, "z", "y", 0, legs_a, rings[0], sems[5], True),
        grads_plan(last, shard, "y", "z", 2, legs_b, rings[1], sems[6], True),
    ]
    step(*lasts)
    hot = one_hot(8, (0, 1))
    for some in blocks:
        p = dot_t(lin[...], w[some])
        part[:, :, :, some] = p.astype(bf16).reshape(2, 2, ROWS, 512)
        gain_one = jnp.sum(p * n1[:, some].astype(f32), 0, keepdims=True) / gains[0:1, some]
        both = jnp.concatenate([gain_one, gain_two[0:1, some], jnp.zeros((6, 512), f32)], 0)
        side[some] = dot_l(both.astype(bf16), hot).astype(bf16)

    def gains_plan():
        halves = [
            grads_plan(side, side_shard, "z", "y", 0, side_a, rings[2], sems[7]),
            grads_plan(side, side_shard, "y", "z", 2, side_b, rings[3], sems[8]),
        ]
        for _ in range(6):
            for half in halves:
                next(half)
            yield
        run(*halves)
        swap = swap_plan([(lambda q: side_shard.at[q], lambda me: side_all.at[me])], sems[1])
        next(swap)
        yield
        run(swap)
        mine[...] = added(side_all[0], side_all[1], side_all[2], side_all[3])
        copy = remote(mine, theirs, *sems[1].take(), copy_of)
        copy.start()
        yield
        copy.wait()
        gain[...] = mine[...] + theirs[...]

    norms = sum_plan(part, summed, sums, sems[9])
    narrow = gains_plan()
    swap_last = swap_plan([(lambda q: shard.at[q], lambda me: out.at[me])], sems[10])
    step(norms, narrow, norms)
    step(*lasts)
    step(*lasts, narrow)
    step(narrow, *lasts, narrow)
    step(norms, *lasts, narrow)
    step(narrow, *lasts, narrow)
    step(narrow, *lasts, swap_last, fed_plan)
    run(narrow, swap_last, norms, *lasts, fed_plan, swap_feed, *feeds)


def back(facts, q, kv, o, lse, do, fed_part, w, n1, n1_t, grad_out, gains, tabs, gain_two, *feeds):
    block, narrow = (32, 1024), (32, HD)
    heads = (4, BLOCK, HD)
    shape, vmem = jax.ShapeDtypeStruct, pltpu.VMEM
    return pl.pallas_call(
        back_kernel,
        out_shape=[
            shape((ROWS, D), f32),
            shape((4, *block), bf16),
            shape(narrow, f32),
            shape((ROWS, D), f32),
            shape((4, *block), bf16),
            shape((4, *block), bf16),
        ],
        in_specs=vmem_specs(7) + [pl.BlockSpec(memory_space=pl.ANY)] * 4 + vmem_specs(7),
        out_specs=vmem_specs(6),
        scratch_shapes=[
            vmem((4, 2, BLOCK, HD), f32),
            vmem(heads, f32),
            vmem(heads, bf16),
            vmem((4, 4, 2, BLOCK, HD), bf16),
            vmem(heads, f32),
            vmem((3, 2, BLOCK, HD), bf16),
            vmem((4, 3, BLOCK, HD), bf16),
            vmem((4, *block), bf16),
            vmem((D, 768), bf16),
            vmem((512, D), bf16),
            vmem((D, 512), bf16),
            vmem((D, 256), bf16),
            vmem((512, 768), bf16),
            vmem((D, 1024), bf16),
            vmem((D, HD), bf16),
            vmem((2, 2, ROWS, D), bf16),
            vmem((4, *block), bf16),
            vmem((4, *block), bf16),
            vmem((4, *narrow), bf16),
            vmem((4, *narrow), bf16),
            vmem(narrow, f32),
            vmem(narrow, f32),
        ]
        + [vmem((4, 2, *block), bf16)] * 2
        + [vmem((4, 2, *narrow), bf16)] * 2
        + ring_buffers(4, (BLOCK, HD))
        + ring_buffers(5, block) * 2
        + ring_buffers(5, narrow) * 2
        + ring_buffers(1, block) * 4
        + SUM_BUFFERS * 2
        + sem_pair(SUM_SEMS)
        + sem_pair(10)
        + sem_pair(RING_SEMS) * 2
        + sem_pair(4 * RING_SEMS + 6)
        + sem_pair(5 * RING_SEMS) * 4
        + sem_pair(SUM_SEMS)
        + sem_pair(3)
        + sem_pair(RING_SEMS) * 2
        + [pltpu.SemaphoreType.DMA((4,))],
        compiler_params=params(6, vmem=62),
        name="back",
    )(facts, q, kv, o, lse, do, fed_part, w, n1, n1_t, grad_out, gains, tabs, gain_two, *feeds)


def finish_kernel(
    *refs,
):
    given, (out, g_in, g_q, g_k, g_v, g_out, g_up, g_down, g_one, g_two), refs = refs[:10], refs[10:20], refs[20:]
    last, grad_down, grad_up, gain, summed, x, grad_middle, gains, middle, fed, total, sems = refs
    loads = [pltpu.make_async_copy(a, b, sems.at[k]) for k, (a, b) in enumerate(zip(given, refs[:10]))]
    for copy in loads:
        copy.start()
    for copy in loads:
        copy.wait()
    total[...] = middle[...] + fed[...]
    to_outer(lambda k: total[:, k * HD : (k + 1) * HD], out, bf16)
    n, rate = norm(x[...].astype(f32))
    total[...] = grad_middle[...] + norm_back(summed[...], n, rate, gains[0:1])
    to_outer(lambda k: total[:, k * HD : (k + 1) * HD], g_in, f32)
    for q in range(4):
        for k, o in enumerate((g_q, g_k, g_v)):
            o[:, q * 256 : (q + 1) * 256] = last[q, :, k * 256 : (k + 1) * 256].astype(f32)
        g_out[:, q * 256 : (q + 1) * 256] = last[q, :, 768:1024].astype(f32)
        g_down[:, q * 1024 : (q + 1) * 1024] = grad_down[q].astype(f32)
        g_up[:, q * 1024 : (q + 1) * 1024] = grad_up[q].astype(f32)
    gain_t = gain[...].T
    g_one[...] = gain_t[0]
    g_two[...] = gain_t[1]


def finish(*args):
    def shape(*dims, kind=f32):
        return jax.ShapeDtypeStruct(dims, kind)

    return pl.pallas_call(
        finish_kernel,
        out_shape=[
            shape(ROWS, D, kind=bf16),
            shape(ROWS, D),
            shape(32, 1024),
            shape(32, 1024),
            shape(32, 1024),
            shape(32, 1024),
            shape(32, 4096),
            shape(32, 4096),
            shape(32),
            shape(32),
        ],
        in_specs=[pl.BlockSpec(memory_space=pl.ANY)] * 10,
        out_specs=vmem_specs(10),
        scratch_shapes=[pltpu.VMEM(a.shape, a.dtype) for a in args]
        + [pltpu.VMEM((ROWS, D), f32), pltpu.SemaphoreType.DMA((10,))],
        compiler_params=params(vmem=60),
        name="finish",
    )(*args)


def local(
    inputs,
    clip_starts,
    pad_lengths,
    w_query,
    w_key,
    w_value,
    w_out,
    w_up,
    w_down,
    gain_first,
    gain_second,
    cotangent,
):
    (
        first,
        x_here,
        incoming,
        tabs,
        normed_one,
        normed_one_t,
        gains,
        facts,
        q,
        kv,
        incoming_all,
        o,
        lse,
        mixed,
        middle,
        normed_two,
        second,
    ) = front(
        w_query,
        w_key,
        w_value,
        w_out.T,
        w_up,
        w_down.T,
        inputs[0],
        cotangent[0],
        gain_first[None],
        gain_second[None],
        clip_starts,
        pad_lengths[None],
    )
    first = first.reshape(D, -1)
    part_out, grad_out, grad_middle, grad_mixed, gain_two, *legs = feed(
        normed_two, incoming_all, middle, incoming, gains, first, second.reshape(D, D), mixed.reshape(512, 256)
    )
    fed, last, gain_grads, summed, grad_down, grad_up = back(
        facts,
        q,
        kv,
        o,
        lse,
        grad_mixed,
        part_out,
        first,
        normed_one,
        normed_one_t,
        grad_out,
        gains,
        tabs,
        gain_two,
        *legs,
    )
    output, grad_input, *rest = finish(
        last, grad_down, grad_up, gain_grads, summed, x_here, grad_middle, gains, middle, fed
    )
    g_query, g_key, g_value, g_out, g_up, g_down, g_one, g_two = rest
    return (output[None], grad_input[None], g_query, g_key, g_value, g_out.T, g_up, g_down.T, g_one, g_two)


def solution(mesh):
    split = Mesh(mesh.devices.reshape(2, 4, 4, 2, 2), ("dp", "z", "y", "c", "mp"))
    seq = ("z", "y", "c")
    weights = ("dp", "z", "y", "c")
    tokens = P("dp", seq, None)
    wide, tall = P(weights, "mp"), P("mp", weights)
    return jax.shard_map(
        local,
        mesh=split,
        in_specs=(tokens, P("dp", None), P("dp"), wide, wide, wide, tall, wide, tall, P(weights), P(weights), tokens),
        out_specs=(tokens, tokens, wide, wide, wide, tall, wide, tall, P(weights), P(weights)),
        check_vma=False,
    )
```

```python
import functools

import jax
import jax.numpy as jnp
from jax import lax
from jax.experimental import pallas as pl
from jax.experimental.pallas import tpu as pltpu
from jax.sharding import Mesh
from jax.sharding import PartitionSpec as P

MESH = pl.DeviceIdType.MESH
HD = 128
FRAME = 32
LEN = 4096
D = 2048
ROWS = 128
BLOCK = 256
ZY = ("z", "y")
epsilon = 1e-05
scale = HD**-0.5
LOG_BASE = 9.210340371976184
f32 = jnp.float32
bf16 = jnp.bfloat16


def params(collective_id=None, vmem=48, **kw):
    if collective_id is not None:
        kw = dict(collective_id=collective_id, has_side_effects=True, **kw)
    return pltpu.CompilerParams(vmem_limit_bytes=vmem * 2**20, **kw)


def vmem_specs(n):
    return [pl.BlockSpec(memory_space=pltpu.VMEM)] * n


def greet(peers):
    barrier = pltpu.get_barrier_semaphore()
    for peer in peers:
        pl.semaphore_signal(barrier, inc=1, device_id=peer, device_id_type=MESH)
    pl.semaphore_wait(barrier, len(peers))


def remote(src, dst, send, recv, peer):
    return pltpu.make_async_remote_copy(
        src_ref=src, dst_ref=dst, send_sem=send, recv_sem=recv, device_id=peer, device_id_type=MESH
    )


def started(copies, src, dst, send, recv, peer):
    copy = remote(src, dst, send, recv, peer)
    copy.start()
    copies.append(copy)
    return copy


class Sems:
    def __init__(self, send, recv):
        self.send, self.recv, self.used = send, recv, 0

    def take(self):
        k = self.used
        self.used += 1
        return self.send.at[k], self.recv.at[k]


def sem_pair(n):
    return [pltpu.SemaphoreType.DMA((n,)), pltpu.SemaphoreType.DMA((n,))]


def tensor_place():
    d, c, m = lax.axis_index("dp"), lax.axis_index("c"), lax.axis_index("mp")
    return d, c, m, {"c": 1 - c}, {"dp": 1 - d, "mp": 1 - m}, {"mp": 1 - m}


def ring(axis, size=4):
    me = lax.axis_index(axis)
    up, down, far = (lax.rem(me + k, size) for k in (1, size - 1, 2))
    return me, up, down, far, {axis: up}, {axis: down}


def added(*values):
    total = values[0].astype(f32)
    for v in values[1:]:
        total = total + v.astype(f32)
    return total


def run(*protocols):
    live = list(protocols)
    while live:
        for p in list(live):
            try:
                next(p)
            except StopIteration:
                live.remove(p)


def swap_plan(pairs, sems):
    d, c = lax.axis_index("dp"), lax.axis_index("c")
    me = 2 * d + c
    copies = []
    for a, b in [(d, 1 - c), (1 - d, c), (1 - d, 1 - c)]:
        for src, dst in pairs:
            started(copies, src(2 * a + b), dst(me), *sems.take(), {"dp": a, "c": b})
    for src, dst in pairs:
        dst(me)[...] = src(me)[...]
    yield
    for copy in copies:
        copy.wait_recv()
    yield
    for copy in copies:
        copy.wait_send()


def quarter(ref):
    wide = ref.shape[1] // 4
    return lambda q: ref.at[:, pl.ds(pl.multiple_of(q * wide, wide), wide)]


class Stores:
    def __init__(self, buffers, outputs, sems):
        self.pairs, self.sems, self.copies = list(zip(buffers, outputs)), sems, []

    def __call__(self, *places):
        for k in places:
            copy = pltpu.make_async_copy(*self.pairs[k], self.sems.at[k])
            copy.start()
            self.copies.append(copy)

    def wait(self):
        for copy in self.copies:
            copy.wait()


def swap_peers():
    d, c = lax.axis_index("dp"), lax.axis_index("c")
    return [{"dp": 1 - d}, {"dp": 1 - d, "c": 1 - c}]


CHUNKS = 4
FINE = 8
HALF = ROWS // 2


def rows_plan(x, o, sems):
    d, c, m, core, across, copy_of = tensor_place()
    me, far = 2 * d + c, 2 * (1 - d) + c
    copies, firsts, seconds = [], [], []
    step = HALF // 2
    mine = [pl.ds(m * HALF + k * step, step) for k in range(2)]
    other = [pl.ds((1 - m) * HALF + k * step, step) for k in range(2)]
    for rows in mine:
        firsts.append(started(copies, x.at[rows], o.at[me, rows], *sems.take(), across))
    near = started(copies, x, o.at[me], *sems.take(), core)
    o[me] = x[...]
    yield
    for k, rows in enumerate(other):
        firsts[k].wait_recv()
        seconds.append(started(copies, o.at[far, rows], o.at[far, rows], *sems.take(), copy_of))
    yield
    lasts = []
    for rows in other:
        lasts.append(started(copies, o.at[far, rows], o.at[far, rows], *sems.take(), core))
    for k, rows in enumerate(mine):
        seconds[k].wait_recv()
        lasts.append(started(copies, o.at[far, rows], o.at[far, rows], *sems.take(), core))
    yield
    near.wait_recv()
    for copy in lasts:
        copy.wait_recv()
    for copy in copies:
        copy.wait_send()


ROWS_SEMS = 9


def sum_plan(x, o, buffers, sems):
    from_core, s_here, s_send, from_across, t_send, from_copy = buffers
    d, c, m, core, across, copy_of = tensor_place()
    step = ROWS // CHUNKS
    rows = [pl.ds(k * step, step) for k in range(CHUNKS)]
    copies, zero, one, two = [], [], [], []
    for r in rows:
        zero.append(started(copies, x.at[:, 1 - c, r], from_core.at[:, r], *sems.take(), core))
    yield
    for k, r in enumerate(rows):
        zero[k].wait_recv()
        s_send[r] = x[1 - d, c, r] + from_core[1 - d, r]
        one.append(started(copies, s_send.at[r], from_across.at[r], *sems.take(), across))
        s_here[r] = x[d, c, r] + from_core[d, r]
    yield
    for k, r in enumerate(rows):
        one[k].wait_recv()
        t_send[r] = s_here[r] + from_across[r]
        two.append(started(copies, t_send.at[r], from_copy.at[r], *sems.take(), copy_of))
    yield
    for k, r in enumerate(rows):
        two[k].wait_recv()
        o[r] = added(t_send[r], from_copy[r])
    for copy in copies:
        copy.wait_send()


SUM_SEMS = 3 * CHUNKS
SUM_BUFFERS = [
    pltpu.VMEM((2, ROWS, D), bf16),
    pltpu.VMEM((ROWS, D), bf16),
    pltpu.VMEM((ROWS, D), bf16),
    pltpu.VMEM((ROWS, D), bf16),
    pltpu.VMEM((ROWS, D), bf16),
    pltpu.VMEM((ROWS, D), bf16),
]


def weights_plan(w, first, second, low, sems):
    i0, i_up, i_down, i_far, to_i_up, to_i_down = ring(first)
    j0, j_up, j_down, j_far, to_j_up, to_j_down = ring(second)

    def at(i, j, part, n):
        return w.at[(j, i) if first == "y" else (i, j)].at[pl.ds(low + part, n)]

    copies = []

    def send(ref, peer):
        return started(copies, ref, ref, *sems.take(), peer)

    def along(i):
        return i, send(at(i, j0, 0, 2), to_j_up), send(at(i, j0, 0, 2), to_j_down)

    from_down, from_up = send(at(i0, j0, 0, 2), to_i_up), send(at(i0, j0, 0, 2), to_i_down)
    second_leg = [along(i0)]
    yield
    from_down.wait_recv()
    far_low = send(at(i_down, j0, 0, 1), to_i_up)
    from_up.wait_recv()
    far_high = send(at(i_up, j0, 1, 1), to_i_down)
    second_leg.append(along(i_down))
    yield
    second_leg.append(along(i_up))
    yield
    onward = []

    def relay(leg):
        i, a, b = leg
        a.wait_recv()
        onward.append(send(at(i, j_down, 0, 1), to_j_up))
        b.wait_recv()
        onward.append(send(at(i, j_up, 1, 1), to_j_down))

    far_low.wait_recv()
    far_high.wait_recv()
    second_leg.append(along(i_far))
    for leg in second_leg:
        yield
        relay(leg)
    yield
    for copy in onward:
        copy.wait_recv()
    for copy in copies:
        copy.wait_send()


WEIGHT_SEMS = 20


def to_inner(x, o):
    for k in range(16):
        low, high = x[:, k * 64 : (k + 1) * 64], x[:, D // 2 + k * 64 : D // 2 + (k + 1) * 64]
        o[:, k * HD : (k + 1) * HD] = jnp.concatenate([low, high], 1)


def to_outer(x, o, kind):
    for k in range(0, 16, 2):
        one, two = x(k), x(k + 1)
        o[:, k * 64 : k * 64 + HD] = jnp.concatenate([one[:, :64], two[:, :64]], 1).astype(kind)
        o[:, D // 2 + k * 64 : D // 2 + k * 64 + HD] = jnp.concatenate([one[:, 64:], two[:, 64:]], 1).astype(kind)


def side_of(one, two, starts, padding):
    lane = lax.broadcasted_iota(jnp.int32, (32, HD), 1)
    same = lax.broadcasted_iota(jnp.int32, (32, 32), 0) == lax.broadcasted_iota(jnp.int32, (32, 32), 1)

    def column(row):
        return jnp.sum(jnp.where(same, row[...].astype(f32), 0.0), 1, keepdims=True)

    value = jnp.where(lane == 0, column(one), 0.0)
    value = jnp.where(lane == 1, column(two), value)
    for k in range(3):
        value = jnp.where(lane == 2 + k, starts[:, k : k + 1].astype(f32), value)
    return jnp.where(lane == 5, padding[...].astype(f32), value).astype(bf16)


def spread_plan(x, q, kv, sems):
    z, z_up, z_down, z_far, to_z_up, to_z_down = ring("z")
    y, y_up, y_down, y_far, to_y_up, to_y_down = ring("y")
    far = {"z": z_far}
    copies, firsts, queries, nears, fars = [], [], [], [], []
    both = pl.ds(1, 2)
    peers = [(z_up, to_z_up, z_down), (z_down, to_z_down, z_up), (z_far, far, z_far)]
    for place, peer, _ in peers:
        firsts.append(started(copies, x.at[place, both], kv.at[z, y], *sems.take(), peer))
    kv[z, y] = x[z, both]

    def along(place):
        ref = kv.at[place, y]
        nears.append(
            (place, started(copies, ref, ref, *sems.take(), to_y_up), started(copies, ref, ref, *sems.take(), to_y_down))
        )

    along(z)
    for place, peer, _ in peers:
        queries.append(started(copies, x.at[place, 0], q.at[z], *sems.take(), peer))
    q[z] = x[z, 0]
    yield
    for k, (_, _, source) in enumerate(peers):
        firsts[k].wait_recv()
        along(source)
        yield
    for copy in queries:
        copy.wait_recv()
    yield
    for place, a, b in nears:
        a.wait_recv()
        ref = kv.at[place, y_down, 0]
        fars.append(started(copies, ref, ref, *sems.take(), to_y_up))
        b.wait_recv()
        ref = kv.at[place, y_up, 1]
        fars.append(started(copies, ref, ref, *sems.take(), to_y_down))
        yield
    for copy in fars:
        copy.wait_recv()
    yield
    for copy in copies:
        copy.wait_send()


def ring_sum(at, axis, buffers, sems, put, late=False):
    one, two, passed = buffers
    me, up, down, far, to_up, to_down = ring(axis)
    copies = []
    a = started(copies, at(far, 0), one.at[0], *sems.take(), to_up)
    b = started(copies, at(far, 1), one.at[1], *sems.take(), to_down)
    if late:
        yield
    plain = [started(copies, at(up, 1), two.at[0, 1], *sems.take(), to_up)]
    if late:
        yield
    plain.append(started(copies, at(down, 0), two.at[1, 0], *sems.take(), to_down))
    if not late:
        yield
    a.wait_recv()
    passed[0] = at(up, 0)[...] + one[0]
    plain.append(started(copies, passed.at[0], two.at[0, 0], *sems.take(), to_up))
    b.wait_recv()
    passed[1] = at(down, 1)[...] + one[1]
    plain.append(started(copies, passed.at[1], two.at[1, 1], *sems.take(), to_down))
    yield
    for copy in plain:
        copy.wait_recv()
    for part in range(2):
        put(part, added(at(me, part)[...], two[0, part], two[1, part]))
    yield
    for copy in copies:
        copy.wait_send()


RING_SEMS = 6


def ring_buffers(n, part):
    return [pltpu.VMEM((n, 2, *part), bf16), pltpu.VMEM((n, 2, 2, *part), bf16), pltpu.VMEM((n, 2, *part), bf16)]


def collect_plan(dq, dkv, o, total, buffers, sems):
    z, peers = z_peers()
    peers = peers + [(z, None)]
    copies, rings = [], []
    for k, (place, peer) in enumerate(peers):

        def at(i, part, place=place):
            return dkv.at[place, i, part]

        def put(part, value, k=k):
            if k < 3:
                total[k, part] = value.astype(bf16)
            else:
                o[z, 1 + part] = value.astype(bf16)

        rings.append(ring_sum(at, "y", [b.at[k] for b in buffers], sems, put, True))
    for _ in range(3):
        for r in rings:
            next(r)
        yield
    for place, peer in peers[:3]:
        started(copies, dq.at[place], o.at[z, 0], *sems.take(), peer)
    o[z, 0] = dq[z]
    for k, r in enumerate(rings):
        next(r)
        if k < 3:
            started(copies, total.at[k], o.at[z, pl.ds(1, 2)], *sems.take(), peers[k][1])
    yield
    for copy in copies:
        copy.wait()
    run(*rings)


def first_leg(g, first, low, legs, buffers, sems, late=False):
    rings = []
    for j in range(4):

        def at(i, part, j=j):
            z, y = (j, i) if first == "y" else (i, j)
            return g.at[pl.ds(pl.multiple_of(((4 * z + y) * 4 + low + part) * 32, 32), 32)]

        def put(part, value, j=j):
            legs[j, part] = value.astype(bf16)

        rings.append(ring_sum(at, first, [b.at[j] for b in buffers], sems, put, late))
    for _ in range(4 if late else 3):
        for r in rings:
            next(r)
        yield
    run(*rings)


def second_leg(legs, shard, second, low, buffers, sems):
    def put(part, value):
        shard[low + part] = value.astype(bf16)

    return ring_sum(lambda i, part: legs.at[i, part], second, [b.at[b.shape[0] - 1] for b in buffers], sems, put)


def grads_plan(g, shard, first, second, low, legs, buffers, sems, late=False):
    leg = first_leg(g, first, low, legs, buffers, sems, late)
    for _ in range(4 if late else 3):
        next(leg)
        yield
    last = second_leg(legs, shard, second, low, buffers, sems)
    for _ in range(3):
        next(last)
        yield
    run(leg, last)


def reach(facts, block, rows):
    t = block * rows + lax.broadcasted_iota(jnp.int32, (rows, 1), 0)
    one, two, three, padding = (facts[:, k : k + 1].astype(jnp.int32) for k in range(2, 6))
    begin = jnp.where(t >= three, three, jnp.where(t >= two, two, one))
    living = t < LEN - padding
    end = jnp.minimum((t // FRAME + 1) * FRAME, LEN - padding)
    return t, begin, jnp.where(living, begin, t), jnp.where(living, end, t + 1)


def dot_t(a, b):
    return lax.dot_general(a, b, (((1,), (1,)), ((), ())), preferred_element_type=f32)


def dot_l(a, b):
    return lax.dot_general(a, b, (((0,), (0,)), ((), ())), preferred_element_type=f32)


def column_scores(facts, q, kv, i, column):
    n = (i + 1) * BLOCK
    _, _, low, high = reach(facts[pl.ds(lax.axis_index("z") // 2, 1)], 4 * i + lax.axis_index("y"), BLOCK)
    k = kv[0 : i + 1, column, 0].reshape(n, HD)
    at = lax.broadcasted_iota(jnp.int32, (1, n), 1)
    at = (at // BLOCK) * (4 * BLOCK) + at % BLOCK + column * BLOCK
    s = dot_t(q[i], k) * scale
    before, own = s[:, : i * BLOCK], s[:, i * BLOCK :]
    here = at[:, i * BLOCK :]
    own = jnp.where((here >= low) & (here < high), own, -1e30)
    if i:
        own = jnp.concatenate([jnp.where(at[:, : i * BLOCK] >= low, before, -1e30), own], 1)
    return k, own


def attend_tile(facts, q, kv, top, total, acc, i, column, first):
    _, s = column_scores(facts, q, kv, i, column)
    v = kv[0 : i + 1, column, 1].reshape((i + 1) * BLOCK, HD)
    now = jnp.max(s, -1, keepdims=True)
    if not first:
        before = top[i][:, :1]
        now = jnp.maximum(before, now)
    p = jnp.exp(s - now)
    plus = jnp.sum(p, -1, keepdims=True)
    out = jnp.dot(p.astype(bf16), v, preferred_element_type=f32)
    if not first:
        shrink = jnp.exp(before - now)
        plus = plus + total[i][:, :1] * shrink
        out = out + acc[i] * shrink
    top[i] = jnp.broadcast_to(now, (BLOCK, HD))
    total[i] = jnp.broadcast_to(plus, (BLOCK, HD))
    acc[i] = out


def attend_back_tile(facts, q, kv, do, lse, inner, dq, acc, i, column, first):
    k, s = column_scores(facts, q, kv, i, column)
    n = i + 1
    v = kv[0:n, column, 1].reshape(n * BLOCK, HD)
    p = jnp.exp(s - lse[i][:, :1])
    ds = (p * (dot_t(do[i], v) - inner[i][:, :1])).astype(bf16)
    dv = dot_l(p.astype(bf16), do[i]).reshape(n, BLOCK, HD)
    dk = dot_l(ds, q[i]).reshape(n, BLOCK, HD)
    part = jnp.dot(ds, k, preferred_element_type=f32)
    if i == 3:
        acc[:, 0], acc[:, 1] = dk, dv
    else:
        acc[0:n, 0] += dk
        acc[0:n, 1] += dv
    dq[i] = part if first else dq[i] + part


def norm(value):
    centre = value - jnp.mean(value, -1, keepdims=True)
    r = lax.rsqrt(jnp.mean(centre * centre, -1, keepdims=True) + epsilon)
    return centre * r, r


def norm_back(grad, n, r, gain):
    e = grad * gain
    return r * (e - jnp.mean(e, -1, keepdims=True) - n * jnp.mean(e * n, -1, keepdims=True))


def one_hot(rows, places):
    at = lax.broadcasted_iota(jnp.int32, (rows, HD), 0)
    lane = lax.broadcasted_iota(jnp.int32, (rows, HD), 1)
    hot = at < 0
    for k, place in enumerate(places):
        hot = hot | ((at == k) & (lane == place))
    return jnp.where(hot, 1.0, 0.0).astype(bf16)


def tables(facts, c):
    block = (4 * lax.axis_index("z") + lax.axis_index("y")) * 2 + c
    t, begin, _, _ = reach(facts, block, ROWS)
    lane = lax.broadcasted_iota(jnp.int32, (1, HD), 1)
    i = jnp.where(lane < HD // 2, lane, lane - HD // 2).astype(f32)
    angles = (t - begin).astype(f32) * jnp.exp(i * (-2.0 * LOG_BASE / HD))
    return jnp.cos(angles), jnp.where(lane < HD // 2, -1.0, 1.0) * jnp.sin(angles)


def sum_norm_plan(x, produce, all_rows, make, buffers, sems, idle=lambda: None):
    from_core, s_here, s_send, from_across, t_send, from_copy = buffers
    d, c, m, core, across, copy_of = tensor_place()
    me, far = 2 * d + c, 2 * (1 - d) + c
    step = ROWS // FINE
    rows = [pl.ds(k * step, step) for k in range(FINE)]
    halves = [pl.ds(pl.multiple_of(k * (D // 2), D // 2), D // 2) for k in (m, 1 - m)]
    copies, zero, one, two = [], [], [], []
    for h in range(2):
        produce(h)
        for r in rows[FINE // 2 * h : FINE // 2 * (h + 1)]:
            zero.append(started(copies, x.at[:, 1 - c, r], from_core.at[:, r], *sems.take(), core))
        for k in range(FINE // 2 * h, FINE // 2 * (h + 1)):
            r = rows[k]
            zero[k].wait_recv()
            s_send[r] = x[1 - d, c, r] + from_core[1 - d, r]
            one.append(started(copies, s_send.at[r], from_across.at[r], *sems.take(), across))
            s_here[r] = x[d, c, r] + from_core[d, r]
    idle()
    for k, r in enumerate(rows):
        if k % 2 == 0:
            idle()
        one[k].wait_recv()
        t_send[r] = s_here[r] + from_across[r]
        two.append(started(copies, t_send.at[r], from_copy.at[r], *sems.take(), copy_of))
    yield
    nears, firsts, seconds, lasts = [], [], [], []
    idle()
    for k, r in enumerate(rows):
        if k % 2 == 0:
            idle()
        two[k].wait_recv()
        all_rows[me, r] = make(r, added(t_send[r], from_copy[r])).astype(bf16)
        nears.append(started(copies, all_rows.at[me, r], all_rows.at[me, r], *sems.take(), core))
        ref = all_rows.at[me, r, halves[0]]
        firsts.append(started(copies, ref, ref, *sems.take(), across))
    yield

    def onward(r, half, peer):
        ref = all_rows.at[far, r, half]
        return started(copies, ref, ref, *sems.take(), peer)

    idle()
    for k, r in enumerate(rows):
        if k % 2 == 0:
            idle()
        firsts[k].wait_recv()
        seconds.append(onward(r, halves[1], copy_of))
        lasts.append(onward(r, halves[1], core))
    yield
    idle()
    for k, r in enumerate(rows):
        if k % 2 == 0:
            idle()
        seconds[k].wait_recv()
        lasts.append(onward(r, halves[0], core))
    yield
    for copy in nears + lasts:
        copy.wait_recv()
    yield
    for copy in copies:
        copy.wait_send()


SUM_NORM_SEMS = 8 * FINE
OUT_COLUMNS = pl.BlockSpec((D, 256), lambda i: (0, 3))


def z_peers():
    z, z_up, z_down, z_far, to_z_up, to_z_down = ring("z")
    return z, [(z_up, to_z_up), (z_down, to_z_down), (z_far, {"z": z_far})]


def front_kernel(
    wq,
    wk,
    wv,
    wo,
    wu,
    wd,
    x_hbm,
    cot_hbm,
    one,
    two,
    starts,
    padding,
    w_hbm,
    *scratch,
):
    outputs, weights_hbm, scratch = scratch[:15], scratch[15], scratch[16:]
    x_here, cot, tabs, n1, n1_t, gains, facts, q, kv, rows, o, lse, mixed, middle, n2 = scratch[:15]
    keep = Stores(scratch[:15], outputs, scratch[15])
    scratch = scratch[16:]
    w, weights, qkv, top, total, acc, low, turned, part, x_raw, cot_raw, side, x, lin = scratch[:14]
    sums, scratch = scratch[14:20], scratch[20:]
    local = scratch[0]
    sems = [Sems(*scratch[1 + 2 * k : 3 + 2 * k]) for k in range(10)]
    keys_sems, rows_sems, norm_sems, turn_sems, leg_a, leg_b, swaps, x_sems, first_a, first_b = sems
    d, c = lax.axis_index("dp"), lax.axis_index("c")
    me = 2 * d + c
    z, peers = z_peers()
    y, up, down, far, y_up, y_down = ring("y")
    here, there = w.at[z, y, me], weights.at[z, y, me]
    firsts = [(wq, 0, 256), (wk, 256, 256), (wv, 512, 256), (wo, 768, 256)]
    rests = [(wu, 0, 1024), (wd, 1024, 1024)]
    loads = [pltpu.make_async_copy(x_hbm, x_raw, local.at[0]), pltpu.make_async_copy(cot_hbm, cot_raw, local.at[1])]
    for k, (src, left, n) in enumerate(firsts):
        loads.append(pltpu.make_async_copy(quarter(src)(me), here.at[:, pl.ds(left, n)], local.at[2 + k]))
    for k, (src, left, n) in enumerate(rests):
        loads.append(pltpu.make_async_copy(quarter(src)(me), there.at[:, pl.ds(left, n)], local.at[6 + k]))
    for copy in loads:
        copy.start()
    side[...] = side_of(one, two, starts, padding)
    here[:, 1024:1152] = side[...]
    greet([*tensor_place()[3:], *swap_peers(), *[peer for _, peer in peers], y_up, y_down])

    def swap(pairs, dst):
        copies = []
        for a, b in [(d, 1 - c), (1 - d, c), (1 - d, 1 - c)]:
            for src, left, n in pairs:
                started(copies, src(2 * a + b), dst.at[:, pl.ds(left, n)], *swaps.take(), {"dp": a, "c": b})
        return copies

    swap_first = swap([(quarter(src), left, n) for src, left, n in firsts] + [(lambda q: side, 1024, HD)], here)
    loads[0].wait()
    to_inner(x_raw, x_here)
    gather_x = rows_plan(x_here, x, x_sems)
    next(gather_x)
    for copy in loads[2:6]:
        copy.wait()
    for copy in swap_first:
        copy.wait_recv()
    legs = [weights_plan(w, "y", "z", 0, first_a), weights_plan(w, "z", "y", 2, first_b)]
    for leg in legs:
        next(leg)
    swap_rest = swap([(quarter(src), left, n) for src, left, n in rests], there)
    for seq in range(2):
        fact = w[z, y, 2 * seq, 0:1, 1024:1152].astype(f32)
        for half in range(2):
            tabs[0, 2 * seq + half], tabs[1, 2 * seq + half] = tables(fact, half)
    loads[1].wait()
    to_inner(cot_raw, cot)
    run(*legs, gather_x)
    store = pltpu.make_async_copy(w, w_hbm, local.at[8])
    store.start()
    keep(0, 1, 2)
    for copy in loads[6:] + swap_rest:
        copy.wait()
    for copy in swap_first:
        copy.wait_send()

    def columns(left, right):
        return w[:, :, :, :, left:right].reshape(D, right - left)

    gather = rows_plan(cot, rows, rows_sems)
    next(gather)
    legs = [weights_plan(weights, "y", "z", 0, leg_a), weights_plan(weights, "z", "y", 2, leg_b)]

    def leg_step():
        for leg in legs:
            next(leg, None)

    leg_step()
    side = columns(1024, 1152)
    gains[...] = dot_t(one_hot(8, (0, 1)), side)
    facts[...] = jnp.zeros_like(facts)
    facts[0:1] = side[0:1].astype(f32)
    facts[1:2] = side[64:65].astype(f32)
    for block in range(4):
        r = pl.ds(block * ROWS, ROWS)
        n1[r] = (norm(x[block].astype(f32))[0] * gains[0:1]).astype(bf16)
    lin[...] = jnp.dot(n1[...], columns(0, 768), preferred_element_type=f32)
    for block in range(4):
        seq, half = block // 2, block % 2
        r = pl.ds(block * ROWS, ROWS)
        for kind in range(3):
            for h in range(2):
                v = lin[r, (2 * kind + h) * HD : (2 * kind + h + 1) * HD]
                if kind < 2:
                    v = v * tabs[0, block] + pltpu.roll(v, HD // 2, 1) * tabs[1, block]
                qkv[2 * seq + h, kind, half * ROWS : (half + 1) * ROWS] = v.astype(bf16)
    keys = spread_plan(qkv, q, kv, keys_sems)
    keep(3, 5, 6)

    def work():
        for k in range(4):
            some = slice(512 * k, 512 * (k + 1))
            n1_t[some] = n1[:, some].T
            yield
        for i in range(4):
            attend_tile(facts, q, kv, top, total, acc, i, y, True)
            yield

    pieces = work()
    next(keys)
    next(gather)
    for _ in range(4):
        next(pieces)
        next(keys)
    next(gather)
    for _ in range(4):
        next(pieces)
        next(keys)
    next(gather, None)
    leg_step()
    for column in (down, up):
        for i in range(4):
            attend_tile(facts, q, kv, top, total, acc, i, column, False)
    run(keys, gather)
    keep(4, 7, 8, 9)
    for i in range(4):
        attend_tile(facts, q, kv, top, total, acc, i, far, False)
    for i in range(4):
        low[i] = (acc[i] / total[i]).astype(bf16)
    copies = []
    for place, peer in peers:
        started(copies, low.at[place], turned.at[z], *turn_sems.take(), peer)
    turned[z] = low[z]
    for i in range(4):
        o[i] = acc[i] / total[i]
        lse[i] = top[i] + jnp.log(total[i])
    keep(10, 11)
    leg_step()
    for copy in copies:
        copy.wait()
    for seq in range(2):
        for h in range(2):
            mixed[seq, :, :, h * HD : (h + 1) * HD] = turned[2 * seq + h].reshape(2, ROWS, HD)
    keep(12)

    def partial(h):
        r = slice(HALF * h, HALF * (h + 1))
        value = dot_t(mixed[:, :, r].reshape(2 * ROWS, 256), columns(768, 1024))
        part[:, :, r] = value.astype(bf16).reshape(2, 2, HALF, D)

    def make(r, value):
        value = x_here[r].astype(f32) + value
        middle[r] = value
        return norm(value)[0] * gains[1:2]

    def legs_work():
        for pause in (0, 0, 1, 3, 6):
            for _ in range(pause):
                yield
            leg_step()
        for _ in range(5):
            yield
        run(*legs)
        pltpu.make_async_copy(weights, weights_hbm, local.at[9]).start()
        yield

    rest = legs_work()
    run(sum_norm_plan(part, partial, n2, make, sums, norm_sems, lambda: next(rest, None)))
    keep(13, 14)
    for _ in rest:
        pass
    keep.wait()
    pltpu.make_async_copy(weights, weights_hbm, local.at[9]).wait()
    store.wait()


def front(*args):
    block = (4, BLOCK, HD)
    shape = jax.ShapeDtypeStruct
    anywhere = pl.BlockSpec(memory_space=pl.ANY)
    whole = lambda *dims: pl.BlockSpec(dims, lambda i: (0,) * len(dims))
    first, second = (4, 4, 4, 32, 1152), (4, 4, 4, 32, 2048)
    kept = [
        shape((ROWS, D), bf16),
        shape((ROWS, D), bf16),
        shape((2, 4, ROWS, HD), f32),
        shape((512, D), bf16),
        shape((D, 512), bf16),
        shape((8, D), f32),
        shape((8, HD), f32),
        shape(block, bf16),
        shape((4, 4, 2, BLOCK, HD), bf16),
        shape((4, ROWS, D), bf16),
        shape(block, f32),
        shape(block, f32),
        shape((2, 2, ROWS, 256), bf16),
        shape((ROWS, D), f32),
        shape((4, ROWS, D), bf16),
    ]
    return pl.pallas_call(
        front_kernel,
        grid=(1,),
        out_shape=[shape(first, bf16), *kept, shape(second, bf16)],
        in_specs=[anywhere] * 8 + [whole(1, 32), whole(1, 32), whole(1, 3), whole(1, 1)],
        out_specs=[anywhere] * 17,
        scratch_shapes=[pltpu.VMEM(a.shape, a.dtype) for a in kept]
        + [pltpu.SemaphoreType.DMA((15,))]
        + [
            pltpu.VMEM(first, bf16),
            pltpu.VMEM(second, bf16),
            pltpu.VMEM((4, 3, BLOCK, HD), bf16),
        ]
        + [pltpu.VMEM(block, f32)] * 3
        + [pltpu.VMEM(block, bf16)] * 2
        + [pltpu.VMEM((2, 2, ROWS, D), bf16)]
        + [pltpu.VMEM((ROWS, D), bf16)] * 2
        + [pltpu.VMEM((32, HD), bf16), pltpu.VMEM((4, ROWS, D), bf16), pltpu.VMEM((512, 768), f32)]
        + SUM_BUFFERS
        + [pltpu.SemaphoreType.DMA((10,))]
        + sem_pair(22)
        + sem_pair(ROWS_SEMS)
        + sem_pair(SUM_NORM_SEMS)
        + sem_pair(3)
        + sem_pair(WEIGHT_SEMS) * 2
        + sem_pair(21)
        + sem_pair(ROWS_SEMS)
        + sem_pair(WEIGHT_SEMS) * 2,
        compiler_params=params(4, vmem=60),
        name="front",
    )(*args)


def feed_kernel(n2_hbm, cot_all_hbm, middle_hbm, cot_hbm, gains, w, weights, mixed_hbm, *scratch):
    outputs, scratch = scratch[:9], scratch[9:]
    fed, grad_out, grad_middle, turned, gain_two, down_a, down_b, up_a, up_b = scratch[:9]
    keep = Stores(scratch[:9], outputs, scratch[9])
    n2, cot_all, middle, cot, mixed = scratch[10:15]
    up, down, n2_t, cot_t, grads_down, grads_up, branch, active, grad_hidden, part, grad_mixed = scratch[15:26]
    scratch = scratch[26:]
    z, peers = z_peers()
    local = scratch[10]
    _, _, _, _, z_up, z_down = ring("z")
    _, _, _, _, y_up, y_down = ring("y")
    loads = [
        pltpu.make_async_copy(cot_all_hbm, cot_all, local.at[0]),
        pltpu.make_async_copy(weights.at[:, pl.ds(1024, 1024)], down, local.at[1]),
        pltpu.make_async_copy(n2_hbm, n2, local.at[2]),
        pltpu.make_async_copy(weights.at[:, pl.ds(0, 1024)], up, local.at[3]),
        pltpu.make_async_copy(middle_hbm, middle, local.at[4]),
        pltpu.make_async_copy(cot_hbm, cot, local.at[5]),
        pltpu.make_async_copy(mixed_hbm, mixed, local.at[6]),
    ]
    for copy in loads:
        copy.start()
    gain_two[...] = jnp.zeros_like(gain_two)
    greet([*tensor_place()[3:], *[peer for _, peer in peers], y_up, y_down])
    loads[0].wait()
    for k in range(4):
        some = slice(512 * k, 512 * (k + 1))
        cot_t[some] = cot_all[:, :, :, some].reshape(512, 512).T
    for copy in loads[1:]:
        copy.wait()

    def activate(h):
        rows = slice(HALF * h, HALF * (h + 1))
        n = n2[:, :, rows].reshape(2 * ROWS, D)
        g = cot_all[:, :, rows].reshape(2 * ROWS, D)
        for j in range(4):
            some = slice(256 * j, 256 * (j + 1))
            grad_active = jnp.dot(g, down[:, some], preferred_element_type=f32)
            hidden = jnp.dot(n, up[:, some], preferred_element_type=f32)
            half = 0.5 * (1.0 + lax.erf(hidden * 0.5**0.5))
            slope = half + hidden * jnp.exp(-0.5 * hidden * hidden) * (0.5 / jnp.pi) ** 0.5
            active[:, :, rows, some] = (hidden * half).astype(bf16).reshape(2, 2, HALF, 256)
            grad_hidden[:, :, rows, some] = (grad_active * slope).astype(bf16).reshape(2, 2, HALF, 256)

    def partial(h):
        activate(h)
        if h == 1:
            for j in range(4):
                down_piece(j)
            step(downs)
        rows = slice(HALF * h, HALF * (h + 1))
        value = grad_hidden[:, :, rows].reshape(2 * ROWS, 1024)
        for k in range(4):
            some = slice(512 * k, 512 * (k + 1))
            part[:, :, rows, some] = dot_t(value, up[some]).astype(bf16).reshape(2, 2, HALF, 512)

    downs = [
        first_leg(grads_down, "z", 0, down_a, scratch[11:14], Sems(*scratch[23:25])),
        first_leg(grads_down, "y", 2, down_b, scratch[14:17], Sems(*scratch[25:27])),
    ]
    ups = [
        first_leg(grads_up, "z", 0, up_a, scratch[17:20], Sems(*scratch[27:29])),
        first_leg(grads_up, "y", 2, up_b, scratch[20:23], Sems(*scratch[29:31])),
    ]

    def turn_n2(k):
        some = slice(512 * k, 512 * (k + 1))
        n2_t[some] = n2[:, :, :, some].reshape(512, 512).T

    def down_piece(j):
        some = slice(256 * j, 256 * (j + 1))
        value = active[:, :, :, some].reshape(512, 256)
        grads_down[:, some] = jnp.dot(cot_t[...], value, preferred_element_type=f32).astype(bf16)

    def up_piece(j):
        some = slice(256 * j, 256 * (j + 1))
        value = grad_hidden[:, :, :, some].reshape(512, 256)
        grads_up[:, some] = jnp.dot(n2_t[...], value, preferred_element_type=f32).astype(bf16)

    def fed_piece(k):
        some = slice(512 * k, 512 * (k + 1))
        value = dot_t(active[...].reshape(512, 1024), down[some])
        fed[:, :, :, some] = value.astype(bf16).reshape(2, 2, ROWS, 512)

    def step(plans):
        for plan in plans:
            next(plan, None)

    def work():
        for k in range(4):
            turn_n2(k)
        yield
        for j in range(4):
            up_piece(j)
            if j == 3:
                step(ups)
            yield
        step(downs)
        yield
        for k in range(4):
            fed_piece(k)
            if k == 3:
                keep(0)
            yield
        step(ups)
        yield

    pieces = work()

    def make(r, total):
        n, rate = norm(middle[r])
        gain_two[0:1] += 0.5 * jnp.sum(total * n, 0, keepdims=True)
        value = cot[r].astype(f32) + norm_back(total, n, rate, gains[1:2])
        grad_middle[r] = value
        return value

    run(sum_norm_plan(part, partial, branch, make, scratch[:6], Sems(*scratch[6:8]), lambda: next(pieces, None)))
    for k in range(4):
        value = jnp.dot(branch[k], w[...], preferred_element_type=f32).astype(bf16)
        for h in range(2):
            grad_mixed[2 * (k // 2) + h, (k % 2) * ROWS : (k % 2 + 1) * ROWS] = value[:, h * HD : (h + 1) * HD]
    turns, copies = Sems(*scratch[8:10]), []
    for place, peer in peers:
        started(copies, grad_mixed.at[place], turned.at[z], *turns.take(), peer)
    turned[z] = grad_mixed[z]
    for _ in pieces:
        pass
    keep(2, 4)
    for k in range(4):
        some = slice(512 * k, 512 * (k + 1))
        grad_out[some] = dot_l(branch[:, :, some].reshape(512, 512), mixed[...]).astype(bf16)
    keep(1)
    for copy in copies:
        copy.wait()
    keep(3)
    run(*downs, *ups)
    keep(5, 6, 7, 8)
    keep.wait()


def feed(n2, cot_all, middle, cot, gains, first, weights, mixed):
    anywhere = pl.BlockSpec(memory_space=pl.ANY)
    rows = (2, 2, ROWS, D)
    shape, vmem = jax.ShapeDtypeStruct, pltpu.VMEM
    kept = [
        shape(rows, bf16),
        shape((D, 256), bf16),
        shape((ROWS, D), f32),
        shape((4, BLOCK, HD), bf16),
        shape((8, D), f32),
    ] + [shape((4, 2, 32, 1024), bf16)] * 4
    return pl.pallas_call(
        feed_kernel,
        grid=(1,),
        out_shape=kept,
        in_specs=[anywhere] * 4 + vmem_specs(1) + [OUT_COLUMNS] + [anywhere] * 2,
        out_specs=[anywhere] * 9,
        scratch_shapes=[vmem(a.shape, a.dtype) for a in kept]
        + [pltpu.SemaphoreType.DMA((9,))]
        + [vmem(rows, bf16), vmem(rows, bf16), vmem((ROWS, D), f32), vmem((ROWS, D), bf16), vmem((512, 256), bf16)]
        + [
            vmem((D, 1024), bf16),
            vmem((D, 1024), bf16),
            vmem((D, 512), bf16),
            vmem((D, 512), bf16),
            vmem((D, 1024), bf16),
            vmem((D, 1024), bf16),
            vmem((4, ROWS, D), bf16),
            vmem((2, 2, ROWS, 1024), bf16),
            vmem((2, 2, ROWS, 1024), bf16),
            vmem(rows, bf16),
            vmem((4, BLOCK, HD), bf16),
        ]
        + SUM_BUFFERS
        + sem_pair(SUM_NORM_SEMS)
        + sem_pair(3)
        + [pltpu.SemaphoreType.DMA((7,))]
        + ring_buffers(4, (32, 1024)) * 4
        + sem_pair(4 * RING_SEMS) * 4,
        compiler_params=params(2, vmem=62),
        name="feed",
    )(n2.reshape(rows), cot_all.reshape(rows), middle, cot, gains, first, weights, mixed)


def back_kernel(
    facts,
    q,
    kv,
    o,
    lse,
    do,
    fed_part,
    w_hbm,
    n1_hbm,
    n1_t_hbm,
    grad_out_hbm,
    gains,
    tabs,
    gain_two,
    down_a,
    down_b,
    up_a,
    up_b,
    fed,
    out,
    gain,
    summed,
    down_all,
    up_all,
    *scratch,
):
    acc, dq, dq_low, dkv, inner, total, grads, down_shard, w, n1, n1_t, grad_out, lin, last, side, part = scratch[:16]
    up_shard, shard, side_shard, side_all, mine, theirs = scratch[16:22]
    legs_a, legs_b, side_a, side_b = scratch[22:26]
    key_buffers = scratch[26:29]
    rings = [scratch[29 + 3 * k : 32 + 3 * k] for k in range(8)]
    fed_buffers, sums = scratch[53:59], scratch[59:65]
    sems = [Sems(*scratch[65 + 2 * k : 67 + 2 * k]) for k in range(13)]
    local = scratch[91]
    pairs = [(n1_t_hbm, n1_t), (grad_out_hbm, grad_out), (w_hbm.at[:, pl.ds(0, 768)], w), (n1_hbm, n1)]
    loads = [pltpu.make_async_copy(a, b, local.at[k]) for k, (a, b) in enumerate(pairs)]
    for copy in loads:
        copy.start()
    d, c, m, core, across, copy_of = tensor_place()
    z, z_up, z_down, z_far, to_z_up, to_z_down = ring("z")
    y, y_up, y_down, y_far, to_y_up, to_y_down = ring("y")
    greet([core, across, copy_of, *swap_peers(), to_z_up, to_z_down, {"z": z_far}, to_y_up, to_y_down])

    def step(*plans):
        for plan in plans:
            next(plan, None)

    fed_plan = sum_plan(fed_part, fed, fed_buffers, sems[0])
    feeds = [
        second_leg(down_a, down_shard, "y", 0, rings[4], sems[2]),
        second_leg(down_b, down_shard, "z", 2, rings[5], sems[3]),
        second_leg(up_a, up_shard, "y", 0, rings[6], sems[11]),
        second_leg(up_b, up_shard, "z", 2, rings[7], sems[12]),
    ]
    swap_feed = swap_plan(
        [(lambda q: down_shard.at[q], lambda me: down_all.at[me]), (lambda q: up_shard.at[q], lambda me: up_all.at[me])],
        sems[1],
    )
    keys = collect_plan(dq_low, dkv, grads, total, key_buffers, sems[4])
    step(fed_plan, *feeds)
    for i in range(4):
        value = jnp.sum(o[i] * do[i].astype(f32), -1, keepdims=True)
        inner[i] = jnp.broadcast_to(value, (BLOCK, HD))
    for column in (y_far, y_up, y_down, y):
        for i in (3, 2, 1, 0):
            attend_back_tile(facts, q, kv, do, lse, inner, dq, acc, i, column, column is y_far)
        for k in range(4):
            dkv[k, column, 0] = (acc[k, 0] * scale).astype(bf16)
            dkv[k, column, 1] = acc[k, 1].astype(bf16)
        if column is y:
            dq_low[...] = (dq[...] * scale).astype(bf16)
        step(keys)
        if column is y_far or column is y:
            step(fed_plan)
    step(*feeds)
    for copy in loads:
        copy.wait()
    run(keys)
    step(*feeds, swap_feed)

    for block in range(4):
        seq, half = block // 2, block % 2
        for kind in range(3):
            for h in range(2):
                v = grads[2 * seq + h, kind, half * ROWS : (half + 1) * ROWS]
                if kind < 2:
                    v = v.astype(f32)
                    v = (v * tabs[0, block] - pltpu.roll(v, HD // 2, 1) * tabs[1, block]).astype(bf16)
                lin[block * ROWS : (block + 1) * ROWS, (2 * kind + h) * HD : (2 * kind + h + 1) * HD] = v
    blocks = [slice(512 * k, 512 * (k + 1)) for k in range(4)]
    for some in blocks:
        last[some, 0:768] = jnp.dot(n1_t[some], lin[...], preferred_element_type=f32).astype(bf16)
        last[some, 768:1024] = grad_out[some]
    lasts = [
        grads_plan(last, shard, "z", "y", 0, legs_a, rings[0], sems[5], True),
        grads_plan(last, shard, "y", "z", 2, legs_b, rings[1], sems[6], True),
    ]
    step(*lasts)
    hot = one_hot(8, (0, 1))
    for some in blocks:
        p = dot_t(lin[...], w[some])
        part[:, :, :, some] = p.astype(bf16).reshape(2, 2, ROWS, 512)
        gain_one = jnp.sum(p * n1[:, some].astype(f32), 0, keepdims=True) / gains[0:1, some]
        both = jnp.concatenate([gain_one, gain_two[0:1, some], jnp.zeros((6, 512), f32)], 0)
        side[some] = dot_l(both.astype(bf16), hot).astype(bf16)

    def gains_plan():
        halves = [
            grads_plan(side, side_shard, "z", "y", 0, side_a, rings[2], sems[7]),
            grads_plan(side, side_shard, "y", "z", 2, side_b, rings[3], sems[8]),
        ]
        for _ in range(6):
            for half in halves:
                next(half)
            yield
        run(*halves)
        swap = swap_plan([(lambda q: side_shard.at[q], lambda me: side_all.at[me])], sems[1])
        next(swap)
        yield
        run(swap)
        mine[...] = added(side_all[0], side_all[1], side_all[2], side_all[3])
        copy = remote(mine, theirs, *sems[1].take(), copy_of)
        copy.start()
        yield
        copy.wait()
        gain[...] = mine[...] + theirs[...]

    norms = sum_plan(part, summed, sums, sems[9])
    narrow = gains_plan()
    swap_last = swap_plan([(lambda q: shard.at[q], lambda me: out.at[me])], sems[10])
    step(norms, narrow, norms)
    step(*lasts)
    step(*lasts, narrow)
    step(narrow, *lasts, narrow)
    step(norms, *lasts, narrow)
    step(narrow, *lasts, narrow)
    step(narrow, *lasts, swap_last, fed_plan)
    run(narrow, swap_last, norms, *lasts, fed_plan, swap_feed, *feeds)


def back(facts, q, kv, o, lse, do, fed_part, w, n1, n1_t, grad_out, gains, tabs, gain_two, *feeds):
    block, narrow = (32, 1024), (32, HD)
    heads = (4, BLOCK, HD)
    shape, vmem = jax.ShapeDtypeStruct, pltpu.VMEM
    return pl.pallas_call(
        back_kernel,
        out_shape=[
            shape((ROWS, D), f32),
            shape((4, *block), bf16),
            shape(narrow, f32),
            shape((ROWS, D), f32),
            shape((4, *block), bf16),
            shape((4, *block), bf16),
        ],
        in_specs=vmem_specs(7) + [pl.BlockSpec(memory_space=pl.ANY)] * 4 + vmem_specs(7),
        out_specs=vmem_specs(6),
        scratch_shapes=[
            vmem((4, 2, BLOCK, HD), f32),
            vmem(heads, f32),
            vmem(heads, bf16),
            vmem((4, 4, 2, BLOCK, HD), bf16),
            vmem(heads, f32),
            vmem((3, 2, BLOCK, HD), bf16),
            vmem((4, 3, BLOCK, HD), bf16),
            vmem((4, *block), bf16),
            vmem((D, 768), bf16),
            vmem((512, D), bf16),
            vmem((D, 512), bf16),
            vmem((D, 256), bf16),
            vmem((512, 768), bf16),
            vmem((D, 1024), bf16),
            vmem((D, HD), bf16),
            vmem((2, 2, ROWS, D), bf16),
            vmem((4, *block), bf16),
            vmem((4, *block), bf16),
            vmem((4, *narrow), bf16),
            vmem((4, *narrow), bf16),
            vmem(narrow, f32),
            vmem(narrow, f32),
        ]
        + [vmem((4, 2, *block), bf16)] * 2
        + [vmem((4, 2, *narrow), bf16)] * 2
        + ring_buffers(4, (BLOCK, HD))
        + ring_buffers(5, block) * 2
        + ring_buffers(5, narrow) * 2
        + ring_buffers(1, block) * 4
        + SUM_BUFFERS * 2
        + sem_pair(SUM_SEMS)
        + sem_pair(10)
        + sem_pair(RING_SEMS) * 2
        + sem_pair(4 * RING_SEMS + 6)
        + sem_pair(5 * RING_SEMS) * 4
        + sem_pair(SUM_SEMS)
        + sem_pair(3)
        + sem_pair(RING_SEMS) * 2
        + [pltpu.SemaphoreType.DMA((4,))],
        compiler_params=params(6, vmem=62),
        name="back",
    )(facts, q, kv, o, lse, do, fed_part, w, n1, n1_t, grad_out, gains, tabs, gain_two, *feeds)


def finish_kernel(
    *refs,
):
    given, (out, g_in, g_q, g_k, g_v, g_out, g_up, g_down, g_one, g_two), refs = refs[:10], refs[10:20], refs[20:]
    last, grad_down, grad_up, gain, summed, x, grad_middle, gains, middle, fed, total, sems = refs
    loads = [pltpu.make_async_copy(a, b, sems.at[k]) for k, (a, b) in enumerate(zip(given, refs[:10]))]
    for copy in loads:
        copy.start()
    for copy in loads:
        copy.wait()
    total[...] = middle[...] + fed[...]
    to_outer(lambda k: total[:, k * HD : (k + 1) * HD], out, bf16)
    n, rate = norm(x[...].astype(f32))
    total[...] = grad_middle[...] + norm_back(summed[...], n, rate, gains[0:1])
    to_outer(lambda k: total[:, k * HD : (k + 1) * HD], g_in, f32)
    for q in range(4):
        for k, o in enumerate((g_q, g_k, g_v)):
            o[:, q * 256 : (q + 1) * 256] = last[q, :, k * 256 : (k + 1) * 256].astype(f32)
        g_out[:, q * 256 : (q + 1) * 256] = last[q, :, 768:1024].astype(f32)
        g_down[:, q * 1024 : (q + 1) * 1024] = grad_down[q].astype(f32)
        g_up[:, q * 1024 : (q + 1) * 1024] = grad_up[q].astype(f32)
    gain_t = gain[...].T
    g_one[...] = gain_t[0]
    g_two[...] = gain_t[1]


def finish(*args):
    def shape(*dims, kind=f32):
        return jax.ShapeDtypeStruct(dims, kind)

    return pl.pallas_call(
        finish_kernel,
        out_shape=[
            shape(ROWS, D, kind=bf16),
            shape(ROWS, D),
            shape(32, 1024),
            shape(32, 1024),
            shape(32, 1024),
            shape(32, 1024),
            shape(32, 4096),
            shape(32, 4096),
            shape(32),
            shape(32),
        ],
        in_specs=[pl.BlockSpec(memory_space=pl.ANY)] * 10,
        out_specs=vmem_specs(10),
        scratch_shapes=[pltpu.VMEM(a.shape, a.dtype) for a in args]
        + [pltpu.VMEM((ROWS, D), f32), pltpu.SemaphoreType.DMA((10,))],
        compiler_params=params(vmem=60),
        name="finish",
    )(*args)


def local(
    inputs,
    clip_starts,
    pad_lengths,
    w_query,
    w_key,
    w_value,
    w_out,
    w_up,
    w_down,
    gain_first,
    gain_second,
    cotangent,
):
    (
        first,
        x_here,
        incoming,
        tabs,
        normed_one,
        normed_one_t,
        gains,
        facts,
        q,
        kv,
        incoming_all,
        o,
        lse,
        mixed,
        middle,
        normed_two,
        second,
    ) = front(
        w_query,
        w_key,
        w_value,
        w_out.T,
        w_up,
        w_down.T,
        inputs[0],
        cotangent[0],
        gain_first[None],
        gain_second[None],
        clip_starts,
        pad_lengths[None],
    )
    first = first.reshape(D, -1)
    part_out, grad_out, grad_middle, grad_mixed, gain_two, *legs = feed(
        normed_two, incoming_all, middle, incoming, gains, first, second.reshape(D, D), mixed.reshape(512, 256)
    )
    fed, last, gain_grads, summed, grad_down, grad_up = back(
        facts,
        q,
        kv,
        o,
        lse,
        grad_mixed,
        part_out,
        first,
        normed_one,
        normed_one_t,
        grad_out,
        gains,
        tabs,
        gain_two,
        *legs,
    )
    output, grad_input, *rest = finish(
        last, grad_down, grad_up, gain_grads, summed, x_here, grad_middle, gains, middle, fed
    )
    g_query, g_key, g_value, g_out, g_up, g_down, g_one, g_two = rest
    return (output[None], grad_input[None], g_query, g_key, g_value, g_out.T, g_up, g_down.T, g_one, g_two)


def solution(mesh):
    split = Mesh(mesh.devices.reshape(2, 4, 4, 2, 2), ("dp", "z", "y", "c", "mp"))
    seq = ("z", "y", "c")
    weights = ("dp", "z", "y", "c")
    tokens = P("dp", seq, None)
    wide, tall = P(weights, "mp"), P("mp", weights)
    return jax.shard_map(
        local,
        mesh=split,
        in_specs=(tokens, P("dp", None), P("dp"), wide, wide, wide, tall, wide, tall, P(weights), P(weights), tokens),
        out_specs=(tokens, tokens, wide, wide, wide, tall, wide, tall, P(weights), P(weights)),
        check_vma=False,
    )
```
